32 devices in a mesh: dp: 16 (over z, x, core), mp: 2 (over y).
Axes of the slice: x: 2, y: 2, z: 4, core: 2. Of those that a mesh axis runs over, the one named last changes fastest.
Arguments:
- block_in: bfloat16 [16384, 768], P(('dp', 'mp')), may hold values from -6 to 6
- cotangent: bfloat16 [16384, 768], P(('dp', 'mp')), may hold values from -6 to 6
- lengths: int32 [16, 21], P('dp'), may hold values from 0 to 256, as said below
- token_mask: int32 [16, 1024], P('dp'), may hold values 0 or 1
- ln1_gain: float32 [768], replicated, may hold values from 0.25 to 1.75
- ln1_bias: float32 [768], replicated, may hold values from -3 to 3
- w_qkv: bfloat16 [768, 3, 768], P(None, None, 'mp'), may hold values from -0.3125 to 0.3125
- b_qv: float32 [2, 768], P(None, 'mp'), may hold values from -3 to 3
- w_out: bfloat16 [768, 768], P('mp'), may hold values from -1.5 to 1.5
- b_out: float32 [768], replicated, may hold values from -3 to 3
- ln2_gain: float32 [768], replicated, may hold values from 0.25 to 1.75
- ln2_bias: float32 [768], replicated, may hold values from -3 to 3
- w_up: bfloat16 [768, 3072], P(None, 'mp'), may hold values from -0.21875 to 0.21875
- b_up: float32 [3072], P('mp'), may hold values from -3 to 3
- w_down: bfloat16 [3072, 768], P('mp'), may hold values from -0.109375 to 0.109375
- b_down: float32 [768], replicated, may hold values from -3 to 3
Outputs:
- block_out: bfloat16 [16384, 768], P(('dp', 'mp'))
- d_block_in: bfloat16 [16384, 768], P(('dp', 'mp'))
- d_ln1_gain: float32 [768], replicated
- d_ln1_bias: float32 [768], replicated
- d_w_qkv: float32 [768, 3, 768], P(None, None, 'mp')
- d_b_qv: float32 [2, 768], P(None, 'mp')
- d_w_out: float32 [768, 768], P('mp')
- d_b_out: float32 [768], replicated
- d_ln2_gain: float32 [768], replicated
- d_ln2_bias: float32 [768], replicated
- d_w_up: float32 [768, 3072], P(None, 'mp')
- d_b_up: float32 [3072], P('mp')
- d_w_down: float32 [3072, 768], P('mp')
- d_b_down: float32 [768], replicated
The draws below stay inside these ranges and needn't reach their ends.
Inputs may be any that keep to these rules, and one draw needn't show every extreme that they name: `lengths`: row r lists, in order, the patch counts of the images packed into packed row r of 1024 tokens: every nonzero entry is 49, 196 or 256, zero entries come only after the nonzero ones, the entries of a row sum to at most 1024, and the last entry of every row is 0.
All inputs are finite; a program needn't handle non-finite values. No bound on the sum of `token_mask` on one device may be relied on, other than what follows from the above.
Results may differ from the reference program's by a relative error of at most 0.017.
The reference program's roundings to bfloat16 on the way count: a program that leaves them out, or rounds other values in their place, can miss the bound.
Values may be sent and summed in bfloat16 or wider, within the bound.
A program may use at most 192 MiB of HBM per device.

```python
import jax
import jax.numpy as jnp
from jax import lax

D = 768
HEADS = 12
HEAD_DIM = 64
FF = 3072
ROW = 1024
SLOTS = 21
NROWS = 16
TOKENS = 16384


def draw_lengths(key, part):
    key = jax.random.fold_in(key, 17)
    chosen = jax.random.randint(key, (NROWS, SLOTS), 0, 3)
    counts = jnp.where(chosen == 0, 49, jnp.where(chosen == 1, 196, 256)).astype(jnp.int32)
    counts = counts.at[0, 0].set(256)
    row_ends = jnp.cumsum(counts, axis=1)
    return jnp.where(row_ends <= ROW, counts, 0).astype(jnp.int32)


def plant(drawn, stream_key, low, high):
    longest = drawn.shape.index(max(drawn.shape))
    spots = []
    for shift in (0, 1):
        where = [jax.random.randint(jax.random.fold_in(stream_key, axis), (), 0, length) for axis, length in enumerate(drawn.shape)]
        where[longest] = (where[longest] + shift) % drawn.shape[longest]
        spots.append(tuple(where))
    return drawn.at[spots[0]].set(low).at[spots[1]].set(high)


def shard_levels(stream_key, shape, split, least, top_value):
    gain = 1.0
    for position, shards_of in split:
        draws = jax.random.uniform(jax.random.fold_in(jax.random.fold_in(stream_key, 6), position), (shards_of,), jnp.float32, least / len(split), top_value / len(split))
        gain = gain * jnp.repeat(jnp.exp(draws), shape[position] // shards_of).reshape((-1,) + (1,) * (len(shape) - 1 - position))
    return gain


def noise(key, shape, deviation, limit, split=(), kind=jnp.bfloat16):
    factor_of = shard_levels(key, shape, split, -0.22, 0.18) if split else 1.0
    entries = jax.random.normal(key, shape, jnp.float32) * deviation * factor_of
    return jnp.minimum(jnp.maximum(entries, -limit), limit).astype(kind)


def setup_inputs(seed: int = 0) -> dict:
    splits = jax.random.split(jax.random.key(seed), 17)
    block_in = noise(splits[0], (TOKENS, D), 1.0, 6.0, ((0, 32),))
    cotangent = noise(splits[1], (TOKENS, D), 1.0, 6.0, ((0, 32),))
    lengths = draw_lengths(jax.random.fold_in(splits[16], 71), 0)
    token_mask = plant((jax.random.randint(splits[3], (NROWS, ROW), 0, 8) < 7).astype(jnp.int32), jax.random.fold_in(splits[3], 1), 0, 1)
    ln1_gain = jnp.clip(1.0 + 0.15 * jax.random.normal(splits[4], (D,), jnp.float32), 0.25, 1.75)
    ln1_bias = noise(splits[5], (D,), 0.3, 3.0, (), jnp.float32)
    w_qkv = noise(splits[6], (D, 3, D), (D // 2) ** -0.5, 0.3125, ((2, 2),))
    b_qv = noise(splits[7], (2, D), 0.3, 3.0, ((1, 2),), jnp.float32)
    w_out = noise(splits[8], (D, D), (max(D // 48, 4)) ** -0.5, 1.5, ((0, 2),))
    b_out = noise(splits[9], (D,), 0.3, 3.0, (), jnp.float32)
    ln2_gain = jnp.clip(1.0 + 0.15 * jax.random.normal(splits[10], (D,), jnp.float32), 0.25, 1.75)
    ln2_bias = noise(splits[11], (D,), 0.3, 3.0, (), jnp.float32)
    w_up = noise(splits[12], (D, FF), D ** -0.5, 0.21875, ((1, 2),))
    b_up = noise(splits[13], (FF,), 0.3, 3.0, ((0, 2),), jnp.float32)
    w_down = noise(splits[14], (FF, D), FF ** -0.5, 0.109375, ((0, 2),))
    b_down = noise(splits[15], (D,), 0.3, 3.0, (), jnp.float32)
    return dict(block_in=block_in, cotangent=cotangent, lengths=lengths, token_mask=token_mask, ln1_gain=ln1_gain, ln1_bias=ln1_bias, w_qkv=w_qkv, b_qv=b_qv, w_out=w_out, b_out=b_out, ln2_gain=ln2_gain, ln2_bias=ln2_bias, w_up=w_up, b_up=b_up, w_down=w_down, b_down=b_down)


@jax.custom_vjp
def low(v):
    return lax.optimization_barrier(v.astype(jnp.bfloat16)).astype(jnp.float32)

@jax.custom_vjp
def low_back(v):
    return v

def low_keep(v):
    return (low(v), None)

def low_pass(kept, grad):
    return (grad,)

def back_keep(v):
    return (v, None)

def back_low(kept, grad):
    return (low(grad),)
low.defvjp(low_keep, low_pass)
low_back.defvjp(back_keep, back_low)
precise = lax.Precision.HIGHEST

def normalize(values, gain_vec, bias_vec):
    centred = values - lax.optimization_barrier(jnp.mean(values, axis=-1, keepdims=True))
    spread = lax.optimization_barrier(jnp.mean(centred * centred, axis=-1, keepdims=True))
    return centred * lax.rsqrt(spread + 1e-06) * gain_vec + bias_vec

def block_row(row_in, allowed, params):
    ln1_gain, ln1_bias, w_qkv, b_qv, w_out, b_out, ln2_gain, ln2_bias, w_up, b_up, w_down, b_down = params
    h1_low = low(normalize(row_in, ln1_gain, ln1_bias))
    queries = low_back(low((jnp.dot(h1_low, w_qkv[:, 0], precision=precise) + b_qv[0]) * HEAD_DIM ** (-0.5)))
    keys_all = low_back(low(jnp.dot(h1_low, w_qkv[:, 1], precision=precise)))
    vals_all = low_back(low(jnp.dot(h1_low, w_qkv[:, 2], precision=precise) + b_qv[1]))
    shape_heads = (ROW, HEADS, HEAD_DIM)
    scores = low_back(jnp.einsum('qhe,khe->hqk', queries.reshape(shape_heads), keys_all.reshape(shape_heads), precision=precise))
    masked = jnp.where(allowed[None], scores, -1e+30)
    row_max = lax.optimization_barrier(jnp.max(masked, axis=-1, keepdims=True))
    raised = jnp.exp(masked - row_max)
    weights_low = low(raised / lax.optimization_barrier(jnp.sum(raised, axis=-1, keepdims=True)))
    attended = jnp.einsum('hqk,khe->qhe', weights_low, vals_all.reshape(shape_heads), precision=precise).reshape(ROW, D)
    attended = low_back(low(attended))
    middle = row_in + low_back(jnp.dot(attended, w_out, precision=precise)) + b_out
    h2_low = low(normalize(middle, ln2_gain, ln2_bias))
    pre_act = low_back(jnp.dot(h2_low, w_up, precision=precise) + b_up)
    activated = low(jax.nn.gelu(pre_act, approximate=False))
    return middle + low_back(jnp.dot(activated, w_down, precision=precise)) + b_down

def reference(block_in, cotangent, lengths, token_mask, ln1_gain, ln1_bias, w_qkv, b_qv, w_out, b_out, ln2_gain, ln2_bias, w_up, b_up, w_down, b_down):
    positions = jnp.arange(ROW, dtype=jnp.int32)
    row_ends = jnp.cumsum(lengths, axis=1).astype(jnp.int32)
    seg_rows = lax.optimization_barrier(jnp.sum((positions[None, :, None] >= row_ends[:, None, :]).astype(jnp.int32), axis=2)).astype(jnp.int32)
    params = tuple((tensor.astype(jnp.float32) for tensor in (ln1_gain, ln1_bias, w_qkv, b_qv, w_out, b_out, ln2_gain, ln2_bias, w_up, b_up, w_down, b_down)))
    inputs = block_in.astype(jnp.float32).reshape(NROWS, ROW, D)

    def forward(inputs, params):

        def one_row(packed):
            row_in, seg_row, mask_row = packed
            same_seg = seg_row[:, None] == seg_row[None, :]
            visible = (mask_row[None, :] == 1) | (positions[:, None] == positions[None, :])
            return jax.checkpoint(block_row)(row_in, same_seg & visible, params)
        return lax.map(one_row, (inputs, seg_rows, token_mask))
    outputs, pullback = jax.vjp(forward, inputs, params)
    d_inputs, d_params = pullback(cotangent.astype(jnp.float32).reshape(NROWS, ROW, D))
    return (outputs.reshape(TOKENS, D).astype(jnp.bfloat16), d_inputs.reshape(TOKENS, D).astype(jnp.bfloat16), d_params[0], d_params[1], d_params[2], d_params[3], d_params[4], d_params[5], d_params[6], d_params[7], d_params[8], d_params[9], d_params[10], d_params[11])
```

```python
import functools
import jax
import jax.numpy as jnp
from jax import lax
from jax.experimental import pallas as pl
from jax.experimental.pallas import tpu as pltpu
from jax.sharding import PartitionSpec as P

HEAD_DIM = 64
MESH = pl.DeviceIdType.MESH
WIDE = 768
GROUPS = 3
LANES = 128


def ring_place(chip, chips):
    return jnp.where(chip % 2 == 0, chip // 2, chips - 1 - chip // 2)


def ring_chip(place, chips):
    return jnp.where(place < chips // 2, 2 * place, 2 * (chips - 1 - place) + 1)


def send_slots(chips):
    return min(chips, 8)


def whole_blocks(rows, n_dp):
    unit = 16 * n_dp
    return -(-rows // unit) * unit


class Here:
    def __init__(self, chips):
        dp, mp = lax.axis_index("dp"), lax.axis_index("mp")
        self.chips = chips
        self.core, chip = dp % 2, dp // 2
        self.place = ring_place(chip, chips)
        self.following = {"dp": ring_chip((self.place + 1) % chips, chips) * 2 + self.core}
        self.previous = {"dp": ring_chip((self.place + chips - 1) % chips, chips) * 2 + self.core}
        self.sibling = {"dp": chip * 2 + 1 - self.core}
        self.partner = {"mp": 1 - mp}
        self.side = chip % 2
        self.beside = {"dp": (chip + 1 - 2 * self.side) * 2 + self.core}


def remote(src, dst, send, recv, to):
    return pltpu.make_async_remote_copy(
        src_ref=src, dst_ref=dst, send_sem=send, recv_sem=recv, device_id=to, device_id_type=MESH
    )


class Segment:
    def __init__(self, here, base, rows, grads, from_core, landed, result, sems, own_sems=None):
        self.here, self.base, self.chips = here, base, here.chips
        self.block = rows // (2 * here.chips)
        self.slots = send_slots(here.chips)
        self.own_sems = own_sems
        self.grads, self.from_core, self.landed, self.result = grads, from_core, landed, result
        (
            self.core_send,
            self.core_recv,
            self.rs_send,
            self.rs_recv,
            self.ag_send,
            self.ag_recv,
            self.pair_send,
            self.pair_recv,
        ) = sems

    def rows_of(self, core, blk):
        start = self.base + (core * self.chips + blk) * self.block
        return pl.ds(pl.multiple_of(start, 16), self.block)

    def near_rows(self, blk):
        start = self.base // 2 + blk * self.block
        return pl.ds(pl.multiple_of(start, 16), self.block)

    def columns(self, ring):
        return pl.ds(ring * LANES, LANES)

    def rs_block(self, ring, step):
        if ring < GROUPS:
            return (self.here.place + 2 * self.chips - 1 - step) % self.chips
        return (self.here.place + 1 + step) % self.chips

    def ag_block(self, ring, step):
        if ring < GROUPS:
            return (self.here.place + self.chips - step) % self.chips
        return (self.here.place + step) % self.chips

    def toward(self, ring):
        return self.here.following if ring < GROUPS else self.here.previous

    def core_copy(self, half, step):
        blk = self.rs_block(half * GROUPS, step)
        cols = pl.ds(half * GROUPS * LANES, GROUPS * LANES)
        return remote(
            self.grads.at[self.rows_of(1 - self.here.core, blk), cols],
            self.from_core.at[self.near_rows(blk), cols],
            self.core_send.at[half, step],
            self.core_recv.at[half, step],
            self.here.sibling,
        )

    def rs_copy(self, ring, step):
        cols = self.columns(ring)
        return remote(
            self.grads.at[self.rows_of(self.here.core, self.rs_block(ring, step)), cols],
            self.landed.at[step, :, cols],
            self.rs_send.at[ring, step % self.slots],
            self.rs_recv.at[ring, step],
            self.toward(ring),
        )

    def result_copy(self, ring, step, send, recv, to):
        rows = self.rows_of(self.here.core, self.ag_block(ring, step))
        spot = self.result.at[rows, self.columns(ring)]
        own = self.own_sems is not None and isinstance(step, int) and step == 0
        held = self.grads.at[rows, self.columns(ring)] if own else spot
        return remote(held, spot, send.at[ring, step % self.slots], recv.at[ring, step], to)

    def own_copy(self, ring):
        spot = (self.rows_of(self.here.core, self.here.place), self.columns(ring))
        return pltpu.make_async_copy(
            self.grads.at[spot], self.result.at[spot], self.own_sems.at[ring]
        )

    def ag_copy(self, ring, step):
        return self.result_copy(ring, step, self.ag_send, self.ag_recv, self.toward(ring))

    def pair_copy(self, ring, step):
        return self.result_copy(ring, step, self.pair_send, self.pair_recv, self.here.sibling)

    def summed(self, ring, step, first):
        blk = self.rs_block(ring, step)
        rows, cols = self.rows_of(self.here.core, blk), self.columns(ring)
        value = self.grads[rows, cols].astype(jnp.float32)
        value = value + self.from_core[self.near_rows(blk), cols].astype(jnp.float32)
        if not first:
            value = value + self.landed[step - 1, :, cols].astype(jnp.float32)
        return rows, cols, value.astype(jnp.bfloat16)

    def send(self, copy, ring, step):
        if self.slots < self.chips:

            @pl.when(step >= self.slots)
            def _():
                copy(ring, step - self.slots).wait_send()

        copy(ring, step).start()

    def swap_cores(self):
        def start(step, carry):
            self.core_copy(0, step).start()
            self.core_copy(1, step).start()
            return carry

        lax.fori_loop(0, self.chips, start, 0)

    def wait_core(self, step):
        self.core_copy(0, step).wait_recv()
        self.core_copy(1, step).wait_recv()

    def begin(self):
        self.wait_core(0)
        for group in range(GROUPS):
            for ring in (group, group + GROUPS):
                rows, cols, value = self.summed(ring, 0, True)
                self.grads[rows, cols] = value
                self.send(self.rs_copy, ring, 0)

    def stage(self, group, step):
        n = self.chips
        rings = (group, group + GROUPS)

        @pl.when(step <= n - 2)
        def _():
            if group == 0:
                self.wait_core(step)
            for ring in rings:
                self.rs_copy(ring, step - 1).wait_recv()
                rows, cols, value = self.summed(ring, step, False)
                self.grads[rows, cols] = value
                self.send(self.rs_copy, ring, step)

        @pl.when(step == n - 1)
        def _():
            if group == 0:
                self.wait_core(n - 1)
            for ring in rings:
                self.rs_copy(ring, n - 2).wait_recv()
                rows, cols, value = self.summed(ring, n - 1, False)
                if self.own_sems is None:
                    self.result[rows, cols] = value
                else:
                    self.grads[rows, cols] = value
                    self.own_copy(ring).start()
                self.send(self.ag_copy, ring, 0)
                self.send(self.pair_copy, ring, 0)

        @pl.when((step >= n) & (step <= 2 * n - 3))
        def _():
            for ring in rings:
                self.ag_copy(ring, step - n).wait_recv()
                self.send(self.ag_copy, ring, step - n + 1)
                self.send(self.pair_copy, ring, step - n + 1)

        @pl.when(step == 2 * n - 2)
        def _():
            for ring in rings:
                self.ag_copy(ring, n - 2).wait_recv()
                self.send(self.pair_copy, ring, n - 1)

    def stages(self, first, last):
        def run(step, carry):
            for group in range(GROUPS):
                self.stage(group, step)
            return carry

        lax.fori_loop(first, last, run, 0)

    def arrive(self):
        def run(step, carry):
            for ring in range(2 * GROUPS):
                self.pair_copy(ring, step).wait_recv()
            return carry

        lax.fori_loop(0, self.chips, run, 0)
        if self.own_sems is not None:
            for ring in range(2 * GROUPS):
                self.own_copy(ring).wait()

    def drain(self):
        def cores(step, carry):
            self.core_copy(0, step).wait_send()
            self.core_copy(1, step).wait_send()
            return carry

        def pairs(step, carry):
            for ring in range(2 * GROUPS):
                self.pair_copy(ring, step).wait_send()
            return carry

        def ring_steps(step, carry):
            for ring in range(2 * GROUPS):
                self.rs_copy(ring, step).wait_send()
                self.ag_copy(ring, step).wait_send()
            return carry

        n, slots = self.chips, self.slots
        lax.fori_loop(0, n, cores, 0)
        lax.fori_loop(n - slots, n, pairs, 0)
        lax.fori_loop(max(n - 1 - slots, 0), n - 1, ring_steps, 0)


def segment_sems(chips):
    dma = pltpu.SemaphoreType.DMA
    rings = 2 * GROUPS
    slots = send_slots(chips)
    both = [dma((rings, slots)), dma((rings, chips))]
    return [dma((2, chips))] * 2 + both * 3


class Small:
    def __init__(self, here, from_core, from_mp, every, pair_sems, ring_sems):
        self.here, self.from_core, self.from_mp, self.every = here, from_core, from_mp, every
        self.pair_sems, self.ring_sems = pair_sems, ring_sems
        self.forward = here.chips // 2
        self.backward = here.chips - 1 - self.forward

    def pair(self, which, src, dst, to):
        return remote(src, dst, self.pair_sems.at[0, which], self.pair_sems.at[1, which], to)

    def start(self, src):
        self.src = src
        self.to_core = self.pair(0, src, self.from_core, self.here.sibling)
        self.to_core.start()

    def core_done(self):
        self.to_core.wait()
        place = self.here.place
        self.every[place] = self.src[...] + self.from_core[...]
        spot = self.every.at[place, pl.ds(8, 8)]
        self.to_mp = self.pair(1, spot, self.from_mp, self.here.partner)
        self.to_mp.start()

    def mp_done(self):
        self.to_mp.wait()
        place = self.here.place
        self.every[place, pl.ds(8, 8)] = self.every[place, pl.ds(8, 8)] + self.from_mp[...]
        self.step(0, 0).start()
        if self.backward:
            self.step(1, 0).start()

    def step(self, way, step):
        n = self.here.chips
        at = (self.here.place + n - step) % n if way == 0 else (self.here.place + step) % n
        spot = self.every.at[at]
        to = self.here.following if way == 0 else self.here.previous
        sems = self.ring_sems
        return remote(spot, spot, sems.at[0, way, step], sems.at[1, way, step], to)

    def hop(self, step):
        for way, count in ((0, self.forward), (1, self.backward)):

            @pl.when(step < count)
            def _():
                self.step(way, step - 1).wait_recv()
                self.step(way, step).start()

    def finish(self, out, hops):
        def run(step, carry):
            self.hop(step)
            return carry

        if hops < self.forward:
            lax.fori_loop(hops, self.forward, run, 0)
        self.step(0, self.forward - 1).wait_recv()
        if self.backward:
            self.step(1, self.backward - 1).wait_recv()
        out[...] = self.every[0]

        def add(chip, carry):
            out[...] += self.every[chip]
            return carry

        lax.fori_loop(1, self.here.chips, add, 0)

        def sent(way, count):
            def run(step, carry):
                self.step(way, step).wait_send()
                return carry

            lax.fori_loop(0, count, run, 0)

        sent(0, self.forward)
        sent(1, self.backward)


def small_scratch(chips):
    dma = pltpu.SemaphoreType.DMA
    return [
        pltpu.VMEM((16, WIDE), jnp.float32),
        pltpu.VMEM((8, WIDE), jnp.float32),
        pltpu.VMEM((chips, 16, WIDE), jnp.float32),
        dma((2, 2)),
        dma((2, 2, chips)),
    ]


LOW = jnp.bfloat16
F32 = jnp.float32
HALF = 512
TILE = 256
SPAN = 128
STRIP = 32
HIDDEN = 256
EPS = 1e-06
FAR = -1e30
SCALE = HEAD_DIM**-0.5
NT = (((1,), (1,)), ((), ()))
TN = (((0,), (0,)), ((), ()))


def nt_dot(a, b):
    return lax.dot_general(a, b, NT, preferred_element_type=F32)


def tn_dot(a, b):
    return lax.dot_general(a, b, TN, preferred_element_type=F32)


def dot(a, b):
    return jnp.dot(a, b, preferred_element_type=F32)


def normal_parts(values):
    centred = values - jnp.mean(values, axis=-1, keepdims=True)
    spread = jnp.mean(centred * centred, axis=-1, keepdims=True)
    return centred, lax.rsqrt(spread + EPS)


def norm_back(d_out, unit, inverse, gain):
    e = d_out * gain
    share = e - jnp.mean(e, -1, keepdims=True)
    return inverse * (share - unit * jnp.mean(e * unit, -1, keepdims=True))


def column_sum(values):
    return jnp.sum(values, axis=0, keepdims=True)


def split_heads(pair):
    low_lanes = lax.broadcasted_iota(jnp.int32, pair.shape, 1) < HEAD_DIM
    zero = jnp.zeros_like(pair)
    return jnp.concatenate([jnp.where(low_lanes, pair, zero), jnp.where(low_lanes, zero, pair)])


def own_blocks(both):
    return jnp.concatenate([both[:HEAD_DIM, :SPAN], both[HEAD_DIM:, SPAN:]], axis=0)


def twice(values):
    return jnp.concatenate([values, values], axis=1)


SCRATCH = (
    "x_own", "h1", "cot", "h2", "wq", "w_mine", "w_got", "q", "k", "v", "att32", "att_send",
    "att_got", "lse", "key_code", "query_seg", "bias", "middle", "out_sum", "out_send", "out_got",
    "dh_own", "dh2_send", "dh2_got", "d_branch", "d_att", "go_send", "go_core", "go_got",
    "small_ref", "grads", "from_core", "result", "landed_m", "landed_q", "local_sems", "swap_sems",
    "pass_sems", "own_sems",
)


def twice_rows(values):
    return jnp.concatenate([values[0:1], values[1:2]], axis=1)


def fold(values, op, rows=8):
    while values.shape[0] > rows:
        half = values.shape[0] // 2
        values = op(values[:half], values[half:])
    return values


def strips(rows):
    return [slice(at, at + STRIP) for at in range(0, rows, STRIP)]


def result_in_hbm(chips):
    return chips > 8


class Names:
    pass


def block_kernel(chips, sizes, *refs):
    (
        x_hbm,
        cot_hbm,
        wq_hbm,
        w_out_hbm,
        up_hbm,
        down_hbm,
        lengths,
        mask_ref,
        gain1,
        bias1,
        b_qv,
        b_out,
        gain2,
        bias2,
        b_up,
        b_down,
        summed_ref,
        out_ref,
        dx_ref,
        small_out,
    ) = refs[:20]
    m = Names()
    for name, ref in zip(SCRATCH, refs[20:]):
        setattr(m, name, ref)
    more = refs[20 + len(SCRATCH) :]
    sems_m, sems_q, small_refs = more[:8], more[8:16], more[16:]
    rows_m, rows_q = sizes
    here = Here(chips)
    direct = result_in_hbm(chips)
    result = summed_ref if direct else m.result
    ring_m = Segment(
        here, 0, rows_m, m.grads, m.from_core, m.landed_m, result, sems_m,
        m.own_sems.at[0] if direct else None,
    )
    ring_q = Segment(
        here, rows_m, rows_q, m.grads, m.from_core, m.landed_q, result, sems_q,
        m.own_sems.at[1] if direct else None,
    )
    small = Small(here, *small_refs)
    width = m.k.shape[1]
    pairs = width // 128
    row_len = 2 * HALF
    hidden = up_hbm.shape[1]
    blocks = row_len // SPAN

    def local(which, src, dst):
        return pltpu.make_async_copy(src, dst, m.local_sems.at[which])

    def swapped(which, src, dst):
        return remote(src, dst, m.swap_sems.at[0, which], m.swap_sems.at[1, which], here.partner)

    def part(chunk):
        return pl.ds(pl.multiple_of(chunk * TILE, TILE), TILE)

    def other(chunk):
        return pl.ds(pl.multiple_of(HALF + chunk * TILE, TILE), TILE)

    def x_swap(chunk):
        return swapped(chunk, x_hbm.at[part(chunk)], m.h1.at[other(chunk)])

    def cot_swap(chunk):
        return swapped(2 + chunk, cot_hbm.at[part(chunk)], m.cot.at[other(chunk)])

    def h2_swap(chunk):
        return swapped(4 + chunk, m.h2.at[part(chunk)], m.h2.at[other(chunk)])

    def dh2_swap(chunk):
        return swapped(6 + chunk, m.dh2_send.at[part(chunk)], m.dh2_got.at[part(chunk)])

    def out_swap(chunk):
        return swapped(8 + chunk, m.out_send.at[part(chunk)], m.out_got.at[part(chunk)])

    def dh1_swap(chunk):
        return swapped(10 + chunk, m.dh2_send.at[part(chunk)], m.dh2_got.at[part(chunk)])

    quarter = width // 2
    w_rows = pl.ds(pl.multiple_of(here.core * quarter, 16), quarter)
    piece = pl.ds(pl.multiple_of((here.core * 2 + here.side) * (quarter // 2), 16), quarter // 2)
    w_swap = swapped(12, w_out_hbm.at[piece], m.w_got.at[piece])
    w_share = remote(
        m.w_got.at[piece], m.w_got.at[piece], m.pass_sems.at[4], m.pass_sems.at[5], here.beside
    )
    w_pass = remote(
        m.w_got.at[w_rows], m.w_got.at[w_rows], m.pass_sems.at[0], m.pass_sems.at[1], here.sibling
    )
    att_swap = swapped(13, m.att_send, m.att_got)
    da_swap = swapped(14, m.att_send, m.d_att.at[pl.ds(HALF, HALF)])
    other_rows = pl.ds(pl.multiple_of((1 - here.core) * quarter, 16), quarter)
    go_pass = remote(
        m.go_send.at[other_rows], m.go_core, m.pass_sems.at[2], m.pass_sems.at[3], here.sibling
    )
    go_swap = swapped(15, m.go_core, m.go_got)

    def as_row(ref):
        return ref[...].reshape(1, ref.shape[0])

    load_x = local(0, x_hbm, m.x_own)
    load_wq = local(1, wq_hbm, m.wq)
    load_w = local(2, w_out_hbm, m.w_mine)
    load_cot = local(3, cot_hbm, m.cot.at[pl.ds(0, HALF)])
    for load in (load_x, load_wq, load_w, load_cot):
        load.start()
    barrier = pltpu.get_barrier_semaphore()
    near = (here.sibling, here.following, here.previous, here.partner, here.beside)
    for device in near:
        pl.semaphore_signal(barrier, inc=1, device_id=device, device_id_type=MESH)
    pl.semaphore_wait(barrier, len(near))
    x_swap(0).start()

    shift = lax.axis_index("mp") * HALF
    ends, total = [], lengths[0, 0]
    for slot in range(lengths.shape[1]):
        ends.append(total)
        if slot + 1 < lengths.shape[1]:
            total = total + lengths[0, slot + 1]

    def segment(shape, axis):
        at = (lax.broadcasted_iota(jnp.int32, shape, axis) + shift) % row_len
        found = jnp.zeros(shape, jnp.int32)
        for end in ends:
            found = found + (at >= end).astype(jnp.int32)
        return found

    seg_row = segment((1, row_len), 1)
    for block in range(blocks):
        m.query_seg[block] = seg_row[:, block * SPAN : (block + 1) * SPAN]
    mask = mask_ref[...]
    turned = jnp.concatenate([mask[:, HALF:], mask[:, :HALF]], axis=1)
    mask = jnp.where(shift == 0, mask, turned)
    code = jnp.where(mask == 1, seg_row, -1).astype(F32)
    m.key_code[...] = jnp.broadcast_to(code, (8, row_len)).T[:, :1].astype(jnp.int32)

    def project(values, rows):
        centred, inverse = normal_parts(values.astype(F32))
        h1 = (centred * inverse * as_row(gain1) + as_row(bias1)).astype(LOW)
        m.h1[rows] = h1
        m.q[rows] = ((dot(h1, m.wq[0]) + b_qv[0:1]) * SCALE).astype(LOW)
        m.k[rows] = dot(h1, m.wq[1]).astype(LOW)
        m.v[rows] = (dot(h1, m.wq[2]) + b_qv[1:2]).astype(LOW)

    load_x.wait()
    load_wq.wait()

    def project_own(chunk, carry):
        project(m.x_own[part(chunk)], part(chunk))
        return carry

    lax.fori_loop(0, HALF // TILE, project_own, 0)
    x_swap(1).start()

    def project_got(chunk, carry):
        x_swap(chunk).wait_recv()

        @pl.when(chunk == HALF // TILE - 1)
        def _():
            w_swap.start()
            cot_swap(0).start()

        project(m.h1[other(chunk)], other(chunk))
        return carry

    lax.fori_loop(0, HALF // TILE, project_got, 0)

    def set_bias(block):
        shape = (row_len, SPAN)
        key_at = lax.broadcasted_iota(jnp.int32, shape, 0)
        query_at = lax.broadcasted_iota(jnp.int32, shape, 1) + block * SPAN
        allowed = (m.key_code[...] == m.query_seg[block]) | (key_at == query_at)
        m.bias[...] = jnp.where(allowed, 0.0, FAR)

    def block_rows(block):
        return pl.ds(pl.multiple_of(block * SPAN, SPAN), SPAN)

    def attend_scope(vt, scores, raised):
        vt[...] = m.v[...].T

        def block_at(at):
            return (at + blocks // 2) % blocks

        def score(block, pair, slot):
            cols = slice(128 * pair, 128 * pair + 128)
            scores[slot] = nt_dot(m.k[:, cols], split_heads(m.q[block_rows(block), cols]))

        def weigh(slot):
            held, out = scores.at[slot], raised.at[slot]
            top = None
            for keys in strips(row_len):
                here = held[keys] + twice(m.bias[keys])
                top = here if top is None else jnp.maximum(top, here)
            top = jnp.max(fold(top, jnp.maximum), axis=0, keepdims=True)
            whole = None
            for keys in strips(row_len):
                here = jnp.exp(held[keys] + twice(m.bias[keys]) - top)
                out[keys] = here.astype(LOW)
                whole = here if whole is None else whole + here
            return top, jnp.sum(fold(whole, jnp.add), axis=0, keepdims=True)

        def gather(block, pair, slot, top, whole):
            cols = slice(128 * pair, 128 * pair + 128)
            outs = own_blocks(dot(vt[cols], raised[slot]) / whole)
            m.att32[block_rows(block), cols] = outs.T
            m.lse[block, pair] = top + jnp.log(whole)

        def attend(couple, carry):
            @pl.when(couple == blocks // 8)
            def _():
                w_swap.wait_recv()
                w_share.start()

            @pl.when(couple == blocks // 4)
            def _():
                m.att_send[...] = m.att32[pl.ds(HALF, HALF)].astype(LOW)
                att_swap.start()
                w_share.wait_recv()
                w_pass.start()

            held = None
            for at in range(2 * pairs):
                pair, slot = at % pairs, at % 2
                turn = couple * 2 + at // pairs
                block = block_at(turn)
                if pair == 0:
                    set_bias(block)
                if pair + 1 < pairs:
                    score(block, pair + 1, 1 - slot)
                else:
                    score(block_at(jnp.minimum(turn + 1, blocks - 1)), 0, 1 - slot)
                now = weigh(slot)
                if held is not None:
                    gather(*held)
                held = (block, pair, slot, *now)
            gather(*held)
            return carry

        score(block_at(0), 0, 0)
        lax.fori_loop(0, blocks // 2, attend, 0)

    pl.run_scoped(
        attend_scope,
        pltpu.VMEM((width, row_len), LOW),
        pltpu.VMEM((2, row_len, 2 * SPAN), F32),
        pltpu.VMEM((2, row_len, 2 * SPAN), LOW),
    )

    load_w.wait()
    w_pass.wait_recv()
    att_swap.wait_recv()

    def branch(chunk, carry):
        rows = part(chunk)
        got = dot(m.att32[rows].astype(LOW), m.w_mine[...]) + dot(m.att_got[rows], m.w_got[...])
        middle = m.x_own[rows].astype(F32) + got + as_row(b_out)
        m.middle[rows] = middle
        centred, inverse = normal_parts(middle)
        m.h2[rows] = (centred * inverse * as_row(gain2) + as_row(bias2)).astype(LOW)

        @pl.when(chunk == 0)
        def _():
            h2_swap(0).start()

        return carry

    lax.fori_loop(0, HALF // TILE, branch, 0)
    load_cot.wait()

    def mlp_scope(act_ref, pre_ref, up_sum):
        def chunks_scope(up, down, out_acc, dh_acc, pre_buf, d_buf, up_row, ht):
            load_up, load_down = local(0, up_hbm, up), local(1, down_hbm, down)
            load_up.start()
            load_down.start()
            load_up.wait()
            load_down.wait()
            up_sum[...] = jnp.zeros_like(up_sum)
            up_row[...] = as_row(b_up)
            tiles = hidden // HIDDEN

            def forth_and_back(begin, tokens, out_to, dh_to):
                rows = pl.ds(begin, tokens)

                def enter(tile):
                    cols = slice(tile * HIDDEN, tile * HIDDEN + HIDDEN)
                    pre_buf[tile % 2, :tokens] = dot(m.h2[rows], up[:, cols])
                    d_buf[tile % 2, :tokens] = nt_dot(m.cot[rows], down[cols])

                def bend(tile):
                    cols = slice(tile * HIDDEN, tile * HIDDEN + HIDDEN)
                    shift_up = up_row[:, cols]
                    total = None
                    for at in range(0, tokens, STRIP):
                        pre = pre_buf[tile % 2, at : at + STRIP] + shift_up
                        cdf = 0.5 * (1.0 + lax.erf(pre * 0.7071067811865476))
                        slope = cdf + pre * (jnp.exp(-0.5 * pre * pre) * 0.3989422804014327)
                        d_pre = (d_buf[tile % 2, at : at + STRIP] * slope).astype(LOW)
                        spot = pl.ds(begin + at, STRIP)
                        act_ref[spot, cols] = (pre * cdf).astype(LOW)
                        pre_ref[spot, cols] = d_pre
                        d_pre = d_pre.astype(F32)
                        total = d_pre if total is None else total + d_pre
                    up_sum[:, cols] += column_sum(fold(total, jnp.add))

                def leave(tile):
                    cols = slice(tile * HIDDEN, tile * HIDDEN + HIDDEN)
                    out = dot(act_ref[rows, cols], down[cols])
                    d_h = nt_dot(pre_ref[rows, cols], up[:, cols])
                    if tile == 0:
                        out_to[...] = out
                        dh_to[...] = d_h
                    else:
                        out_to[...] += out
                        dh_to[...] += d_h

                enter(0)
                for tile in range(tiles):
                    if tile + 1 < tiles:
                        enter(tile + 1)
                    bend(tile)
                    if tile > 0:
                        leave(tile - 1)
                leave(tiles - 1)

            def grad_part(begin, count):
                span = WIDE // 2
                tokens = pl.ds(begin, count)
                ht[:, :count] = m.h2[tokens].T

                def put(rows, cols, value):
                    if begin:
                        value = value + m.grads[rows, cols].astype(F32)
                    m.grads[rows, cols] = value.astype(LOW)

                def grad_step(at, carry):
                    cols = pl.ds(pl.multiple_of(at * span, 128), span)
                    up_rows = pl.ds(pl.multiple_of(at // 2 * WIDE, WIDE), WIDE)
                    up_cols = pl.ds(pl.multiple_of(at % 2 * span, 128), span)
                    put(up_rows, up_cols, dot(ht[:, :count], pre_ref[tokens, cols]))
                    down_rows = pl.ds(pl.multiple_of(hidden + at * span, 128), span)
                    put(down_rows, slice(None), tn_dot(act_ref[tokens, cols], m.cot[tokens]))
                    return carry

                lax.fori_loop(0, hidden // span, grad_step, 0)

            forth_and_back(0, HALF, m.out_sum, m.dh_own)
            m.out_sum[...] += m.middle[...] + as_row(b_down)
            for chunk in range(2):
                if chunk == 0:
                    h2_swap(1).start()
                    h2_swap(0).wait_recv()
                    cot_swap(1).start()
                    cot_swap(0).wait_recv()
                else:
                    grad_part(0, HALF)
                    grad_part(HALF, TILE)
                    h2_swap(1).wait_recv()
                    cot_swap(1).wait_recv()
                    dh2_swap(0).start()
                forth_and_back(HALF + chunk * TILE, TILE, out_acc, dh_acc)
                sent = pl.ds(chunk * TILE, TILE)
                m.dh2_send[sent] = dh_acc[...].astype(LOW)
                m.out_send[sent] = out_acc[...].astype(LOW)
            dh2_swap(1).start()
            grad_part(HALF + TILE, TILE)

        pl.run_scoped(
            chunks_scope,
            pltpu.VMEM((WIDE, hidden), LOW),
            pltpu.VMEM((hidden, WIDE), LOW),
            pltpu.VMEM((TILE, WIDE), F32),
            pltpu.VMEM((TILE, WIDE), F32),
            pltpu.VMEM((2, HALF, HIDDEN), F32),
            pltpu.VMEM((2, HALF, HIDDEN), F32),
            pltpu.VMEM((1, hidden), F32),
            pltpu.VMEM((WIDE, HALF), LOW),
        )
        m.small_ref[...] = jnp.zeros_like(m.small_ref)
        m.small_ref[0:1] = up_sum[:, :WIDE]
        m.small_ref[1:2] = up_sum[:, WIDE:]

    pl.run_scoped(
        mlp_scope,
        pltpu.VMEM((row_len, hidden), LOW),
        pltpu.VMEM((row_len, hidden), LOW),
        pltpu.VMEM((1, hidden), F32),
    )
    if rows_m > 2 * hidden:
        m.grads[pl.ds(2 * hidden, rows_m - 2 * hidden)] = jnp.zeros(
            (rows_m - 2 * hidden, WIDE), LOW
        )
    ring_m.swap_cores()
    ring_m.begin()

    begun = 4
    done = begun + blocks
    out_rows = width
    att_swap.wait_send()

    def back_scope(d_qkv, dk_acc, dv_acc, kt, ht, scores, d_probs, probs, d_scores):
        kt[...] = m.k[...].T
        dk_acc[...] = jnp.zeros_like(dk_acc)
        dv_acc[...] = jnp.zeros_like(dv_acc)
        heads_of = jnp.where(
            lax.broadcasted_iota(jnp.int32, (8, 128), 1) // HEAD_DIM
            == lax.broadcasted_iota(jnp.int32, (8, 128), 0),
            1.0,
            0.0,
        ).astype(LOW)

        ht[...] = m.h1[...].T
        probs[...] = jnp.zeros_like(probs)
        d_scores[...] = jnp.zeros_like(d_scores)

        ring_m.stages(1, 3)

        def middle_back(chunk, carry):
            rows = part(chunk)
            dh2_swap(chunk).wait_recv()
            d_h2 = m.dh_own[rows] + m.dh2_got[rows].astype(F32)
            cot = m.cot[rows].astype(F32)
            centred, inverse = normal_parts(m.middle[rows])
            unit = centred * inverse
            d_middle = cot + norm_back(d_h2, unit, inverse, as_row(gain2))
            m.middle[rows] = d_middle
            d_branch = d_middle.astype(LOW)
            m.d_branch[rows] = d_branch
            m.att_send[rows] = nt_dot(d_branch, m.w_got[...]).astype(LOW)
            m.d_att[rows] = nt_dot(d_branch, m.w_mine[...]).astype(LOW)
            for at, term in enumerate((d_middle, d_h2 * unit, d_h2, cot)):
                m.small_ref[10 + at : 11 + at] += column_sum(term)
            return carry

        lax.fori_loop(0, HALF // TILE, middle_back, 0)
        da_swap.start()
        ring_m.stages(3, 4)
        m.go_send[...] = tn_dot(m.att_got[...], m.d_branch[...]).astype(LOW)
        go_pass.start()
        m.grads[pl.ds(rows_m, out_rows)] = tn_dot(
            m.att32[pl.ds(0, HALF)].astype(LOW), m.d_branch[...]
        ).astype(LOW)

        def enter(block, pair, slot):
            rows, cols = block_rows(block), slice(128 * pair, 128 * pair + 128)
            scores[slot] = nt_dot(m.k[:, cols], split_heads(m.q[rows, cols]))
            d_probs[slot] = nt_dot(m.v[:, cols], split_heads(m.d_att[rows, cols]))

        def weigh(block, pair, slot):
            rows, cols = block_rows(block), slice(128 * pair, 128 * pair + 128)
            weighed = m.d_att[rows, cols].astype(F32) * m.att32[rows, cols]
            high = weighed.astype(LOW)
            rest = (weighed - high.astype(F32)).astype(LOW)
            inner = nt_dot(heads_of, high) + nt_dot(heads_of, rest)
            inner = twice_rows(inner)
            lse = m.lse[block, pair]
            for keys in strips(row_len):
                prob = jnp.exp(scores[slot, keys] + twice(m.bias[keys]) - lse)
                probs[slot, keys] = prob.astype(LOW)
                d_scores[slot, keys] = (prob * (d_probs[slot, keys] - inner)).astype(LOW)

        def leave(block, pair, slot):
            rows, cols = block_rows(block), slice(128 * pair, 128 * pair + 128)
            dk_acc[:, cols] += dot(d_scores[slot], split_heads(m.q[rows, cols]))
            dv_acc[:, cols] += dot(probs[slot], split_heads(m.d_att[rows, cols]))
            d_query = own_blocks(dot(kt[cols], d_scores[slot])).T.astype(LOW)
            d_qkv[0, rows, cols] = d_query * jnp.asarray(SCALE, LOW)

        def two_blocks(couple, carry):
            @pl.when(couple == blocks // 4 - 1)
            def _():
                da_swap.wait_recv()
                go_pass.wait()
                go = m.go_send[w_rows].astype(F32) + m.go_core[...].astype(F32)
                m.go_core[...] = go.astype(LOW)
                go_swap.start()
                out_swap(0).start()
                out_swap(1).start()

            for at in range(2 * pairs):
                block, pair, slot = couple * 2 + at // pairs, at % pairs, at % 2
                before, after = (pair + pairs - 1) % pairs, (pair + 1) % pairs
                block_in = block if pair + 1 < pairs else jnp.minimum(block + 1, blocks - 1)
                block_out = block if pair > 0 else jnp.maximum(block - 1, 0)
                if pair == 0:
                    set_bias(block)
                enter(block_in, after, 1 - slot)
                leave(block_out, before, 1 - slot)
                weigh(block, pair, slot)
                ring_m.stage(at % pairs, begun + block)
            return carry

        enter(0, 0, 0)
        lax.fori_loop(0, blocks // 2, two_blocks, 0)
        leave(blocks - 1, pairs - 1, (blocks * pairs - 1) % 2)
        d_qkv[1] = dk_acc[...].astype(LOW)
        d_qkv[2] = dv_acc[...].astype(LOW)

        for t in range(3):
            full = dot(ht[...], d_qkv[t]).astype(LOW)
            at = rows_m + out_rows + t * width
            m.grads[pl.ds(at, width), pl.ds(0, width)] = full[:width]
            m.grads[pl.ds(at, width), pl.ds(width, width)] = full[width:]
        go_swap.wait_recv()
        own_rows = pl.ds(pl.multiple_of(rows_m + here.core * quarter, 16), quarter)
        own = m.grads[own_rows].astype(F32)
        m.grads[own_rows] = (own + m.go_got[...].astype(F32)).astype(LOW)
        used = out_rows + 3 * width
        if rows_q > used:
            m.grads[pl.ds(rows_m + used, rows_q - used)] = jnp.zeros((rows_q - used, WIDE), LOW)
        ring_q.swap_cores()
        ring_m.stages(done, done + 1)
        ring_q.begin()

        def input_rows(rows):
            terms = [nt_dot(d_qkv[t, rows], m.wq[t]) for t in range(3)]
            return terms[0] + terms[1] + terms[2]

        dh2_swap(0).wait_send()
        dh2_swap(1).wait_send()

        def input_got(chunk, carry):
            m.dh2_send[part(chunk)] = input_rows(other(chunk)).astype(LOW)
            dh1_swap(chunk).start()
            return carry

        lax.fori_loop(0, HALF // TILE, input_got, 0)
        ring_q.stages(1, 2)
        m.small_ref[2:3, :width] = column_sum(d_qkv[0].astype(F32))
        m.small_ref[2:3, width:] = column_sum(d_qkv[2].astype(F32))

        def input_own(chunk, carry):
            m.dh_own[part(chunk)] = input_rows(part(chunk))
            return carry

        lax.fori_loop(0, HALF // TILE, input_own, 0)

    pl.run_scoped(
        back_scope,
        pltpu.VMEM((3, row_len, width), LOW),
        pltpu.VMEM((row_len, width), F32),
        pltpu.VMEM((row_len, width), F32),
        pltpu.VMEM((width, row_len), LOW),
        pltpu.VMEM((WIDE, row_len), LOW),
        pltpu.VMEM((2, row_len, 2 * SPAN), F32),
        pltpu.VMEM((2, row_len, 2 * SPAN), F32),
        pltpu.VMEM((2, row_len, 2 * SPAN), LOW),
        pltpu.VMEM((2, row_len, 2 * SPAN), LOW),
    )

    def both(step, carry):
        for group in range(GROUPS):
            ring_m.stage(group, done + step)
            ring_q.stage(group, step + 1)
        return carry

    left = max(2 * chips - 1 - (done + 1), 0)
    lax.fori_loop(1, left + 1, both, 0)
    out_swap(0).wait_recv()
    out_swap(1).wait_recv()
    out_ref[...] = (m.out_sum[...] + m.out_got[...].astype(F32)).astype(LOW)
    passed = max(chips + 1, left + 2)
    ring_q.stages(left + 2, passed)

    def first_back(chunk, carry):
        rows = part(chunk)
        dh1_swap(chunk).wait_recv()
        d_h1 = m.dh_own[rows] + m.dh2_got[rows].astype(F32)
        centred, inverse = normal_parts(m.x_own[rows].astype(F32))
        unit = centred * inverse
        dx_ref[rows] = (m.middle[rows] + norm_back(d_h1, unit, inverse, as_row(gain1))).astype(LOW)
        m.small_ref[8:9] += column_sum(d_h1 * unit)
        m.small_ref[9:10] += column_sum(d_h1)
        return carry

    lax.fori_loop(0, HALF // TILE, first_back, 0)
    ring_m.arrive()
    writes = []

    def write_out(which, start, rows):
        if not direct:
            spot = pl.ds(start, rows)
            writes.append(local(which, m.result.at[spot], summed_ref.at[spot]))
            writes[-1].start()

    write_out(0, 0, rows_m)
    small.start(m.small_ref)
    at = passed
    for then in (small.core_done, small.mp_done):
        ring_q.stages(at, at + 1)
        then()
        at += 1
    for hop in range(1, 4):
        ring_q.stages(at, at + 1)
        small.hop(hop)
        at += 1
    ring_q.stages(at, 2 * chips - 1)
    small.finish(small_out, 4)
    ring_q.arrive()
    write_out(1, rows_m, rows_q)
    ring_m.drain()
    ring_q.drain()
    for chunk in range(2):
        for copy in (x_swap, cot_swap, h2_swap, out_swap, dh1_swap):
            copy(chunk).wait_send()
    for copy in (w_swap, w_share, w_pass, da_swap, go_swap):
        copy.wait_send()
    for write in writes:
        write.wait()


def whole_block(x, cot, wq, w_out, w_up, w_down, lengths, mask, gain1, bias1, b_qv, b_out, gain2, bias2, b_up, b_down):
    n_dp = lax.axis_size("dp")
    chips = n_dp // 2
    width = w_out.shape[0]
    hidden = w_up.shape[1]
    row_len = 2 * HALF
    rows_m = whole_blocks(2 * hidden, n_dp)
    rows_q = whole_blocks(4 * width, n_dp)
    rows = rows_m + rows_q
    any_spec = pl.BlockSpec(memory_space=pl.ANY)
    vmem = pl.BlockSpec(memory_space=pltpu.VMEM)
    dma = pltpu.SemaphoreType.DMA
    blocks, pairs = row_len // SPAN, width // 128

    def low(*shape):
        return pltpu.VMEM(shape, LOW)

    def full(*shape):
        return pltpu.VMEM(shape, F32)

    scratch = dict(
        x_own=low(HALF, WIDE),
        h1=low(row_len, WIDE),
        cot=low(row_len, WIDE),
        h2=low(row_len, WIDE),
        wq=low(3, WIDE, width),
        w_mine=low(width, WIDE),
        w_got=low(width, WIDE),
        q=low(row_len, width),
        k=low(row_len, width),
        v=low(row_len, width),
        att32=full(row_len, width),
        att_send=low(HALF, width),
        att_got=low(HALF, width),
        lse=full(blocks, pairs, 1, 2 * SPAN),
        key_code=pltpu.VMEM((row_len, 1), jnp.int32),
        query_seg=pltpu.VMEM((blocks, 1, SPAN), jnp.int32),
        bias=full(row_len, SPAN),
        middle=full(HALF, WIDE),
        out_sum=full(HALF, WIDE),
        out_send=low(HALF, WIDE),
        out_got=low(HALF, WIDE),
        dh_own=full(HALF, WIDE),
        dh2_send=low(HALF, WIDE),
        dh2_got=low(HALF, WIDE),
        d_branch=low(HALF, WIDE),
        d_att=low(row_len, width),
        go_send=low(width, WIDE),
        go_core=low(width // 2, WIDE),
        go_got=low(width // 2, WIDE),
        small_ref=full(16, WIDE),
        grads=low(rows, WIDE),
        from_core=low(rows // 2, WIDE),
        result=low(16 if result_in_hbm(chips) else rows, WIDE),
        landed_m=low(chips - 1, rows_m // n_dp, WIDE),
        landed_q=low(chips - 1, rows_q // n_dp, WIDE),
        local_sems=dma((4,)),
        swap_sems=dma((2, 16)),
        pass_sems=dma((6,)),
        own_sems=dma((2, 2 * GROUPS)),
    )
    return pl.pallas_call(
        functools.partial(block_kernel, chips, (rows_m, rows_q)),
        out_shape=(
            jax.ShapeDtypeStruct((rows, WIDE), LOW),
            jax.ShapeDtypeStruct((HALF, WIDE), LOW),
            jax.ShapeDtypeStruct((HALF, WIDE), LOW),
            jax.ShapeDtypeStruct((16, WIDE), F32),
        ),
        in_specs=[any_spec] * 6 + [pl.BlockSpec(memory_space=pltpu.SMEM)] + [vmem] * 9,
        out_specs=(any_spec, vmem, vmem, vmem),
        scratch_shapes=[scratch[name] for name in SCRATCH]
        + segment_sems(chips) * 2
        + small_scratch(chips),
        compiler_params=pltpu.CompilerParams(
            collective_id=0, has_side_effects=True, vmem_limit_bytes=62 * 2**20
        ),
        cost_estimate=pl.CostEstimate(
            flops=int(40e9), bytes_accessed=int(40e6), transcendentals=0
        ),
        name="whole_block",
    )(x, cot, wq, w_out, w_up, w_down, lengths, mask, gain1, bias1, b_qv, b_out, gain2, bias2, b_up, b_down)


def unpack_kernel(base, pieces, sum_ref, small_ref, a_ref, b_ref, *refs):
    low_buf, full_buf, tokens, in_sems, out_sems, copy_sems = refs[-6:]
    up_ref, down_ref, out_ref, qkv_ref, a_out, b_out, up_sum, qv_ref = refs[:8]
    vectors = refs[8:-6]
    span = low_buf.shape[1]
    half = WIDE // 2
    firm = 2 * (WIDE * 2) // span
    starts = [at * span if at < firm else base + (at - firm) * span for at in range(pieces)]
    fetches = [
        pltpu.make_async_copy(sum_ref.at[pl.ds(start, span)], low_buf.at[at], in_sems.at[at])
        for at, start in enumerate(starts)
    ]
    for fetch in fetches:
        fetch.start()
    ins = [
        pltpu.make_async_copy(ref, tokens.at[at], copy_sems.at[0, at])
        for at, ref in enumerate((a_ref, b_ref))
    ]
    outs = [
        pltpu.make_async_copy(tokens.at[at], ref, copy_sems.at[1, at])
        for at, ref in enumerate((a_out, b_out))
    ]
    for copy in ins:
        copy.start()
    writes = []

    def write(at, lane, src, dst):
        writes.append(pltpu.make_async_copy(src, dst, out_sems.at[at, lane]))
        writes[-1].start()

    for at, fetch in enumerate(fetches):
        fetch.wait()
        held = full_buf.at[at]
        held[...] = low_buf[at].astype(F32)
        row = at * span
        if row < 2 * WIDE:
            rows, cols = pl.ds(row % WIDE, span), pl.ds(row // WIDE * WIDE, WIDE)
            write(at, 0, held, up_ref.at[rows, cols])
        elif row < 4 * WIDE:
            write(at, 0, held, down_ref.at[pl.ds(row - 2 * WIDE, span)])
        elif row < 4 * WIDE + half:
            write(at, 0, held, out_ref.at[pl.ds(row - 4 * WIDE, span)])
        else:
            row = row - 4 * WIDE - half
            for side in range(2):
                rows = pl.ds(side * half + row % half, span)
                write(at, side, held.at[:, pl.ds(side * half, half)], qkv_ref.at[row // half, rows])
    for come, go in zip(ins, outs):
        come.wait()
        go.start()
    up_sum[...] = jnp.concatenate([small_ref[0:1], small_ref[1:2]], axis=1).reshape(2 * WIDE)
    qv_ref[0:1] = small_ref[2:3, :half]
    qv_ref[1:2] = small_ref[2:3, half:]
    for at, vector in enumerate(vectors):
        vector[...] = small_ref[8 + at : 9 + at].reshape(WIDE)
    for copy in outs + writes:
        copy.wait()


def unpack(summed, small, block_out, d_block_in, base, hidden, width):
    pieces = 12
    span = WIDE // 2
    any_spec = pl.BlockSpec(memory_space=pl.ANY)
    vmem = pl.BlockSpec(memory_space=pltpu.VMEM)
    shapes = [(WIDE, hidden), (hidden, WIDE), (width, WIDE), (3, WIDE, width)]
    dma = pltpu.SemaphoreType.DMA
    return pl.pallas_call(
        functools.partial(unpack_kernel, base, pieces),
        out_shape=[jax.ShapeDtypeStruct(s, F32) for s in shapes]
        + [jax.ShapeDtypeStruct((HALF, WIDE), LOW)] * 2
        + [jax.ShapeDtypeStruct((hidden,), F32), jax.ShapeDtypeStruct((2, width), F32)]
        + [jax.ShapeDtypeStruct((WIDE,), F32)] * 6,
        in_specs=[any_spec, vmem, any_spec, any_spec],
        out_specs=[any_spec] * 6 + [vmem] * 8,
        scratch_shapes=[
            pltpu.VMEM((pieces, span, WIDE), LOW),
            pltpu.VMEM((pieces, span, WIDE), F32),
            pltpu.VMEM((2, HALF, WIDE), LOW),
            dma((pieces,)),
            dma((pieces, 2)),
            dma((2, 2)),
        ],
        compiler_params=pltpu.CompilerParams(vmem_limit_bytes=62 * 2**20),
        cost_estimate=pl.CostEstimate(flops=int(1e6), bytes_accessed=int(24e6), transcendentals=0),
        name="unpack",
    )(summed, small, block_out, d_block_in)


def local(
    block_in,
    cotangent,
    lengths,
    token_mask,
    ln1_gain,
    ln1_bias,
    w_qkv,
    b_qv,
    w_out,
    b_out,
    ln2_gain,
    ln2_bias,
    w_up,
    b_up,
    w_down,
    b_down,
):
    summed, block_out, d_block_in, small = whole_block(
        block_in,
        cotangent,
        w_qkv.transpose(1, 0, 2),
        w_out,
        w_up,
        w_down,
        lengths,
        token_mask,
        ln1_gain,
        ln1_bias,
        b_qv,
        b_out,
        ln2_gain,
        ln2_bias,
        b_up,
        b_down,
    )
    base = whole_blocks(2 * w_up.shape[1], lax.axis_size("dp"))
    (
        d_w_up,
        d_w_down,
        d_w_out,
        d_w_qkv,
        block_out,
        d_block_in,
        d_b_up,
        d_b_qv,
        d_ln1_gain,
        d_ln1_bias,
        d_b_out,
        d_ln2_gain,
        d_ln2_bias,
        d_b_down,
    ) = unpack(summed, small, block_out, d_block_in, base, w_up.shape[1], w_out.shape[0])
    return (
        block_out,
        d_block_in,
        d_ln1_gain,
        d_ln1_bias,
        d_w_qkv.transpose(1, 0, 2),
        d_b_qv,
        d_w_out,
        d_b_out,
        d_ln2_gain,
        d_ln2_bias,
        d_w_up,
        d_b_up,
        d_w_down,
        d_b_down,
    )


def solution(mesh):
    in_specs = (
        P(("dp", "mp"), None),
        P(("dp", "mp"), None),
        P("dp", None),
        P("dp", None),
        P(),
        P(),
        P(None, None, "mp"),
        P(None, "mp"),
        P("mp", None),
        P(),
        P(),
        P(),
        P(None, "mp"),
        P("mp"),
        P("mp", None),
        P(),
    )
    out_specs = (
        P(("dp", "mp"), None),
        P(("dp", "mp"), None),
        P(),
        P(),
        P(None, None, "mp"),
        P(None, "mp"),
        P("mp", None),
        P(),
        P(),
        P(),
        P(None, "mp"),
        P("mp"),
        P("mp", None),
        P(),
    )
    return jax.shard_map(local, mesh=mesh, in_specs=in_specs, out_specs=out_specs, check_vma=False)
```

```python
import functools
import jax
import jax.numpy as jnp
from jax import lax
from jax.experimental import pallas as pl
from jax.experimental.pallas import tpu as pltpu
from jax.sharding import PartitionSpec as P

HEAD_DIM = 64
MESH = pl.DeviceIdType.MESH
WIDE = 768
GROUPS = 3
LANES = 128


def ring_place(chip, chips):
    return jnp.where(chip % 2 == 0, chip // 2, chips - 1 - chip // 2)


def ring_chip(place, chips):
    return jnp.where(place < chips // 2, 2 * place, 2 * (chips - 1 - place) + 1)


def send_slots(chips):
    return min(chips, 8)


def whole_blocks(rows, n_dp):
    unit = 16 * n_dp
    return -(-rows // unit) * unit


class Here:
    def __init__(self, chips):
        dp, mp = lax.axis_index("dp"), lax.axis_index("mp")
        self.chips = chips
        self.core, chip = dp % 2, dp // 2
        self.place = ring_place(chip, chips)
        self.following = {"dp": ring_chip((self.place + 1) % chips, chips) * 2 + self.core}
        self.previous = {"dp": ring_chip((self.place + chips - 1) % chips, chips) * 2 + self.core}
        self.sibling = {"dp": chip * 2 + 1 - self.core}
        self.partner = {"mp": 1 - mp}
        self.side = chip % 2
        self.beside = {"dp": (chip + 1 - 2 * self.side) * 2 + self.core}


def remote(src, dst, send, recv, to):
    return pltpu.make_async_remote_copy(
        src_ref=src, dst_ref=dst, send_sem=send, recv_sem=recv, device_id=to, device_id_type=MESH
    )


class Segment:
    def __init__(self, here, base, rows, grads, from_core, landed, result, sems, own_sems=None):
        self.here, self.base, self.chips = here, base, here.chips
        self.block = rows // (2 * here.chips)
        self.slots = send_slots(here.chips)
        self.own_sems = own_sems
        self.grads, self.from_core, self.landed, self.result = grads, from_core, landed, result
        (
            self.core_send,
            self.core_recv,
            self.rs_send,
            self.rs_recv,
            self.ag_send,
            self.ag_recv,
            self.pair_send,
            self.pair_recv,
        ) = sems

    def rows_of(self, core, blk):
        start = self.base + (core * self.chips + blk) * self.block
        return pl.ds(pl.multiple_of(start, 16), self.block)

    def near_rows(self, blk):
        start = self.base // 2 + blk * self.block
        return pl.ds(pl.multiple_of(start, 16), self.block)

    def columns(self, ring):
        return pl.ds(ring * LANES, LANES)

    def rs_block(self, ring, step):
        if ring < GROUPS:
            return (self.here.place + 2 * self.chips - 1 - step) % self.chips
        return (self.here.place + 1 + step) % self.chips

    def ag_block(self, ring, step):
        if ring < GROUPS:
            return (self.here.place + self.chips - step) % self.chips
        return (self.here.place + step) % self.chips

    def toward(self, ring):
        return self.here.following if ring < GROUPS else self.here.previous

    def core_copy(self, half, step):
        blk = self.rs_block(half * GROUPS, step)
        cols = pl.ds(half * GROUPS * LANES, GROUPS * LANES)
        return remote(
            self.grads.at[self.rows_of(1 - self.here.core, blk), cols],
            self.from_core.at[self.near_rows(blk), cols],
            self.core_send.at[half, step],
            self.core_recv.at[half, step],
            self.here.sibling,
        )

    def rs_copy(self, ring, step):
        cols = self.columns(ring)
        return remote(
            self.grads.at[self.rows_of(self.here.core, self.rs_block(ring, step)), cols],
            self.landed.at[step, :, cols],
            self.rs_send.at[ring, step % self.slots],
            self.rs_recv.at[ring, step],
            self.toward(ring),
        )

    def result_copy(self, ring, step, send, recv, to, wide=1):
        rows = self.rows_of(self.here.core, self.ag_block(ring, step))
        cols = pl.ds(ring * LANES, wide * LANES)
        spot = self.result.at[rows, cols]
        own = self.own_sems is not None and isinstance(step, int) and step == 0
        held = self.grads.at[rows, cols] if own else spot
        lane = ring // wide
        return remote(held, spot, send.at[lane, step % self.slots], recv.at[lane, step], to)

    def own_copy(self, ring):
        spot = (self.rows_of(self.here.core, self.here.place), self.columns(ring))
        return pltpu.make_async_copy(
            self.grads.at[spot], self.result.at[spot], self.own_sems.at[ring]
        )

    def ag_copy(self, ring, step):
        return self.result_copy(ring, step, self.ag_send, self.ag_recv, self.toward(ring))

    def pair_copy(self, way, step):
        to = self.here.sibling
        return self.result_copy(way * GROUPS, step, self.pair_send, self.pair_recv, to, GROUPS)

    def pass_on(self, group, step):
        if group == GROUPS - 1:
            self.send(self.pair_copy, 0, step)
            self.send(self.pair_copy, 1, step)

    def summed(self, ring, step, first):
        blk = self.rs_block(ring, step)
        rows, cols = self.rows_of(self.here.core, blk), self.columns(ring)
        value = self.grads[rows, cols].astype(jnp.float32)
        value = value + self.from_core[self.near_rows(blk), cols].astype(jnp.float32)
        if not first:
            value = value + self.landed[step - 1, :, cols].astype(jnp.float32)
        return rows, cols, value.astype(jnp.bfloat16)

    def send(self, copy, ring, step):
        if self.slots < self.chips:

            @pl.when(step >= self.slots)
            def _():
                copy(ring, step - self.slots).wait_send()

        copy(ring, step).start()

    def swap_cores(self):
        def start(step, carry):
            self.core_copy(0, step).start()
            self.core_copy(1, step).start()
            return carry

        lax.fori_loop(0, self.chips, start, 0)

    def wait_core(self, step):
        self.core_copy(0, step).wait_recv()
        self.core_copy(1, step).wait_recv()

    def begin(self):
        self.wait_core(0)
        for group in range(GROUPS):
            for ring in (group, group + GROUPS):
                rows, cols, value = self.summed(ring, 0, True)
                self.grads[rows, cols] = value
                self.send(self.rs_copy, ring, 0)

    def stage(self, group, step):
        n = self.chips
        rings = (group, group + GROUPS)

        @pl.when(step <= n - 2)
        def _():
            if group == 0:
                self.wait_core(step)
            for ring in rings:
                self.rs_copy(ring, step - 1).wait_recv()
                rows, cols, value = self.summed(ring, step, False)
                self.grads[rows, cols] = value
                self.send(self.rs_copy, ring, step)

        @pl.when(step == n - 1)
        def _():
            if group == 0:
                self.wait_core(n - 1)
            for ring in rings:
                self.rs_copy(ring, n - 2).wait_recv()
                rows, cols, value = self.summed(ring, n - 1, False)
                if self.own_sems is None:
                    self.result[rows, cols] = value
                else:
                    self.grads[rows, cols] = value
                    self.own_copy(ring).start()
                self.send(self.ag_copy, ring, 0)
            self.pass_on(group, 0)

        @pl.when((step >= n) & (step <= 2 * n - 3))
        def _():
            for ring in rings:
                self.ag_copy(ring, step - n).wait_recv()
                self.send(self.ag_copy, ring, step - n + 1)
            self.pass_on(group, step - n + 1)

        @pl.when(step == 2 * n - 2)
        def _():
            for ring in rings:
                self.ag_copy(ring, n - 2).wait_recv()
            self.pass_on(group, n - 1)

    def stages(self, first, last):
        def run(step, carry):
            for group in range(GROUPS):
                self.stage(group, step)
            return carry

        lax.fori_loop(first, last, run, 0)

    def arrive(self):
        def run(step, carry):
            for way in range(2):
                self.pair_copy(way, step).wait_recv()
            return carry

        lax.fori_loop(0, self.chips, run, 0)
        if self.own_sems is not None:
            for ring in range(2 * GROUPS):
                self.own_copy(ring).wait()

    def drain(self):
        def cores(step, carry):
            self.core_copy(0, step).wait_send()
            self.core_copy(1, step).wait_send()
            return carry

        def pairs(step, carry):
            for way in range(2):
                self.pair_copy(way, step).wait_send()
            return carry

        def ring_steps(step, carry):
            for ring in range(2 * GROUPS):
                self.rs_copy(ring, step).wait_send()
                self.ag_copy(ring, step).wait_send()
            return carry

        n, slots = self.chips, self.slots
        lax.fori_loop(0, n, cores, 0)
        lax.fori_loop(n - slots, n, pairs, 0)
        lax.fori_loop(max(n - 1 - slots, 0), n - 1, ring_steps, 0)


def segment_sems(chips):
    dma = pltpu.SemaphoreType.DMA
    rings = 2 * GROUPS
    slots = send_slots(chips)
    both = [dma((rings, slots)), dma((rings, chips))]
    return [dma((2, chips))] * 2 + both * 2 + [dma((2, slots)), dma((2, chips))]


class Small:
    def __init__(self, here, from_core, from_mp, every, pair_sems, ring_sems):
        self.here, self.from_core, self.from_mp, self.every = here, from_core, from_mp, every
        self.pair_sems, self.ring_sems = pair_sems, ring_sems
        self.forward = here.chips // 2
        self.backward = here.chips - 1 - self.forward

    def pair(self, which, src, dst, to):
        return remote(src, dst, self.pair_sems.at[0, which], self.pair_sems.at[1, which], to)

    def start(self, src):
        self.src = src
        self.to_core = self.pair(0, src, self.from_core, self.here.sibling)
        self.to_core.start()

    def core_done(self):
        self.to_core.wait()
        place = self.here.place
        self.every[place] = self.src[...] + self.from_core[...]
        spot = self.every.at[place, pl.ds(8, 8)]
        self.to_mp = self.pair(1, spot, self.from_mp, self.here.partner)
        self.to_mp.start()

    def mp_done(self):
        self.to_mp.wait()
        place = self.here.place
        self.every[place, pl.ds(8, 8)] = self.every[place, pl.ds(8, 8)] + self.from_mp[...]
        self.step(0, 0).start()
        if self.backward:
            self.step(1, 0).start()

    def step(self, way, step):
        n = self.here.chips
        at = (self.here.place + n - step) % n if way == 0 else (self.here.place + step) % n
        spot = self.every.at[at]
        to = self.here.following if way == 0 else self.here.previous
        sems = self.ring_sems
        return remote(spot, spot, sems.at[0, way, step], sems.at[1, way, step], to)

    def hop(self, step):
        for way, count in ((0, self.forward), (1, self.backward)):

            @pl.when(step < count)
            def _():
                self.step(way, step - 1).wait_recv()
                self.step(way, step).start()

    def finish(self, out, hops):
        def run(step, carry):
            self.hop(step)
            return carry

        if hops < self.forward:
            lax.fori_loop(hops, self.forward, run, 0)
        self.step(0, self.forward - 1).wait_recv()
        if self.backward:
            self.step(1, self.backward - 1).wait_recv()
        out[...] = self.every[0]

        def add(chip, carry):
            out[...] += self.every[chip]
            return carry

        lax.fori_loop(1, self.here.chips, add, 0)

        def sent(way, count):
            def run(step, carry):
                self.step(way, step).wait_send()
                return carry

            lax.fori_loop(0, count, run, 0)

        sent(0, self.forward)
        sent(1, self.backward)


def small_scratch(chips):
    dma = pltpu.SemaphoreType.DMA
    return [
        pltpu.VMEM((16, WIDE), jnp.float32),
        pltpu.VMEM((8, WIDE), jnp.float32),
        pltpu.VMEM((chips, 16, WIDE), jnp.float32),
        dma((2, 2)),
        dma((2, 2, chips)),
    ]


LOW = jnp.bfloat16
F32 = jnp.float32
HALF = 512
TILE = 256
SPAN = 128
STRIP = 32
HIDDEN = 256
EPS = 1e-06
FAR = -1e30
SCALE = HEAD_DIM**-0.5
NT = (((1,), (1,)), ((), ()))
TN = (((0,), (0,)), ((), ()))


def nt_dot(a, b):
    return lax.dot_general(a, b, NT, preferred_element_type=F32)


def tn_dot(a, b):
    return lax.dot_general(a, b, TN, preferred_element_type=F32)


def dot(a, b):
    return jnp.dot(a, b, preferred_element_type=F32)


def normal_parts(values):
    centred = values - jnp.mean(values, axis=-1, keepdims=True)
    spread = jnp.mean(centred * centred, axis=-1, keepdims=True)
    return centred, lax.rsqrt(spread + EPS)


def norm_back(d_out, unit, inverse, gain):
    e = d_out * gain
    share = e - jnp.mean(e, -1, keepdims=True)
    return inverse * (share - unit * jnp.mean(e * unit, -1, keepdims=True))


def column_sum(values):
    return jnp.sum(values, axis=0, keepdims=True)


def split_heads(pair):
    low_lanes = lax.broadcasted_iota(jnp.int32, pair.shape, 1) < HEAD_DIM
    zero = jnp.zeros_like(pair)
    return jnp.concatenate([jnp.where(low_lanes, pair, zero), jnp.where(low_lanes, zero, pair)])


def own_blocks(both):
    return jnp.concatenate([both[:HEAD_DIM, :SPAN], both[HEAD_DIM:, SPAN:]], axis=0)


def twice(values):
    return jnp.concatenate([values, values], axis=1)


SCRATCH = (
    "x_own", "h1", "cot", "h2", "wq", "w_mine", "w_got", "q", "k", "v", "att32", "att_send",
    "att_got", "lse", "key_code", "query_seg", "bias", "middle", "out_sum", "out_send", "out_got",
    "dh_own", "dh2_send", "dh2_got", "d_branch", "d_att", "go_send", "go_core", "go_got",
    "small_ref", "grads", "from_core", "result", "landed_m", "landed_q", "local_sems", "swap_sems",
    "pass_sems", "own_sems",
)


def twice_rows(values):
    return jnp.concatenate([values[0:1], values[1:2]], axis=1)


def fold(values, op, rows=8):
    while values.shape[0] > rows:
        half = values.shape[0] // 2
        values = op(values[:half], values[half:])
    return values


def strips(rows):
    return [slice(at, at + STRIP) for at in range(0, rows, STRIP)]


def result_in_hbm(chips):
    return chips > 8


class Names:
    pass


def block_kernel(chips, sizes, *refs):
    (
        x_hbm,
        cot_hbm,
        wq_hbm,
        w_out_hbm,
        up_hbm,
        down_hbm,
        lengths,
        mask_ref,
        gain1,
        bias1,
        b_qv,
        b_out,
        gain2,
        bias2,
        b_up,
        b_down,
        summed_ref,
        out_ref,
        dx_ref,
        small_out,
    ) = refs[:20]
    m = Names()
    for name, ref in zip(SCRATCH, refs[20:]):
        setattr(m, name, ref)
    more = refs[20 + len(SCRATCH) :]
    sems_m, sems_q, small_refs = more[:8], more[8:16], more[16:]
    rows_m, rows_q = sizes
    here = Here(chips)
    direct = result_in_hbm(chips)
    result = summed_ref if direct else m.result
    ring_m = Segment(
        here, 0, rows_m, m.grads, m.from_core, m.landed_m, result, sems_m,
        m.own_sems.at[0] if direct else None,
    )
    ring_q = Segment(
        here, rows_m, rows_q, m.grads, m.from_core, m.landed_q, result, sems_q,
        m.own_sems.at[1] if direct else None,
    )
    small = Small(here, *small_refs)
    width = m.k.shape[1]
    pairs = width // 128
    row_len = 2 * HALF
    hidden = up_hbm.shape[1]
    blocks = row_len // SPAN

    def local(which, src, dst):
        return pltpu.make_async_copy(src, dst, m.local_sems.at[which])

    def swapped(which, src, dst):
        return remote(src, dst, m.swap_sems.at[0, which], m.swap_sems.at[1, which], here.partner)

    def part(chunk):
        return pl.ds(pl.multiple_of(chunk * TILE, TILE), TILE)

    def other(chunk):
        return pl.ds(pl.multiple_of(HALF + chunk * TILE, TILE), TILE)

    def x_swap(chunk):
        return swapped(chunk, x_hbm.at[part(chunk)], m.h1.at[other(chunk)])

    def cot_swap(chunk):
        return swapped(2 + chunk, cot_hbm.at[part(chunk)], m.cot.at[other(chunk)])

    def h2_swap(chunk):
        return swapped(4 + chunk, m.h2.at[part(chunk)], m.h2.at[other(chunk)])

    def dh2_swap(chunk):
        return swapped(6 + chunk, m.dh2_send.at[part(chunk)], m.dh2_got.at[part(chunk)])

    def out_swap(chunk):
        return swapped(8 + chunk, m.out_send.at[part(chunk)], m.out_got.at[part(chunk)])

    def dh1_swap(chunk):
        return swapped(10 + chunk, m.dh2_send.at[part(chunk)], m.dh2_got.at[part(chunk)])

    quarter = width // 2
    w_rows = pl.ds(pl.multiple_of(here.core * quarter, 16), quarter)
    piece = pl.ds(pl.multiple_of((here.core * 2 + here.side) * (quarter // 2), 16), quarter // 2)
    w_swap = swapped(12, w_out_hbm.at[piece], m.w_got.at[piece])
    w_share = remote(
        m.w_got.at[piece], m.w_got.at[piece], m.pass_sems.at[4], m.pass_sems.at[5], here.beside
    )
    w_pass = remote(
        m.w_got.at[w_rows], m.w_got.at[w_rows], m.pass_sems.at[0], m.pass_sems.at[1], here.sibling
    )
    att_swap = swapped(13, m.att_send, m.att_got)
    da_swap = swapped(14, m.att_send, m.d_att.at[pl.ds(HALF, HALF)])
    other_rows = pl.ds(pl.multiple_of((1 - here.core) * quarter, 16), quarter)
    go_pass = remote(
        m.go_send.at[other_rows], m.go_core, m.pass_sems.at[2], m.pass_sems.at[3], here.sibling
    )
    go_swap = swapped(15, m.go_core, m.go_got)

    def as_row(ref):
        return ref[...].reshape(1, ref.shape[0])

    load_x = local(0, x_hbm, m.x_own)
    load_wq = local(1, wq_hbm, m.wq)
    load_w = local(2, w_out_hbm, m.w_mine)
    load_cot = local(3, cot_hbm, m.cot.at[pl.ds(0, HALF)])
    for load in (load_x, load_wq, load_w, load_cot):
        load.start()
    barrier = pltpu.get_barrier_semaphore()
    near = (here.sibling, here.following, here.previous, here.partner, here.beside)
    for device in near:
        pl.semaphore_signal(barrier, inc=1, device_id=device, device_id_type=MESH)
    pl.semaphore_wait(barrier, len(near))
    x_swap(0).start()

    shift = lax.axis_index("mp") * HALF
    ends, total = [], lengths[0, 0]
    for slot in range(lengths.shape[1]):
        ends.append(total)
        if slot + 1 < lengths.shape[1]:
            total = total + lengths[0, slot + 1]

    def segment(shape, axis):
        at = (lax.broadcasted_iota(jnp.int32, shape, axis) + shift) % row_len
        found = jnp.zeros(shape, jnp.int32)
        for end in ends:
            found = found + (at >= end).astype(jnp.int32)
        return found

    seg_row = segment((1, row_len), 1)
    for block in range(blocks):
        m.query_seg[block] = seg_row[:, block * SPAN : (block + 1) * SPAN]
    mask = mask_ref[...]
    turned = jnp.concatenate([mask[:, HALF:], mask[:, :HALF]], axis=1)
    mask = jnp.where(shift == 0, mask, turned)
    code = jnp.where(mask == 1, seg_row, -1).astype(F32)
    m.key_code[...] = jnp.broadcast_to(code, (8, row_len)).T[:, :1].astype(jnp.int32)

    def project(values, rows):
        centred, inverse = normal_parts(values.astype(F32))
        h1 = (centred * inverse * as_row(gain1) + as_row(bias1)).astype(LOW)
        m.h1[rows] = h1
        m.q[rows] = ((dot(h1, m.wq[0]) + b_qv[0:1]) * SCALE).astype(LOW)
        m.k[rows] = dot(h1, m.wq[1]).astype(LOW)
        m.v[rows] = (dot(h1, m.wq[2]) + b_qv[1:2]).astype(LOW)

    load_x.wait()
    load_wq.wait()

    def project_own(chunk, carry):
        project(m.x_own[part(chunk)], part(chunk))
        return carry

    lax.fori_loop(0, HALF // TILE, project_own, 0)
    x_swap(1).start()

    def project_got(chunk, carry):
        x_swap(chunk).wait_recv()

        @pl.when(chunk == HALF // TILE - 1)
        def _():
            w_swap.start()
            cot_swap(0).start()

        project(m.h1[other(chunk)], other(chunk))
        return carry

    lax.fori_loop(0, HALF // TILE, project_got, 0)

    def set_bias(block):
        shape = (row_len, SPAN)
        key_at = lax.broadcasted_iota(jnp.int32, shape, 0)
        query_at = lax.broadcasted_iota(jnp.int32, shape, 1) + block * SPAN
        allowed = (m.key_code[...] == m.query_seg[block]) | (key_at == query_at)
        m.bias[...] = jnp.where(allowed, 0.0, FAR)

    def block_rows(block):
        return pl.ds(pl.multiple_of(block * SPAN, SPAN), SPAN)

    def attend_scope(vt, scores, raised):
        vt[...] = m.v[...].T

        def block_at(at):
            return (at + blocks // 2) % blocks

        def score(block, pair, slot):
            cols = slice(128 * pair, 128 * pair + 128)
            scores[slot] = nt_dot(m.k[:, cols], split_heads(m.q[block_rows(block), cols]))

        def weigh(slot):
            held, out = scores.at[slot], raised.at[slot]
            top = None
            for keys in strips(row_len):
                here = held[keys] + twice(m.bias[keys])
                top = here if top is None else jnp.maximum(top, here)
            top = jnp.max(fold(top, jnp.maximum), axis=0, keepdims=True)
            whole = None
            for keys in strips(row_len):
                here = jnp.exp(held[keys] + twice(m.bias[keys]) - top)
                out[keys] = here.astype(LOW)
                whole = here if whole is None else whole + here
            return top, jnp.sum(fold(whole, jnp.add), axis=0, keepdims=True)

        def gather(block, pair, slot, top, whole):
            cols = slice(128 * pair, 128 * pair + 128)
            outs = own_blocks(dot(vt[cols], raised[slot]) / whole)
            m.att32[block_rows(block), cols] = outs.T
            m.lse[block, pair : pair + 1] = top + jnp.log(whole)

        def attend(couple, carry):
            @pl.when(couple == blocks // 8)
            def _():
                w_swap.wait_recv()
                w_share.start()

            @pl.when(couple == blocks // 4)
            def _():
                m.att_send[...] = m.att32[pl.ds(HALF, HALF)].astype(LOW)
                att_swap.start()
                w_share.wait_recv()
                w_pass.start()

            held = None
            for at in range(2 * pairs):
                pair, slot = at % pairs, at % 2
                turn = couple * 2 + at // pairs
                block = block_at(turn)
                if pair == 0:
                    set_bias(block)
                if pair + 1 < pairs:
                    score(block, pair + 1, 1 - slot)
                else:
                    score(block_at(jnp.minimum(turn + 1, blocks - 1)), 0, 1 - slot)
                now = weigh(slot)
                if held is not None:
                    gather(*held)
                held = (block, pair, slot, *now)
            gather(*held)
            return carry

        score(block_at(0), 0, 0)
        lax.fori_loop(0, blocks // 2, attend, 0)

    pl.run_scoped(
        attend_scope,
        pltpu.VMEM((width, row_len), LOW),
        pltpu.VMEM((2, row_len, 2 * SPAN), F32),
        pltpu.VMEM((2, row_len, 2 * SPAN), LOW),
    )

    load_w.wait()
    w_pass.wait_recv()
    att_swap.wait_recv()
    cot_swap(1).start()

    def branch(chunk, carry):
        rows = part(chunk)
        got = dot(m.att32[rows].astype(LOW), m.w_mine[...]) + dot(m.att_got[rows], m.w_got[...])
        middle = m.x_own[rows].astype(F32) + got + as_row(b_out)
        m.middle[rows] = middle
        centred, inverse = normal_parts(middle)
        m.h2[rows] = (centred * inverse * as_row(gain2) + as_row(bias2)).astype(LOW)

        @pl.when(chunk == 0)
        def _():
            h2_swap(0).start()

        return carry

    lax.fori_loop(0, HALF // TILE, branch, 0)
    load_cot.wait()

    if rows_m > 2 * hidden:
        m.grads[pl.ds(2 * hidden, rows_m - 2 * hidden)] = jnp.zeros(
            (rows_m - 2 * hidden, WIDE), LOW
        )

    def mlp_scope(act_ref, pre_ref, up_sum):
        def chunks_scope(up, down, pre_buf, d_buf, up_row, ht):
            load_up, load_down = local(0, up_hbm, up), local(1, down_hbm, down)
            load_up.start()
            load_down.start()
            load_up.wait()
            load_down.wait()
            up_sum[...] = jnp.zeros_like(up_sum)
            up_row[...] = as_row(b_up)
            tiles = hidden // HIDDEN

            def through(begin, tokens):
                rows = pl.ds(begin, tokens)

                def enter(tile):
                    cols = slice(tile * HIDDEN, tile * HIDDEN + HIDDEN)
                    pre_buf[tile % 2, :tokens] = dot(m.h2[rows], up[:, cols])
                    d_buf[tile % 2, :tokens] = nt_dot(m.cot[rows], down[cols])

                def bend(tile):
                    cols = slice(tile * HIDDEN, tile * HIDDEN + HIDDEN)
                    shift_up = up_row[:, cols]
                    total = None
                    for at in range(0, tokens, STRIP):
                        pre = pre_buf[tile % 2, at : at + STRIP] + shift_up
                        cdf = 0.5 * (1.0 + lax.erf(pre * 0.7071067811865476))
                        slope = cdf + pre * (jnp.exp(-0.5 * pre * pre) * 0.3989422804014327)
                        d_pre = (d_buf[tile % 2, at : at + STRIP] * slope).astype(LOW)
                        spot = pl.ds(begin + at, STRIP)
                        act_ref[spot, cols] = (pre * cdf).astype(LOW)
                        pre_ref[spot, cols] = d_pre
                        d_pre = d_pre.astype(F32)
                        total = d_pre if total is None else total + d_pre
                    up_sum[:, cols] += column_sum(fold(total, jnp.add))

                enter(0)
                for tile in range(tiles):
                    if tile + 1 < tiles:
                        enter(tile + 1)
                    bend(tile)

            def grad_part(begin, count):
                span = WIDE // 2
                tokens = pl.ds(begin, count)
                ht[:, :count] = m.h2[tokens].T

                def put(rows, cols, value):
                    if begin:
                        value = value + m.grads[rows, cols].astype(F32)
                    m.grads[rows, cols] = value.astype(LOW)

                def grad_step(at, carry):
                    cols = pl.ds(pl.multiple_of(at * span, 128), span)
                    up_rows = pl.ds(pl.multiple_of(at // 2 * WIDE, WIDE), WIDE)
                    up_cols = pl.ds(pl.multiple_of(at % 2 * span, 128), span)
                    put(up_rows, up_cols, dot(ht[:, :count], pre_ref[tokens, cols]))
                    down_rows = pl.ds(pl.multiple_of(hidden + at * span, 128), span)
                    put(down_rows, slice(None), tn_dot(act_ref[tokens, cols], m.cot[tokens]))
                    return carry

                lax.fori_loop(0, hidden // span, grad_step, 0)

            def products_out(begin, tokens):
                rows = pl.ds(begin, tokens)
                return dot(act_ref[rows], down[...]), nt_dot(pre_ref[rows], up[...])

            through(0, HALF)
            h2_swap(1).start()
            for chunk in range(2):
                rows = pl.ds(chunk * TILE, TILE)
                out, m.dh_own[rows] = products_out(chunk * TILE, TILE)
                m.out_sum[rows] = out + m.middle[rows] + as_row(b_down)
            for chunk in range(2):
                begin = HALF + chunk * TILE
                if chunk == 0:
                    grad_part(0, HALF)
                    h2_swap(0).wait_recv()
                    cot_swap(0).wait_recv()
                else:
                    grad_part(HALF, TILE)
                    h2_swap(1).wait_recv()
                    cot_swap(1).wait_recv()
                    dh2_swap(0).start()
                through(begin, TILE)
                if chunk == 1:
                    grad_part(begin, TILE)
                    ring_m.swap_cores()
                    ring_m.begin()
                out, d_h = products_out(begin, TILE)
                sent = pl.ds(chunk * TILE, TILE)
                m.dh2_send[sent] = d_h.astype(LOW)
                m.out_send[sent] = out.astype(LOW)
            dh2_swap(1).start()

        pl.run_scoped(
            chunks_scope,
            pltpu.VMEM((WIDE, hidden), LOW),
            pltpu.VMEM((hidden, WIDE), LOW),
            pltpu.VMEM((2, HALF, HIDDEN), F32),
            pltpu.VMEM((2, HALF, HIDDEN), F32),
            pltpu.VMEM((1, hidden), F32),
            pltpu.VMEM((WIDE, HALF), LOW),
        )
        m.small_ref[...] = jnp.zeros_like(m.small_ref)
        m.small_ref[0:1] = up_sum[:, :WIDE]
        m.small_ref[1:2] = up_sum[:, WIDE:]

    pl.run_scoped(
        mlp_scope,
        pltpu.VMEM((row_len, hidden), LOW),
        pltpu.VMEM((row_len, hidden), LOW),
        pltpu.VMEM((1, hidden), F32),
    )
    begun = 1
    done = begun + blocks // 2 * pairs
    out_rows = width
    att_swap.wait_send()

    def back_scope(d_qkv, dk_acc, dv_acc, kt, ht, scores, d_probs, probs, d_scores):
        kt[...] = m.k[...].T
        dk_acc[...] = jnp.zeros_like(dk_acc)
        dv_acc[...] = jnp.zeros_like(dv_acc)
        heads_of = jnp.where(
            lax.broadcasted_iota(jnp.int32, (8, 128), 1) // HEAD_DIM
            == lax.broadcasted_iota(jnp.int32, (8, 128), 0),
            1.0,
            0.0,
        ).astype(LOW)

        ht[...] = m.h1[...].T
        probs[...] = jnp.zeros_like(probs)
        d_scores[...] = jnp.zeros_like(d_scores)

        def middle_back(chunk):
            dh2_swap(chunk).wait_recv()

            def some_rows(at, carry):
                rows = pl.ds(pl.multiple_of(chunk * TILE + at * SPAN, SPAN), SPAN)
                d_h2 = m.dh_own[rows] + m.dh2_got[rows].astype(F32)
                cot = m.cot[rows].astype(F32)
                centred, inverse = normal_parts(m.middle[rows])
                unit = centred * inverse
                d_middle = cot + norm_back(d_h2, unit, inverse, as_row(gain2))
                m.middle[rows] = d_middle
                d_branch = d_middle.astype(LOW)
                m.d_branch[rows] = d_branch
                m.att_send[rows] = nt_dot(d_branch, m.w_got[...]).astype(LOW)
                m.d_att[rows] = nt_dot(d_branch, m.w_mine[...]).astype(LOW)
                for at, term in enumerate((d_middle, d_h2 * unit, d_h2, cot)):
                    m.small_ref[10 + at : 11 + at] += column_sum(term)
                return carry

            lax.fori_loop(0, TILE // SPAN, some_rows, 0)

        def out_grads():
            def send_rows(pair, carry):
                cols = pl.ds(pl.multiple_of(pair * 128, 128), 128)
                m.go_send[cols] = tn_dot(m.att_got[:, cols], m.d_branch[...]).astype(LOW)
                return carry

            def own_rows(pair, carry):
                cols = pl.ds(pl.multiple_of(pair * 128, 128), 128)
                rows = pl.ds(pl.multiple_of(rows_m + pair * 128, 128), 128)
                held = m.att32[pl.ds(0, HALF), cols].astype(LOW)
                m.grads[rows] = tn_dot(held, m.d_branch[...]).astype(LOW)
                return carry

            lax.fori_loop(0, pairs, send_rows, 0)
            go_pass.start()
            lax.fori_loop(0, pairs, own_rows, 0)

        def out_grads_on():
            go_pass.wait()
            go = m.go_send[w_rows].astype(F32) + m.go_core[...].astype(F32)
            m.go_core[...] = go.astype(LOW)
            go_swap.start()
            out_swap(0).start()
            out_swap(1).start()

        def enter(block, pair, slot):
            rows, cols = block_rows(block), slice(128 * pair, 128 * pair + 128)
            scores[slot] = nt_dot(m.k[:, cols], split_heads(m.q[rows, cols]))
            d_probs[slot] = nt_dot(m.v[:, cols], split_heads(m.d_att[rows, cols]))

        def weigh(block, pair, slot):
            rows, cols = block_rows(block), slice(128 * pair, 128 * pair + 128)
            weighed = m.d_att[rows, cols].astype(F32) * m.att32[rows, cols]
            high = weighed.astype(LOW)
            rest = (weighed - high.astype(F32)).astype(LOW)
            inner = nt_dot(heads_of, high) + nt_dot(heads_of, rest)
            inner = twice_rows(inner)
            lse = m.lse[block, pair : pair + 1]
            for keys in strips(row_len):
                prob = jnp.exp(scores[slot, keys] + twice(m.bias[keys]) - lse)
                probs[slot, keys] = prob.astype(LOW)
                d_scores[slot, keys] = (prob * (d_probs[slot, keys] - inner)).astype(LOW)

        def leave(block, pair, slot):
            rows, cols = block_rows(block), slice(128 * pair, 128 * pair + 128)
            dk_acc[:, cols] += dot(d_scores[slot], split_heads(m.q[rows, cols]))
            dv_acc[:, cols] += dot(probs[slot], split_heads(m.d_att[rows, cols]))
            d_query = own_blocks(dot(kt[cols], d_scores[slot])).T.astype(LOW)
            d_qkv[0, rows, cols] = d_query * jnp.asarray(SCALE, LOW)

        def two_blocks(couple, carry):
            for at in range(2 * pairs):
                block, pair, slot = couple * 2 + at // pairs, at % pairs, at % 2
                before, after = (pair + pairs - 1) % pairs, (pair + 1) % pairs
                block_in = block if pair + 1 < pairs else jnp.minimum(block + 1, blocks - 1)
                block_out = block if pair > 0 else jnp.maximum(block - 1, 0)
                if pair == 0:
                    set_bias(block)
                if at == 2 * pairs - 1:

                    @pl.when(couple == blocks // 8 - 1)
                    def _():
                        middle_back(1)
                        da_swap.start()
                        out_grads()

                    @pl.when(couple == blocks // 4 - 1)
                    def _():
                        da_swap.wait_recv()
                        out_grads_on()

                enter(block_in, after, 1 - slot)
                leave(block_out, before, 1 - slot)
                weigh(block, pair, slot)
                for group in ((0,), (1, 2))[at % 2]:
                    ring_m.stage(group, begun + couple * pairs + at // 2)
            return carry

        middle_back(0)
        enter(0, 0, 0)
        lax.fori_loop(0, blocks // 2, two_blocks, 0)
        leave(blocks - 1, pairs - 1, (blocks * pairs - 1) % 2)
        d_qkv[1] = dk_acc[...].astype(LOW)
        d_qkv[2] = dv_acc[...].astype(LOW)

        for t in range(3):
            full = dot(ht[...], d_qkv[t]).astype(LOW)
            at = rows_m + out_rows + t * width
            m.grads[pl.ds(at, width), pl.ds(0, width)] = full[:width]
            m.grads[pl.ds(at, width), pl.ds(width, width)] = full[width:]
        go_swap.wait_recv()
        own_rows = pl.ds(pl.multiple_of(rows_m + here.core * quarter, 16), quarter)
        own = m.grads[own_rows].astype(F32)
        m.grads[own_rows] = (own + m.go_got[...].astype(F32)).astype(LOW)
        used = out_rows + 3 * width
        if rows_q > used:
            m.grads[pl.ds(rows_m + used, rows_q - used)] = jnp.zeros((rows_q - used, WIDE), LOW)
        ring_q.swap_cores()
        ring_m.stages(done, done + 1)
        ring_q.begin()

        def input_rows(rows):
            terms = [nt_dot(d_qkv[t, rows], m.wq[t]) for t in range(3)]
            return terms[0] + terms[1] + terms[2]

        dh2_swap(0).wait_send()
        dh2_swap(1).wait_send()

        def input_got(chunk, carry):
            m.dh2_send[part(chunk)] = input_rows(other(chunk)).astype(LOW)
            dh1_swap(chunk).start()
            return carry

        lax.fori_loop(0, HALF // TILE, input_got, 0)
        ring_q.stages(1, 2)
        m.small_ref[2:3, :width] = column_sum(d_qkv[0].astype(F32))
        m.small_ref[2:3, width:] = column_sum(d_qkv[2].astype(F32))

        def input_own(chunk, carry):
            m.dh_own[part(chunk)] = input_rows(part(chunk))
            return carry

        lax.fori_loop(0, HALF // TILE, input_own, 0)

    pl.run_scoped(
        back_scope,
        pltpu.VMEM((3, row_len, width), LOW),
        pltpu.VMEM((row_len, width), F32),
        pltpu.VMEM((row_len, width), F32),
        pltpu.VMEM((width, row_len), LOW),
        pltpu.VMEM((WIDE, row_len), LOW),
        pltpu.VMEM((2, row_len, 2 * SPAN), F32),
        pltpu.VMEM((2, row_len, 2 * SPAN), F32),
        pltpu.VMEM((2, row_len, 2 * SPAN), LOW),
        pltpu.VMEM((2, row_len, 2 * SPAN), LOW),
    )

    def both(step, carry):
        for group in range(GROUPS):
            ring_m.stage(group, done + step)
            ring_q.stage(group, step + 1)
        return carry

    left = max(2 * chips - 1 - (done + 1), 0)
    lax.fori_loop(1, left + 1, both, 0)
    out_swap(0).wait_recv()
    out_swap(1).wait_recv()
    out_ref[...] = (m.out_sum[...] + m.out_got[...].astype(F32)).astype(LOW)
    passed = max(chips + 1, left + 2)
    ring_q.stages(left + 2, passed)

    def first_back(chunk, carry):
        rows = part(chunk)
        dh1_swap(chunk).wait_recv()
        d_h1 = m.dh_own[rows] + m.dh2_got[rows].astype(F32)
        centred, inverse = normal_parts(m.x_own[rows].astype(F32))
        unit = centred * inverse
        dx_ref[rows] = (m.middle[rows] + norm_back(d_h1, unit, inverse, as_row(gain1))).astype(LOW)
        m.small_ref[8:9] += column_sum(d_h1 * unit)
        m.small_ref[9:10] += column_sum(d_h1)
        return carry

    lax.fori_loop(0, HALF // TILE, first_back, 0)
    ring_m.arrive()
    writes = []

    def write_out(which, start, rows):
        if not direct:
            spot = pl.ds(start, rows)
            writes.append(local(which, m.result.at[spot], summed_ref.at[spot]))
            writes[-1].start()

    write_out(0, 0, rows_m)
    small.start(m.small_ref)
    at = passed
    for then in (small.core_done, small.mp_done):
        ring_q.stages(at, at + 1)
        then()
        at += 1
    for hop in range(1, 4):
        ring_q.stages(at, at + 1)
        small.hop(hop)
        at += 1
    ring_q.stages(at, 2 * chips - 1)
    small.finish(small_out, 4)
    ring_q.arrive()
    write_out(1, rows_m, rows_q)
    ring_m.drain()
    ring_q.drain()
    for chunk in range(2):
        for copy in (x_swap, cot_swap, h2_swap, out_swap, dh1_swap):
            copy(chunk).wait_send()
    for copy in (w_swap, w_share, w_pass, da_swap, go_swap):
        copy.wait_send()
    for write in writes:
        write.wait()


def whole_block(x, cot, wq, w_out, w_up, w_down, lengths, mask, gain1, bias1, b_qv, b_out, gain2, bias2, b_up, b_down):
    n_dp = lax.axis_size("dp")
    chips = n_dp // 2
    width = w_out.shape[0]
    hidden = w_up.shape[1]
    row_len = 2 * HALF
    rows_m = whole_blocks(2 * hidden, n_dp)
    rows_q = whole_blocks(4 * width, n_dp)
    rows = rows_m + rows_q
    any_spec = pl.BlockSpec(memory_space=pl.ANY)
    vmem = pl.BlockSpec(memory_space=pltpu.VMEM)
    dma = pltpu.SemaphoreType.DMA
    blocks, pairs = row_len // SPAN, width // 128

    def low(*shape):
        return pltpu.VMEM(shape, LOW)

    def full(*shape):
        return pltpu.VMEM(shape, F32)

    scratch = dict(
        x_own=low(HALF, WIDE),
        h1=low(row_len, WIDE),
        cot=low(row_len, WIDE),
        h2=low(row_len, WIDE),
        wq=low(3, WIDE, width),
        w_mine=low(width, WIDE),
        w_got=low(width, WIDE),
        q=low(row_len, width),
        k=low(row_len, width),
        v=low(row_len, width),
        att32=full(row_len, width),
        att_send=low(HALF, width),
        att_got=low(HALF, width),
        lse=full(blocks, pairs, 2 * SPAN),
        key_code=pltpu.VMEM((row_len, 1), jnp.int32),
        query_seg=pltpu.VMEM((blocks, 1, SPAN), jnp.int32),
        bias=full(row_len, SPAN),
        middle=full(HALF, WIDE),
        out_sum=full(HALF, WIDE),
        out_send=low(HALF, WIDE),
        out_got=low(HALF, WIDE),
        dh_own=full(HALF, WIDE),
        dh2_send=low(HALF, WIDE),
        dh2_got=low(HALF, WIDE),
        d_branch=low(HALF, WIDE),
        d_att=low(row_len, width),
        go_send=low(width, WIDE),
        go_core=low(width // 2, WIDE),
        go_got=low(width // 2, WIDE),
        small_ref=full(16, WIDE),
        grads=low(rows, WIDE),
        from_core=low(rows // 2, WIDE),
        result=low(16 if result_in_hbm(chips) else rows, WIDE),
        landed_m=low(chips - 1, rows_m // n_dp, WIDE),
        landed_q=low(chips - 1, rows_q // n_dp, WIDE),
        local_sems=dma((4,)),
        swap_sems=dma((2, 16)),
        pass_sems=dma((6,)),
        own_sems=dma((2, 2 * GROUPS)),
    )
    return pl.pallas_call(
        functools.partial(block_kernel, chips, (rows_m, rows_q)),
        out_shape=(
            jax.ShapeDtypeStruct((rows, WIDE), LOW),
            jax.ShapeDtypeStruct((HALF, WIDE), LOW),
            jax.ShapeDtypeStruct((HALF, WIDE), LOW),
            jax.ShapeDtypeStruct((16, WIDE), F32),
        ),
        in_specs=[any_spec] * 6 + [pl.BlockSpec(memory_space=pltpu.SMEM)] + [vmem] * 9,
        out_specs=(any_spec, vmem, vmem, vmem),
        scratch_shapes=[scratch[name] for name in SCRATCH]
        + segment_sems(chips) * 2
        + small_scratch(chips),
        compiler_params=pltpu.CompilerParams(
            collective_id=0, has_side_effects=True, vmem_limit_bytes=63 * 2**20
        ),
        cost_estimate=pl.CostEstimate(
            flops=int(40e9), bytes_accessed=int(40e6), transcendentals=0
        ),
        name="whole_block",
    )(x, cot, wq, w_out, w_up, w_down, lengths, mask, gain1, bias1, b_qv, b_out, gain2, bias2, b_up, b_down)


def unpack_kernel(base, pieces, sum_ref, small_ref, a_ref, b_ref, *refs):
    low_buf, full_buf, tokens, in_sems, out_sems, copy_sems = refs[-6:]
    up_ref, down_ref, out_ref, qkv_ref, a_out, b_out, up_sum, qv_ref = refs[:8]
    vectors = refs[8:-6]
    span = low_buf.shape[1]
    half = WIDE // 2
    firm = 2 * (WIDE * 2) // span
    starts = [at * span if at < firm else base + (at - firm) * span for at in range(pieces)]
    fetches = [
        pltpu.make_async_copy(sum_ref.at[pl.ds(start, span)], low_buf.at[at], in_sems.at[at])
        for at, start in enumerate(starts)
    ]
    for fetch in fetches:
        fetch.start()
    ins = [
        pltpu.make_async_copy(ref, tokens.at[at], copy_sems.at[0, at])
        for at, ref in enumerate((a_ref, b_ref))
    ]
    outs = [
        pltpu.make_async_copy(tokens.at[at], ref, copy_sems.at[1, at])
        for at, ref in enumerate((a_out, b_out))
    ]
    for copy in ins:
        copy.start()
    writes = []

    def write(at, lane, src, dst):
        writes.append(pltpu.make_async_copy(src, dst, out_sems.at[at, lane]))
        writes[-1].start()

    for at, fetch in enumerate(fetches):
        fetch.wait()
        held = full_buf.at[at]
        held[...] = low_buf[at].astype(F32)
        row = at * span
        if row < 2 * WIDE:
            rows, cols = pl.ds(row % WIDE, span), pl.ds(row // WIDE * WIDE, WIDE)
            write(at, 0, held, up_ref.at[rows, cols])
        elif row < 4 * WIDE:
            write(at, 0, held, down_ref.at[pl.ds(row - 2 * WIDE, span)])
        elif row < 4 * WIDE + half:
            write(at, 0, held, out_ref.at[pl.ds(row - 4 * WIDE, span)])
        else:
            row = row - 4 * WIDE - half
            for side in range(2):
                rows = pl.ds(side * half + row % half, span)
                write(at, side, held.at[:, pl.ds(side * half, half)], qkv_ref.at[row // half, rows])
    for come, go in zip(ins, outs):
        come.wait()
        go.start()
    up_sum[...] = jnp.concatenate([small_ref[0:1], small_ref[1:2]], axis=1).reshape(2 * WIDE)
    qv_ref[0:1] = small_ref[2:3, :half]
    qv_ref[1:2] = small_ref[2:3, half:]
    for at, vector in enumerate(vectors):
        vector[...] = small_ref[8 + at : 9 + at].reshape(WIDE)
    for copy in outs + writes:
        copy.wait()


def unpack(summed, small, block_out, d_block_in, base, hidden, width):
    pieces = 12
    span = WIDE // 2
    any_spec = pl.BlockSpec(memory_space=pl.ANY)
    vmem = pl.BlockSpec(memory_space=pltpu.VMEM)
    shapes = [(WIDE, hidden), (hidden, WIDE), (width, WIDE), (3, WIDE, width)]
    dma = pltpu.SemaphoreType.DMA
    return pl.pallas_call(
        functools.partial(unpack_kernel, base, pieces),
        out_shape=[jax.ShapeDtypeStruct(s, F32) for s in shapes]
        + [jax.ShapeDtypeStruct((HALF, WIDE), LOW)] * 2
        + [jax.ShapeDtypeStruct((hidden,), F32), jax.ShapeDtypeStruct((2, width), F32)]
        + [jax.ShapeDtypeStruct((WIDE,), F32)] * 6,
        in_specs=[any_spec, vmem, any_spec, any_spec],
        out_specs=[any_spec] * 6 + [vmem] * 8,
        scratch_shapes=[
            pltpu.VMEM((pieces, span, WIDE), LOW),
            pltpu.VMEM((pieces, span, WIDE), F32),
            pltpu.VMEM((2, HALF, WIDE), LOW),
            dma((pieces,)),
            dma((pieces, 2)),
            dma((2, 2)),
        ],
        compiler_params=pltpu.CompilerParams(vmem_limit_bytes=62 * 2**20),
        cost_estimate=pl.CostEstimate(flops=int(1e6), bytes_accessed=int(24e6), transcendentals=0),
        name="unpack",
    )(summed, small, block_out, d_block_in)


def local(
    block_in,
    cotangent,
    lengths,
    token_mask,
    ln1_gain,
    ln1_bias,
    w_qkv,
    b_qv,
    w_out,
    b_out,
    ln2_gain,
    ln2_bias,
    w_up,
    b_up,
    w_down,
    b_down,
):
    summed, block_out, d_block_in, small = whole_block(
        block_in,
        cotangent,
        w_qkv.transpose(1, 0, 2),
        w_out,
        w_up,
        w_down,
        lengths,
        token_mask,
        ln1_gain,
        ln1_bias,
        b_qv,
        b_out,
        ln2_gain,
        ln2_bias,
        b_up,
        b_down,
    )
    base = whole_blocks(2 * w_up.shape[1], lax.axis_size("dp"))
    (
        d_w_up,
        d_w_down,
        d_w_out,
        d_w_qkv,
        block_out,
        d_block_in,
        d_b_up,
        d_b_qv,
        d_ln1_gain,
        d_ln1_bias,
        d_b_out,
        d_ln2_gain,
        d_ln2_bias,
        d_b_down,
    ) = unpack(summed, small, block_out, d_block_in, base, w_up.shape[1], w_out.shape[0])
    return (
        block_out,
        d_block_in,
        d_ln1_gain,
        d_ln1_bias,
        d_w_qkv.transpose(1, 0, 2),
        d_b_qv,
        d_w_out,
        d_b_out,
        d_ln2_gain,
        d_ln2_bias,
        d_w_up,
        d_b_up,
        d_w_down,
        d_b_down,
    )


def solution(mesh):
    in_specs = (
        P(("dp", "mp"), None),
        P(("dp", "mp"), None),
        P("dp", None),
        P("dp", None),
        P(),
        P(),
        P(None, None, "mp"),
        P(None, "mp"),
        P("mp", None),
        P(),
        P(),
        P(),
        P(None, "mp"),
        P("mp"),
        P("mp", None),
        P(),
    )
    out_specs = (
        P(("dp", "mp"), None),
        P(("dp", "mp"), None),
        P(),
        P(),
        P(None, None, "mp"),
        P(None, "mp"),
        P("mp", None),
        P(),
        P(),
        P(),
        P(None, "mp"),
        P("mp"),
        P("mp", None),
        P(),
    )
    return jax.shard_map(local, mesh=mesh, in_specs=in_specs, out_specs=out_specs, check_vma=False)
```

```python
import functools
import jax
import jax.numpy as jnp
from jax import lax
from jax.experimental import pallas as pl
from jax.experimental.pallas import tpu as pltpu
from jax.sharding import PartitionSpec as P

HEAD_DIM = 64
MESH = pl.DeviceIdType.MESH
WIDE = 768
GROUPS = 3
LANES = 128


def ring_place(chip, chips):
    return jnp.where(chip % 2 == 0, chip // 2, chips - 1 - chip // 2)


def ring_chip(place, chips):
    return jnp.where(place < chips // 2, 2 * place, 2 * (chips - 1 - place) + 1)


def send_slots(chips):
    return min(chips, 8)


def whole_blocks(rows, n_dp):
    unit = 16 * n_dp
    return -(-rows // unit) * unit


class Here:
    def __init__(self, chips):
        dp, mp = lax.axis_index("dp"), lax.axis_index("mp")
        self.chips = chips
        self.core, chip = dp % 2, dp // 2
        self.place = ring_place(chip, chips)
        self.following = {"dp": ring_chip((self.place + 1) % chips, chips) * 2 + self.core}
        self.previous = {"dp": ring_chip((self.place + chips - 1) % chips, chips) * 2 + self.core}
        self.sibling = {"dp": chip * 2 + 1 - self.core}
        self.partner = {"mp": 1 - mp}
        self.side = chip % 2
        self.beside = {"dp": (chip + 1 - 2 * self.side) * 2 + self.core}


def remote(src, dst, send, recv, to):
    return pltpu.make_async_remote_copy(
        src_ref=src, dst_ref=dst, send_sem=send, recv_sem=recv, device_id=to, device_id_type=MESH
    )


class Segment:
    def __init__(self, here, base, rows, grads, from_core, landed, result, sems, own_sems=None):
        self.here, self.base, self.chips = here, base, here.chips
        self.block = rows // (2 * here.chips)
        self.slots = send_slots(here.chips)
        self.own_sems = own_sems
        self.grads, self.from_core, self.landed, self.result = grads, from_core, landed, result
        (
            self.core_send,
            self.core_recv,
            self.rs_send,
            self.rs_recv,
            self.ag_send,
            self.ag_recv,
            self.pair_send,
            self.pair_recv,
        ) = sems

    def rows_of(self, core, blk):
        start = self.base + (core * self.chips + blk) * self.block
        return pl.ds(pl.multiple_of(start, 16), self.block)

    def near_rows(self, blk):
        start = self.base // 2 + blk * self.block
        return pl.ds(pl.multiple_of(start, 16), self.block)

    def columns(self, ring):
        return pl.ds(ring * LANES, LANES)

    def rs_block(self, ring, step):
        if ring < GROUPS:
            return (self.here.place + 2 * self.chips - 1 - step) % self.chips
        return (self.here.place + 1 + step) % self.chips

    def ag_block(self, ring, step):
        if ring < GROUPS:
            return (self.here.place + self.chips - step) % self.chips
        return (self.here.place + step) % self.chips

    def toward(self, ring):
        return self.here.following if ring < GROUPS else self.here.previous

    def core_copy(self, half, step):
        blk = self.rs_block(half * GROUPS, step)
        cols = pl.ds(half * GROUPS * LANES, GROUPS * LANES)
        return remote(
            self.grads.at[self.rows_of(1 - self.here.core, blk), cols],
            self.from_core.at[self.near_rows(blk), cols],
            self.core_send.at[half, step],
            self.core_recv.at[half, step],
            self.here.sibling,
        )

    def rs_copy(self, ring, step):
        cols = self.columns(ring)
        return remote(
            self.grads.at[self.rows_of(self.here.core, self.rs_block(ring, step)), cols],
            self.landed.at[step, :, cols],
            self.rs_send.at[ring, step % self.slots],
            self.rs_recv.at[ring, step],
            self.toward(ring),
        )

    def result_copy(self, ring, step, send, recv, to, wide=1):
        rows = self.rows_of(self.here.core, self.ag_block(ring, step))
        cols = pl.ds(ring * LANES, wide * LANES)
        spot = self.result.at[rows, cols]
        own = self.own_sems is not None and isinstance(step, int) and step == 0
        held = self.grads.at[rows, cols] if own else spot
        lane = ring // wide
        return remote(held, spot, send.at[lane, step % self.slots], recv.at[lane, step], to)

    def own_copy(self, ring):
        spot = (self.rows_of(self.here.core, self.here.place), self.columns(ring))
        return pltpu.make_async_copy(
            self.grads.at[spot], self.result.at[spot], self.own_sems.at[ring]
        )

    def ag_copy(self, ring, step):
        return self.result_copy(ring, step, self.ag_send, self.ag_recv, self.toward(ring))

    def pair_copy(self, way, step):
        to = self.here.sibling
        return self.result_copy(way * GROUPS, step, self.pair_send, self.pair_recv, to, GROUPS)

    def pass_on(self, group, step):
        if group == GROUPS - 1:
            self.send(self.pair_copy, 0, step)
            self.send(self.pair_copy, 1, step)

    def summed(self, ring, step, first):
        blk = self.rs_block(ring, step)
        rows, cols = self.rows_of(self.here.core, blk), self.columns(ring)
        value = self.grads[rows, cols].astype(jnp.float32)
        value = value + self.from_core[self.near_rows(blk), cols].astype(jnp.float32)
        if not first:
            value = value + self.landed[step - 1, :, cols].astype(jnp.float32)
        return rows, cols, value.astype(jnp.bfloat16)

    def send(self, copy, ring, step):
        if self.slots < self.chips:

            @pl.when(step >= self.slots)
            def _():
                copy(ring, step - self.slots).wait_send()

        copy(ring, step).start()

    def swap_cores(self):
        def start(step, carry):
            self.core_copy(0, step).start()
            self.core_copy(1, step).start()
            return carry

        lax.fori_loop(0, self.chips, start, 0)

    def wait_core(self, step):
        self.core_copy(0, step).wait_recv()
        self.core_copy(1, step).wait_recv()

    def begin(self):
        self.wait_core(0)
        for group in range(GROUPS):
            for ring in (group, group + GROUPS):
                rows, cols, value = self.summed(ring, 0, True)
                self.grads[rows, cols] = value
                self.send(self.rs_copy, ring, 0)

    def stage(self, group, step):
        n = self.chips
        rings = (group, group + GROUPS)

        @pl.when(step <= n - 2)
        def _():
            if group == 0:
                self.wait_core(step)
            for ring in rings:
                self.rs_copy(ring, step - 1).wait_recv()
                rows, cols, value = self.summed(ring, step, False)
                self.grads[rows, cols] = value
                self.send(self.rs_copy, ring, step)

        @pl.when(step == n - 1)
        def _():
            if group == 0:
                self.wait_core(n - 1)
            for ring in rings:
                self.rs_copy(ring, n - 2).wait_recv()
                rows, cols, value = self.summed(ring, n - 1, False)
                if self.own_sems is None:
                    self.result[rows, cols] = value
                else:
                    self.grads[rows, cols] = value
                    self.own_copy(ring).start()
                self.send(self.ag_copy, ring, 0)
            self.pass_on(group, 0)

        @pl.when((step >= n) & (step <= 2 * n - 3))
        def _():
            for ring in rings:
                self.ag_copy(ring, step - n).wait_recv()
                self.send(self.ag_copy, ring, step - n + 1)
            self.pass_on(group, step - n + 1)

        @pl.when(step == 2 * n - 2)
        def _():
            for ring in rings:
                self.ag_copy(ring, n - 2).wait_recv()
            self.pass_on(group, n - 1)

    def stages(self, first, last):
        def run(step, carry):
            for group in range(GROUPS):
                self.stage(group, step)
            return carry

        lax.fori_loop(first, last, run, 0)

    def arrive(self):
        def run(step, carry):
            for way in range(2):
                self.pair_copy(way, step).wait_recv()
            return carry

        lax.fori_loop(0, self.chips, run, 0)
        if self.own_sems is not None:
            for ring in range(2 * GROUPS):
                self.own_copy(ring).wait()

    def drain(self):
        def cores(step, carry):
            self.core_copy(0, step).wait_send()
            self.core_copy(1, step).wait_send()
            return carry

        def pairs(step, carry):
            for way in range(2):
                self.pair_copy(way, step).wait_send()
            return carry

        def ring_steps(step, carry):
            for ring in range(2 * GROUPS):
                self.rs_copy(ring, step).wait_send()
                self.ag_copy(ring, step).wait_send()
            return carry

        n, slots = self.chips, self.slots
        lax.fori_loop(0, n, cores, 0)
        lax.fori_loop(n - slots, n, pairs, 0)
        lax.fori_loop(max(n - 1 - slots, 0), n - 1, ring_steps, 0)


def segment_sems(chips):
    dma = pltpu.SemaphoreType.DMA
    rings = 2 * GROUPS
    slots = send_slots(chips)
    both = [dma((rings, slots)), dma((rings, chips))]
    return [dma((2, chips))] * 2 + both * 2 + [dma((2, slots)), dma((2, chips))]


class Small:
    def __init__(self, here, from_core, from_mp, every, pair_sems, ring_sems):
        self.here, self.from_core, self.from_mp, self.every = here, from_core, from_mp, every
        self.pair_sems, self.ring_sems = pair_sems, ring_sems
        self.forward = here.chips // 2
        self.backward = here.chips - 1 - self.forward

    def pair(self, which, src, dst, to):
        return remote(src, dst, self.pair_sems.at[0, which], self.pair_sems.at[1, which], to)

    def start(self, src):
        self.src = src
        self.to_core = self.pair(0, src, self.from_core, self.here.sibling)
        self.to_core.start()

    def core_done(self):
        self.to_core.wait()
        place = self.here.place
        self.every[place] = self.src[...] + self.from_core[...]
        spot = self.every.at[place, pl.ds(8, 8)]
        self.to_mp = self.pair(1, spot, self.from_mp, self.here.partner)
        self.to_mp.start()

    def mp_done(self):
        self.to_mp.wait()
        place = self.here.place
        self.every[place, pl.ds(8, 8)] = self.every[place, pl.ds(8, 8)] + self.from_mp[...]
        self.step(0, 0).start()
        if self.backward:
            self.step(1, 0).start()

    def step(self, way, step):
        n = self.here.chips
        at = (self.here.place + n - step) % n if way == 0 else (self.here.place + step) % n
        spot = self.every.at[at]
        to = self.here.following if way == 0 else self.here.previous
        sems = self.ring_sems
        return remote(spot, spot, sems.at[0, way, step], sems.at[1, way, step], to)

    def hop(self, step):
        for way, count in ((0, self.forward), (1, self.backward)):

            @pl.when(step < count)
            def _():
                self.step(way, step - 1).wait_recv()
                self.step(way, step).start()

    def finish(self, out, hops):
        def run(step, carry):
            self.hop(step)
            return carry

        if hops < self.forward:
            lax.fori_loop(hops, self.forward, run, 0)
        self.step(0, self.forward - 1).wait_recv()
        if self.backward:
            self.step(1, self.backward - 1).wait_recv()
        out[...] = self.every[0]

        def add(chip, carry):
            out[...] += self.every[chip]
            return carry

        lax.fori_loop(1, self.here.chips, add, 0)

        def sent(way, count):
            def run(step, carry):
                self.step(way, step).wait_send()
                return carry

            lax.fori_loop(0, count, run, 0)

        sent(0, self.forward)
        sent(1, self.backward)


def small_scratch(chips):
    dma = pltpu.SemaphoreType.DMA
    return [
        pltpu.VMEM((16, WIDE), jnp.float32),
        pltpu.VMEM((8, WIDE), jnp.float32),
        pltpu.VMEM((chips, 16, WIDE), jnp.float32),
        dma((2, 2)),
        dma((2, 2, chips)),
    ]


LOW = jnp.bfloat16
F32 = jnp.float32
HALF = 512
TILE = 256
SPAN = 128
STRIP = 32
HIDDEN = 256
EPS = 1e-06
FAR = -1e30
SCALE = HEAD_DIM**-0.5
NT = (((1,), (1,)), ((), ()))
TN = (((0,), (0,)), ((), ()))


def nt_dot(a, b):
    return lax.dot_general(a, b, NT, preferred_element_type=F32)


def tn_dot(a, b):
    return lax.dot_general(a, b, TN, preferred_element_type=F32)


def dot(a, b):
    return jnp.dot(a, b, preferred_element_type=F32)


def normal_parts(values):
    centred = values - jnp.mean(values, axis=-1, keepdims=True)
    spread = jnp.mean(centred * centred, axis=-1, keepdims=True)
    return centred, lax.rsqrt(spread + EPS)


def norm_back(d_out, unit, inverse, gain):
    e = d_out * gain
    share = e - jnp.mean(e, -1, keepdims=True)
    return inverse * (share - unit * jnp.mean(e * unit, -1, keepdims=True))


def column_sum(values):
    return jnp.sum(values, axis=0, keepdims=True)


def split_heads(pair):
    low_lanes = lax.broadcasted_iota(jnp.int32, pair.shape, 1) < HEAD_DIM
    zero = jnp.zeros_like(pair)
    return jnp.concatenate([jnp.where(low_lanes, pair, zero), jnp.where(low_lanes, zero, pair)])


def own_blocks(both):
    return jnp.concatenate([both[:HEAD_DIM, :SPAN], both[HEAD_DIM:, SPAN:]], axis=0)


def twice(values):
    return jnp.concatenate([values, values], axis=1)


SCRATCH = (
    "x_own", "h1", "cot", "h2", "wq", "w_mine", "w_got", "q", "k", "v", "att32", "att_send",
    "att_got", "lse", "key_code", "query_seg", "bias", "middle", "out_sum", "out_send", "out_got",
    "dh_own", "dh2_send", "dh2_got", "d_branch", "d_att", "go_send", "go_core", "go_got",
    "small_ref", "grads", "from_core", "result", "landed_m", "landed_q", "local_sems", "swap_sems",
    "pass_sems", "own_sems",
)


def twice_rows(values):
    return jnp.concatenate([values[0:1], values[1:2]], axis=1)


def fold(values, op, rows=8):
    while values.shape[0] > rows:
        half = values.shape[0] // 2
        values = op(values[:half], values[half:])
    return values


def strips(rows):
    return [slice(at, at + STRIP) for at in range(0, rows, STRIP)]


def result_in_hbm(chips):
    return chips > 8


class Names:
    pass


def block_kernel(chips, sizes, *refs):
    (
        x_hbm,
        cot_hbm,
        wq_hbm,
        w_out_hbm,
        up_hbm,
        down_hbm,
        lengths,
        mask_ref,
        gain1,
        bias1,
        b_qv,
        b_out,
        gain2,
        bias2,
        b_up,
        b_down,
        summed_ref,
        out_ref,
        dx_ref,
        small_out,
    ) = refs[:20]
    m = Names()
    for name, ref in zip(SCRATCH, refs[20:]):
        setattr(m, name, ref)
    more = refs[20 + len(SCRATCH) :]
    sems_m, sems_q, small_refs = more[:8], more[8:16], more[16:]
    rows_m, rows_q = sizes
    here = Here(chips)
    direct = result_in_hbm(chips)
    result = summed_ref if direct else m.result
    ring_m = Segment(
        here, 0, rows_m, m.grads, m.from_core, m.landed_m, result, sems_m,
        m.own_sems.at[0] if direct else None,
    )
    ring_q = Segment(
        here, rows_m, rows_q, m.grads, m.from_core, m.landed_q, result, sems_q,
        m.own_sems.at[1] if direct else None,
    )
    small = Small(here, *small_refs)
    width = m.k.shape[1]
    pairs = width // 128
    row_len = 2 * HALF
    hidden = up_hbm.shape[1]
    blocks = row_len // SPAN

    def local(which, src, dst):
        return pltpu.make_async_copy(src, dst, m.local_sems.at[which])

    def swapped(which, src, dst):
        return remote(src, dst, m.swap_sems.at[0, which], m.swap_sems.at[1, which], here.partner)

    def part(chunk):
        return pl.ds(pl.multiple_of(chunk * TILE, TILE), TILE)

    def other(chunk):
        return pl.ds(pl.multiple_of(HALF + chunk * TILE, TILE), TILE)

    def x_swap(chunk):
        return swapped(chunk, x_hbm.at[part(chunk)], m.h1.at[other(chunk)])

    def cot_swap(chunk):
        return swapped(2 + chunk, cot_hbm.at[part(chunk)], m.cot.at[other(chunk)])

    def h2_swap(chunk):
        return swapped(4 + chunk, m.h2.at[part(chunk)], m.h2.at[other(chunk)])

    def dh2_swap(chunk):
        return swapped(6 + chunk, m.dh2_send.at[part(chunk)], m.dh2_got.at[part(chunk)])

    def out_swap(chunk):
        return swapped(8 + chunk, m.out_send.at[part(chunk)], m.out_got.at[part(chunk)])

    def dh1_swap(chunk):
        return swapped(10 + chunk, m.dh2_send.at[part(chunk)], m.dh2_got.at[part(chunk)])

    quarter = width // 2
    w_rows = pl.ds(pl.multiple_of(here.core * quarter, 16), quarter)
    piece = pl.ds(pl.multiple_of((here.core * 2 + here.side) * (quarter // 2), 16), quarter // 2)
    w_swap = swapped(12, w_out_hbm.at[piece], m.w_got.at[piece])
    w_share = remote(
        m.w_got.at[piece], m.w_got.at[piece], m.pass_sems.at[4], m.pass_sems.at[5], here.beside
    )
    w_pass = remote(
        m.w_got.at[w_rows], m.w_got.at[w_rows], m.pass_sems.at[0], m.pass_sems.at[1], here.sibling
    )
    att_swap = swapped(13, m.att_send, m.att_got)
    da_swap = swapped(14, m.att_send, m.d_att.at[pl.ds(HALF, HALF)])
    other_rows = pl.ds(pl.multiple_of((1 - here.core) * quarter, 16), quarter)
    go_pass = remote(
        m.go_send.at[other_rows], m.go_core, m.pass_sems.at[2], m.pass_sems.at[3], here.sibling
    )
    go_swap = swapped(15, m.go_core, m.go_got)

    def as_row(ref):
        return ref[...].reshape(1, ref.shape[0])

    load_x = local(0, x_hbm, m.x_own)
    load_wq = local(1, wq_hbm, m.wq)
    load_w = local(2, w_out_hbm, m.w_mine)
    load_cot = local(3, cot_hbm, m.cot.at[pl.ds(0, HALF)])
    for load in (load_x, load_wq, load_w, load_cot):
        load.start()
    barrier = pltpu.get_barrier_semaphore()
    near = (here.sibling, here.following, here.previous, here.partner, here.beside)
    for device in near:
        pl.semaphore_signal(barrier, inc=1, device_id=device, device_id_type=MESH)
    pl.semaphore_wait(barrier, len(near))
    x_swap(0).start()

    shift = lax.axis_index("mp") * HALF
    ends, total = [], lengths[0, 0]
    for slot in range(lengths.shape[1]):
        ends.append(total)
        if slot + 1 < lengths.shape[1]:
            total = total + lengths[0, slot + 1]

    def segment(shape, axis):
        at = (lax.broadcasted_iota(jnp.int32, shape, axis) + shift) % row_len
        found = jnp.zeros(shape, jnp.int32)
        for end in ends:
            found = found + (at >= end).astype(jnp.int32)
        return found

    seg_row = segment((1, row_len), 1)
    for block in range(blocks):
        m.query_seg[block] = seg_row[:, block * SPAN : (block + 1) * SPAN]
    mask = mask_ref[...]
    turned = jnp.concatenate([mask[:, HALF:], mask[:, :HALF]], axis=1)
    mask = jnp.where(shift == 0, mask, turned)
    code = jnp.where(mask == 1, seg_row, -1).astype(F32)
    m.key_code[...] = jnp.broadcast_to(code, (8, row_len)).T[:, :1].astype(jnp.int32)

    def project(values, rows):
        centred, inverse = normal_parts(values.astype(F32))
        h1 = (centred * inverse * as_row(gain1) + as_row(bias1)).astype(LOW)
        m.h1[rows] = h1
        m.q[rows] = ((dot(h1, m.wq[0]) + b_qv[0:1]) * SCALE).astype(LOW)
        m.k[rows] = dot(h1, m.wq[1]).astype(LOW)
        m.v[rows] = (dot(h1, m.wq[2]) + b_qv[1:2]).astype(LOW)

    load_x.wait()
    load_wq.wait()

    def project_own(chunk, carry):
        project(m.x_own[part(chunk)], part(chunk))
        return carry

    lax.fori_loop(0, HALF // TILE, project_own, 0)
    x_swap(1).start()

    def project_got(chunk, carry):
        x_swap(chunk).wait_recv()

        @pl.when(chunk == HALF // TILE - 1)
        def _():
            w_swap.start()
            cot_swap(0).start()

        project(m.h1[other(chunk)], other(chunk))
        return carry

    lax.fori_loop(0, HALF // TILE, project_got, 0)

    def set_bias(block):
        shape = (row_len, SPAN)
        key_at = lax.broadcasted_iota(jnp.int32, shape, 0)
        query_at = lax.broadcasted_iota(jnp.int32, shape, 1) + block * SPAN
        allowed = (m.key_code[...] == m.query_seg[block]) | (key_at == query_at)
        m.bias[...] = jnp.where(allowed, 0.0, FAR)

    def block_rows(block):
        return pl.ds(pl.multiple_of(block * SPAN, SPAN), SPAN)

    def attend_scope(vt, scores, raised):
        vt[...] = m.v[...].T

        def block_at(at):
            return (at + blocks // 2) % blocks

        def score(block, pair, slot):
            cols = slice(128 * pair, 128 * pair + 128)
            scores[slot] = nt_dot(m.k[:, cols], split_heads(m.q[block_rows(block), cols]))

        def weigh(slot):
            held, out = scores.at[slot], raised.at[slot]
            top = None
            for keys in strips(row_len):
                here = held[keys] + twice(m.bias[keys])
                top = here if top is None else jnp.maximum(top, here)
            top = jnp.max(fold(top, jnp.maximum), axis=0, keepdims=True)
            whole = None
            for keys in strips(row_len):
                here = jnp.exp(held[keys] + twice(m.bias[keys]) - top)
                out[keys] = here.astype(LOW)
                whole = here if whole is None else whole + here
            return top, jnp.sum(fold(whole, jnp.add), axis=0, keepdims=True)

        def gather(block, pair, slot, top, whole):
            cols = slice(128 * pair, 128 * pair + 128)
            outs = own_blocks(dot(vt[cols], raised[slot]) / whole)
            m.att32[block_rows(block), cols] = outs.T
            m.lse[block, pair : pair + 1] = top + jnp.log(whole)

        def attend(couple, carry):
            @pl.when(couple == blocks // 8)
            def _():
                w_swap.wait_recv()
                w_share.start()

            @pl.when(couple == blocks // 4)
            def _():
                m.att_send[...] = m.att32[pl.ds(HALF, HALF)].astype(LOW)
                att_swap.start()
                w_share.wait_recv()
                w_pass.start()

            held = None
            for at in range(2 * pairs):
                pair, slot = at % pairs, at % 2
                turn = couple * 2 + at // pairs
                block = block_at(turn)
                if pair == 0:
                    set_bias(block)
                if pair + 1 < pairs:
                    score(block, pair + 1, 1 - slot)
                else:
                    score(block_at(jnp.minimum(turn + 1, blocks - 1)), 0, 1 - slot)
                now = weigh(slot)
                if held is not None:
                    gather(*held)
                held = (block, pair, slot, *now)
            gather(*held)
            return carry

        score(block_at(0), 0, 0)
        lax.fori_loop(0, blocks // 2, attend, 0)

    pl.run_scoped(
        attend_scope,
        pltpu.VMEM((width, row_len), LOW),
        pltpu.VMEM((2, row_len, 2 * SPAN), F32),
        pltpu.VMEM((2, row_len, 2 * SPAN), LOW),
    )

    load_w.wait()
    w_pass.wait_recv()
    att_swap.wait_recv()
    cot_swap(1).start()

    def branch(chunk, carry):
        rows = part(chunk)
        got = dot(m.att32[rows].astype(LOW), m.w_mine[...]) + dot(m.att_got[rows], m.w_got[...])
        middle = m.x_own[rows].astype(F32) + got + as_row(b_out)
        m.middle[rows] = middle
        centred, inverse = normal_parts(middle)
        m.h2[rows] = (centred * inverse * as_row(gain2) + as_row(bias2)).astype(LOW)

        @pl.when(chunk == 0)
        def _():
            h2_swap(0).start()

        return carry

    lax.fori_loop(0, HALF // TILE, branch, 0)
    load_cot.wait()

    if rows_m > 2 * hidden:
        m.grads[pl.ds(2 * hidden, rows_m - 2 * hidden)] = jnp.zeros(
            (rows_m - 2 * hidden, WIDE), LOW
        )

    def mlp_scope(act_ref, pre_ref, up_sum):
        def chunks_scope(up, down, pre_buf, d_buf, up_row, ht):
            load_up, load_down = local(0, up_hbm, up), local(1, down_hbm, down)
            load_up.start()
            load_down.start()
            load_up.wait()
            load_down.wait()
            up_sum[...] = jnp.zeros_like(up_sum)
            up_row[...] = as_row(b_up)
            tiles = hidden // HIDDEN

            def through(begin, tokens):
                rows = pl.ds(begin, tokens)

                def enter(tile):
                    cols = slice(tile * HIDDEN, tile * HIDDEN + HIDDEN)
                    pre_buf[tile % 2, :tokens] = dot(m.h2[rows], up[:, cols])
                    d_buf[tile % 2, :tokens] = nt_dot(m.cot[rows], down[cols])

                def bend(tile):
                    cols = slice(tile * HIDDEN, tile * HIDDEN + HIDDEN)
                    shift_up = up_row[:, cols]
                    total = None
                    for at in range(0, tokens, STRIP):
                        pre = pre_buf[tile % 2, at : at + STRIP] + shift_up
                        cdf = 0.5 * (1.0 + lax.erf(pre * 0.7071067811865476))
                        slope = cdf + pre * (jnp.exp(-0.5 * pre * pre) * 0.3989422804014327)
                        d_pre = (d_buf[tile % 2, at : at + STRIP] * slope).astype(LOW)
                        spot = pl.ds(begin + at, STRIP)
                        act_ref[spot, cols] = (pre * cdf).astype(LOW)
                        pre_ref[spot, cols] = d_pre
                        d_pre = d_pre.astype(F32)
                        total = d_pre if total is None else total + d_pre
                    up_sum[:, cols] += column_sum(fold(total, jnp.add))

                enter(0)
                for tile in range(tiles):
                    if tile + 1 < tiles:
                        enter(tile + 1)
                    bend(tile)

            def grad_part(begin, count):
                span = WIDE // 2
                tokens = pl.ds(begin, count)
                ht[:, :count] = m.h2[tokens].T

                def put(rows, cols, value):
                    if begin:
                        value = value + m.grads[rows, cols].astype(F32)
                    m.grads[rows, cols] = value.astype(LOW)

                def grad_step(at, carry):
                    cols = pl.ds(pl.multiple_of(at * span, 128), span)
                    up_rows = pl.ds(pl.multiple_of(at // 2 * WIDE, WIDE), WIDE)
                    up_cols = pl.ds(pl.multiple_of(at % 2 * span, 128), span)
                    put(up_rows, up_cols, dot(ht[:, :count], pre_ref[tokens, cols]))
                    down_rows = pl.ds(pl.multiple_of(hidden + at * span, 128), span)
                    put(down_rows, slice(None), tn_dot(act_ref[tokens, cols], m.cot[tokens]))
                    return carry

                lax.fori_loop(0, hidden // span, grad_step, 0)

            def products_out(begin, tokens):
                rows = pl.ds(begin, tokens)
                return dot(act_ref[rows], down[...]), nt_dot(pre_ref[rows], up[...])

            through(0, HALF)
            h2_swap(1).start()
            for chunk in range(2):
                rows = pl.ds(chunk * TILE, TILE)
                out, m.dh_own[rows] = products_out(chunk * TILE, TILE)
                m.out_sum[rows] = out + m.middle[rows] + as_row(b_down)
            for chunk in range(2):
                begin = HALF + chunk * TILE
                if chunk == 0:
                    grad_part(0, HALF)
                    h2_swap(0).wait_recv()
                    cot_swap(0).wait_recv()
                else:
                    grad_part(HALF, TILE)
                    h2_swap(1).wait_recv()
                    cot_swap(1).wait_recv()
                    dh2_swap(0).start()
                through(begin, TILE)
                if chunk == 1:
                    grad_part(begin, TILE)
                    ring_m.swap_cores()
                    ring_m.begin()
                out, d_h = products_out(begin, TILE)
                sent = pl.ds(chunk * TILE, TILE)
                m.dh2_send[sent] = d_h.astype(LOW)
                m.out_send[sent] = out.astype(LOW)
            dh2_swap(1).start()

        pl.run_scoped(
            chunks_scope,
            pltpu.VMEM((WIDE, hidden), LOW),
            pltpu.VMEM((hidden, WIDE), LOW),
            pltpu.VMEM((2, HALF, HIDDEN), F32),
            pltpu.VMEM((2, HALF, HIDDEN), F32),
            pltpu.VMEM((1, hidden), F32),
            pltpu.VMEM((WIDE, HALF), LOW),
        )
        m.small_ref[...] = jnp.zeros_like(m.small_ref)
        m.small_ref[0:1] = up_sum[:, :WIDE]
        m.small_ref[1:2] = up_sum[:, WIDE:]

    pl.run_scoped(
        mlp_scope,
        pltpu.VMEM((row_len, hidden), LOW),
        pltpu.VMEM((row_len, hidden), LOW),
        pltpu.VMEM((1, hidden), F32),
    )
    begun = 1
    done = begun + blocks + 2
    out_rows = width
    att_swap.wait_send()

    def back_scope(d_qkv, dk_acc, dv_acc, kt, ht, scores, d_probs, probs, d_scores):
        kt[...] = m.k[...].T
        dk_acc[...] = jnp.zeros_like(dk_acc)
        dv_acc[...] = jnp.zeros_like(dv_acc)
        heads_of = jnp.where(
            lax.broadcasted_iota(jnp.int32, (8, 128), 1) // HEAD_DIM
            == lax.broadcasted_iota(jnp.int32, (8, 128), 0),
            1.0,
            0.0,
        ).astype(LOW)

        ht[...] = m.h1[...].T
        probs[...] = jnp.zeros_like(probs)
        d_scores[...] = jnp.zeros_like(d_scores)

        def middle_back(chunk):
            dh2_swap(chunk).wait_recv()

            def some_rows(at, carry):
                rows = pl.ds(pl.multiple_of(chunk * TILE + at * SPAN, SPAN), SPAN)
                d_h2 = m.dh_own[rows] + m.dh2_got[rows].astype(F32)
                cot = m.cot[rows].astype(F32)
                centred, inverse = normal_parts(m.middle[rows])
                unit = centred * inverse
                d_middle = cot + norm_back(d_h2, unit, inverse, as_row(gain2))
                m.middle[rows] = d_middle
                d_branch = d_middle.astype(LOW)
                m.d_branch[rows] = d_branch
                m.att_send[rows] = nt_dot(d_branch, m.w_got[...]).astype(LOW)
                m.d_att[rows] = nt_dot(d_branch, m.w_mine[...]).astype(LOW)
                for at, term in enumerate((d_middle, d_h2 * unit, d_h2, cot)):
                    m.small_ref[10 + at : 11 + at] += column_sum(term)
                return carry

            lax.fori_loop(0, TILE // SPAN, some_rows, 0)

        def out_grads():
            def send_rows(pair, carry):
                cols = pl.ds(pl.multiple_of(pair * 128, 128), 128)
                m.go_send[cols] = tn_dot(m.att_got[:, cols], m.d_branch[...]).astype(LOW)
                return carry

            def own_rows(pair, carry):
                cols = pl.ds(pl.multiple_of(pair * 128, 128), 128)
                rows = pl.ds(pl.multiple_of(rows_m + pair * 128, 128), 128)
                held = m.att32[pl.ds(0, HALF), cols].astype(LOW)
                m.grads[rows] = tn_dot(held, m.d_branch[...]).astype(LOW)
                return carry

            lax.fori_loop(0, pairs, send_rows, 0)
            go_pass.start()
            lax.fori_loop(0, pairs, own_rows, 0)

        def out_grads_on():
            go_pass.wait()
            go = m.go_send[w_rows].astype(F32) + m.go_core[...].astype(F32)
            m.go_core[...] = go.astype(LOW)
            go_swap.start()
            out_swap(0).start()
            out_swap(1).start()

        def enter(block, pair, slot):
            rows, cols = block_rows(block), slice(128 * pair, 128 * pair + 128)
            scores[slot] = nt_dot(m.k[:, cols], split_heads(m.q[rows, cols]))
            d_probs[slot] = nt_dot(m.v[:, cols], split_heads(m.d_att[rows, cols]))

        def weigh(block, pair, slot):
            rows, cols = block_rows(block), slice(128 * pair, 128 * pair + 128)
            weighed = m.d_att[rows, cols].astype(F32) * m.att32[rows, cols]
            high = weighed.astype(LOW)
            rest = (weighed - high.astype(F32)).astype(LOW)
            inner = nt_dot(heads_of, high) + nt_dot(heads_of, rest)
            inner = twice_rows(inner)
            lse = m.lse[block, pair : pair + 1]
            for keys in strips(row_len):
                prob = jnp.exp(scores[slot, keys] + twice(m.bias[keys]) - lse)
                probs[slot, keys] = prob.astype(LOW)
                d_scores[slot, keys] = (prob * (d_probs[slot, keys] - inner)).astype(LOW)

        def leave(block, pair, slot):
            rows, cols = block_rows(block), slice(128 * pair, 128 * pair + 128)
            dk_acc[:, cols] += dot(d_scores[slot], split_heads(m.q[rows, cols]))
            dv_acc[:, cols] += dot(probs[slot], split_heads(m.d_att[rows, cols]))
            d_query = own_blocks(dot(kt[cols], d_scores[slot])).T.astype(LOW)
            d_qkv[0, rows, cols] = d_query * jnp.asarray(SCALE, LOW)

        def two_blocks(couple, carry):
            for at in range(2 * pairs):
                block, pair, slot = couple * 2 + at // pairs, at % pairs, at % 2
                before, after = (pair + pairs - 1) % pairs, (pair + 1) % pairs
                block_in = block if pair + 1 < pairs else jnp.minimum(block + 1, blocks - 1)
                block_out = block if pair > 0 else jnp.maximum(block - 1, 0)
                if pair == 0:
                    set_bias(block)
                if at == 2 * pairs - 1:

                    @pl.when(couple == blocks // 8 - 1)
                    def _():
                        middle_back(1)
                        da_swap.start()
                        out_grads()

                    @pl.when(couple == blocks // 4 - 1)
                    def _():
                        da_swap.wait_recv()
                        out_grads_on()

                enter(block_in, after, 1 - slot)
                leave(block_out, before, 1 - slot)
                weigh(block, pair, slot)
                ring_m.stage(pair, begun + block + 2 * jnp.minimum(couple, 1))
                if at == 2 * pairs - 1:

                    @pl.when(couple == 0)
                    def _():
                        ring_m.stages(begun + 2, begun + 4)

            return carry

        middle_back(0)
        enter(0, 0, 0)
        lax.fori_loop(0, blocks // 2, two_blocks, 0)
        leave(blocks - 1, pairs - 1, (blocks * pairs - 1) % 2)
        d_qkv[1] = dk_acc[...].astype(LOW)
        d_qkv[2] = dv_acc[...].astype(LOW)

        for t in range(3):
            full = dot(ht[...], d_qkv[t]).astype(LOW)
            at = rows_m + out_rows + t * width
            m.grads[pl.ds(at, width), pl.ds(0, width)] = full[:width]
            m.grads[pl.ds(at, width), pl.ds(width, width)] = full[width:]
        go_swap.wait_recv()
        own_rows = pl.ds(pl.multiple_of(rows_m + here.core * quarter, 16), quarter)
        own = m.grads[own_rows].astype(F32)
        m.grads[own_rows] = (own + m.go_got[...].astype(F32)).astype(LOW)
        used = out_rows + 3 * width
        if rows_q > used:
            m.grads[pl.ds(rows_m + used, rows_q - used)] = jnp.zeros((rows_q - used, WIDE), LOW)
        ring_q.swap_cores()
        ring_m.stages(done, done + 1)
        ring_q.begin()

        def input_rows(rows):
            terms = [nt_dot(d_qkv[t, rows], m.wq[t]) for t in range(3)]
            return terms[0] + terms[1] + terms[2]

        dh2_swap(0).wait_send()
        dh2_swap(1).wait_send()

        def input_got(chunk, carry):
            m.dh2_send[part(chunk)] = input_rows(other(chunk)).astype(LOW)
            dh1_swap(chunk).start()
            return carry

        lax.fori_loop(0, HALF // TILE, input_got, 0)
        ring_q.stages(1, 2)
        m.small_ref[2:3, :width] = column_sum(d_qkv[0].astype(F32))
        m.small_ref[2:3, width:] = column_sum(d_qkv[2].astype(F32))

        def input_own(chunk, carry):
            m.dh_own[part(chunk)] = input_rows(part(chunk))
            return carry

        lax.fori_loop(0, HALF // TILE, input_own, 0)

    pl.run_scoped(
        back_scope,
        pltpu.VMEM((3, row_len, width), LOW),
        pltpu.VMEM((row_len, width), F32),
        pltpu.VMEM((row_len, width), F32),
        pltpu.VMEM((width, row_len), LOW),
        pltpu.VMEM((WIDE, row_len), LOW),
        pltpu.VMEM((2, row_len, 2 * SPAN), F32),
        pltpu.VMEM((2, row_len, 2 * SPAN), F32),
        pltpu.VMEM((2, row_len, 2 * SPAN), LOW),
        pltpu.VMEM((2, row_len, 2 * SPAN), LOW),
    )

    def both(step, carry):
        for group in range(GROUPS):
            ring_m.stage(group, done + step)
            ring_q.stage(group, step + 1)
        return carry

    left = max(2 * chips - 1 - (done + 1), 0)
    lax.fori_loop(1, left + 1, both, 0)
    out_swap(0).wait_recv()
    out_swap(1).wait_recv()
    out_ref[...] = (m.out_sum[...] + m.out_got[...].astype(F32)).astype(LOW)
    passed = max(chips + 1, left + 2)
    ring_q.stages(left + 2, passed)

    def first_back(chunk, carry):
        rows = part(chunk)
        dh1_swap(chunk).wait_recv()
        d_h1 = m.dh_own[rows] + m.dh2_got[rows].astype(F32)
        centred, inverse = normal_parts(m.x_own[rows].astype(F32))
        unit = centred * inverse
        dx_ref[rows] = (m.middle[rows] + norm_back(d_h1, unit, inverse, as_row(gain1))).astype(LOW)
        m.small_ref[8:9] += column_sum(d_h1 * unit)
        m.small_ref[9:10] += column_sum(d_h1)
        return carry

    lax.fori_loop(0, HALF // TILE, first_back, 0)
    ring_m.arrive()
    writes = []

    def write_out(which, start, rows):
        if not direct:
            spot = pl.ds(start, rows)
            writes.append(local(which, m.result.at[spot], summed_ref.at[spot]))
            writes[-1].start()

    write_out(0, 0, rows_m)
    small.start(m.small_ref)
    at = passed
    for then in (small.core_done, small.mp_done):
        ring_q.stages(at, at + 1)
        then()
        at += 1
    for hop in range(1, 4):
        ring_q.stages(at, at + 1)
        small.hop(hop)
        at += 1
    ring_q.stages(at, 2 * chips - 1)
    small.finish(small_out, 4)
    ring_q.arrive()
    write_out(1, rows_m, rows_q)
    ring_m.drain()
    ring_q.drain()
    for chunk in range(2):
        for copy in (x_swap, cot_swap, h2_swap, out_swap, dh1_swap):
            copy(chunk).wait_send()
    for copy in (w_swap, w_share, w_pass, da_swap, go_swap):
        copy.wait_send()
    for write in writes:
        write.wait()


def whole_block(x, cot, wq, w_out, w_up, w_down, lengths, mask, gain1, bias1, b_qv, b_out, gain2, bias2, b_up, b_down):
    n_dp = lax.axis_size("dp")
    chips = n_dp // 2
    width = w_out.shape[0]
    hidden = w_up.shape[1]
    row_len = 2 * HALF
    rows_m = whole_blocks(2 * hidden, n_dp)
    rows_q = whole_blocks(4 * width, n_dp)
    rows = rows_m + rows_q
    any_spec = pl.BlockSpec(memory_space=pl.ANY)
    vmem = pl.BlockSpec(memory_space=pltpu.VMEM)
    dma = pltpu.SemaphoreType.DMA
    blocks, pairs = row_len // SPAN, width // 128

    def low(*shape):
        return pltpu.VMEM(shape, LOW)

    def full(*shape):
        return pltpu.VMEM(shape, F32)

    scratch = dict(
        x_own=low(HALF, WIDE),
        h1=low(row_len, WIDE),
        cot=low(row_len, WIDE),
        h2=low(row_len, WIDE),
        wq=low(3, WIDE, width),
        w_mine=low(width, WIDE),
        w_got=low(width, WIDE),
        q=low(row_len, width),
        k=low(row_len, width),
        v=low(row_len, width),
        att32=full(row_len, width),
        att_send=low(HALF, width),
        att_got=low(HALF, width),
        lse=full(blocks, pairs, 2 * SPAN),
        key_code=pltpu.VMEM((row_len, 1), jnp.int32),
        query_seg=pltpu.VMEM((blocks, 1, SPAN), jnp.int32),
        bias=full(row_len, SPAN),
        middle=full(HALF, WIDE),
        out_sum=full(HALF, WIDE),
        out_send=low(HALF, WIDE),
        out_got=low(HALF, WIDE),
        dh_own=full(HALF, WIDE),
        dh2_send=low(HALF, WIDE),
        dh2_got=low(HALF, WIDE),
        d_branch=low(HALF, WIDE),
        d_att=low(row_len, width),
        go_send=low(width, WIDE),
        go_core=low(width // 2, WIDE),
        go_got=low(width // 2, WIDE),
        small_ref=full(16, WIDE),
        grads=low(rows, WIDE),
        from_core=low(rows // 2, WIDE),
        result=low(16 if result_in_hbm(chips) else rows, WIDE),
        landed_m=low(chips - 1, rows_m // n_dp, WIDE),
        landed_q=low(chips - 1, rows_q // n_dp, WIDE),
        local_sems=dma((4,)),
        swap_sems=dma((2, 16)),
        pass_sems=dma((6,)),
        own_sems=dma((2, 2 * GROUPS)),
    )
    return pl.pallas_call(
        functools.partial(block_kernel, chips, (rows_m, rows_q)),
        out_shape=(
            jax.ShapeDtypeStruct((rows, WIDE), LOW),
            jax.ShapeDtypeStruct((HALF, WIDE), LOW),
            jax.ShapeDtypeStruct((HALF, WIDE), LOW),
            jax.ShapeDtypeStruct((16, WIDE), F32),
        ),
        in_specs=[any_spec] * 6 + [pl.BlockSpec(memory_space=pltpu.SMEM)] + [vmem] * 9,
        out_specs=(any_spec, vmem, vmem, vmem),
        scratch_shapes=[scratch[name] for name in SCRATCH]
        + segment_sems(chips) * 2
        + small_scratch(chips),
        compiler_params=pltpu.CompilerParams(
            collective_id=0, has_side_effects=True, vmem_limit_bytes=63 * 2**20
        ),
        cost_estimate=pl.CostEstimate(
            flops=int(40e9), bytes_accessed=int(40e6), transcendentals=0
        ),
        name="whole_block",
    )(x, cot, wq, w_out, w_up, w_down, lengths, mask, gain1, bias1, b_qv, b_out, gain2, bias2, b_up, b_down)


def unpack_kernel(base, pieces, sum_ref, small_ref, a_ref, b_ref, *refs):
    low_buf, full_buf, tokens, in_sems, out_sems, copy_sems = refs[-6:]
    up_ref, down_ref, out_ref, qkv_ref, a_out, b_out, up_sum, qv_ref = refs[:8]
    vectors = refs[8:-6]
    span = low_buf.shape[1]
    half = WIDE // 2
    firm = 2 * (WIDE * 2) // span
    starts = [at * span if at < firm else base + (at - firm) * span for at in range(pieces)]
    fetches = [
        pltpu.make_async_copy(sum_ref.at[pl.ds(start, span)], low_buf.at[at], in_sems.at[at])
        for at, start in enumerate(starts)
    ]
    for fetch in fetches:
        fetch.start()
    ins = [
        pltpu.make_async_copy(ref, tokens.at[at], copy_sems.at[0, at])
        for at, ref in enumerate((a_ref, b_ref))
    ]
    outs = [
        pltpu.make_async_copy(tokens.at[at], ref, copy_sems.at[1, at])
        for at, ref in enumerate((a_out, b_out))
    ]
    for copy in ins:
        copy.start()
    writes = []

    def write(at, lane, src, dst):
        writes.append(pltpu.make_async_copy(src, dst, out_sems.at[at, lane]))
        writes[-1].start()

    for at, fetch in enumerate(fetches):
        fetch.wait()
        held = full_buf.at[at]
        held[...] = low_buf[at].astype(F32)
        row = at * span
        if row < 2 * WIDE:
            rows, cols = pl.ds(row % WIDE, span), pl.ds(row // WIDE * WIDE, WIDE)
            write(at, 0, held, up_ref.at[rows, cols])
        elif row < 4 * WIDE:
            write(at, 0, held, down_ref.at[pl.ds(row - 2 * WIDE, span)])
        elif row < 4 * WIDE + half:
            write(at, 0, held, out_ref.at[pl.ds(row - 4 * WIDE, span)])
        else:
            row = row - 4 * WIDE - half
            for side in range(2):
                rows = pl.ds(side * half + row % half, span)
                write(at, side, held.at[:, pl.ds(side * half, half)], qkv_ref.at[row // half, rows])
    for come, go in zip(ins, outs):
        come.wait()
        go.start()
    up_sum[...] = jnp.concatenate([small_ref[0:1], small_ref[1:2]], axis=1).reshape(2 * WIDE)
    qv_ref[0:1] = small_ref[2:3, :half]
    qv_ref[1:2] = small_ref[2:3, half:]
    for at, vector in enumerate(vectors):
        vector[...] = small_ref[8 + at : 9 + at].reshape(WIDE)
    for copy in outs + writes:
        copy.wait()


def unpack(summed, small, block_out, d_block_in, base, hidden, width):
    pieces = 12
    span = WIDE // 2
    any_spec = pl.BlockSpec(memory_space=pl.ANY)
    vmem = pl.BlockSpec(memory_space=pltpu.VMEM)
    shapes = [(WIDE, hidden), (hidden, WIDE), (width, WIDE), (3, WIDE, width)]
    dma = pltpu.SemaphoreType.DMA
    return pl.pallas_call(
        functools.partial(unpack_kernel, base, pieces),
        out_shape=[jax.ShapeDtypeStruct(s, F32) for s in shapes]
        + [jax.ShapeDtypeStruct((HALF, WIDE), LOW)] * 2
        + [jax.ShapeDtypeStruct((hidden,), F32), jax.ShapeDtypeStruct((2, width), F32)]
        + [jax.ShapeDtypeStruct((WIDE,), F32)] * 6,
        in_specs=[any_spec, vmem, any_spec, any_spec],
        out_specs=[any_spec] * 6 + [vmem] * 8,
        scratch_shapes=[
            pltpu.VMEM((pieces, span, WIDE), LOW),
            pltpu.VMEM((pieces, span, WIDE), F32),
            pltpu.VMEM((2, HALF, WIDE), LOW),
            dma((pieces,)),
            dma((pieces, 2)),
            dma((2, 2)),
        ],
        compiler_params=pltpu.CompilerParams(vmem_limit_bytes=62 * 2**20),
        cost_estimate=pl.CostEstimate(flops=int(1e6), bytes_accessed=int(24e6), transcendentals=0),
        name="unpack",
    )(summed, small, block_out, d_block_in)


def local(
    block_in,
    cotangent,
    lengths,
    token_mask,
    ln1_gain,
    ln1_bias,
    w_qkv,
    b_qv,
    w_out,
    b_out,
    ln2_gain,
    ln2_bias,
    w_up,
    b_up,
    w_down,
    b_down,
):
    summed, block_out, d_block_in, small = whole_block(
        block_in,
        cotangent,
        w_qkv.transpose(1, 0, 2),
        w_out,
        w_up,
        w_down,
        lengths,
        token_mask,
        ln1_gain,
        ln1_bias,
        b_qv,
        b_out,
        ln2_gain,
        ln2_bias,
        b_up,
        b_down,
    )
    base = whole_blocks(2 * w_up.shape[1], lax.axis_size("dp"))
    (
        d_w_up,
        d_w_down,
        d_w_out,
        d_w_qkv,
        block_out,
        d_block_in,
        d_b_up,
        d_b_qv,
        d_ln1_gain,
        d_ln1_bias,
        d_b_out,
        d_ln2_gain,
        d_ln2_bias,
        d_b_down,
    ) = unpack(summed, small, block_out, d_block_in, base, w_up.shape[1], w_out.shape[0])
    return (
        block_out,
        d_block_in,
        d_ln1_gain,
        d_ln1_bias,
        d_w_qkv.transpose(1, 0, 2),
        d_b_qv,
        d_w_out,
        d_b_out,
        d_ln2_gain,
        d_ln2_bias,
        d_w_up,
        d_b_up,
        d_w_down,
        d_b_down,
    )


def solution(mesh):
    in_specs = (
        P(("dp", "mp"), None),
        P(("dp", "mp"), None),
        P("dp", None),
        P("dp", None),
        P(),
        P(),
        P(None, None, "mp"),
        P(None, "mp"),
        P("mp", None),
        P(),
        P(),
        P(),
        P(None, "mp"),
        P("mp"),
        P("mp", None),
        P(),
    )
    out_specs = (
        P(("dp", "mp"), None),
        P(("dp", "mp"), None),
        P(),
        P(),
        P(None, None, "mp"),
        P(None, "mp"),
        P("mp", None),
        P(),
        P(),
        P(),
        P(None, "mp"),
        P("mp"),
        P("mp", None),
        P(),
    )
    return jax.shard_map(local, mesh=mesh, in_specs=in_specs, out_specs=out_specs, check_vma=False)
```

```python
import functools
import jax
import jax.numpy as jnp
from jax import lax
from jax.experimental import pallas as pl
from jax.experimental.pallas import tpu as pltpu
from jax.sharding import PartitionSpec as P

HEAD_DIM = 64
MESH = pl.DeviceIdType.MESH
WIDE = 768
GROUPS = 3
LANES = 128


def ring_place(chip, chips):
    return jnp.where(chip % 2 == 0, chip // 2, chips - 1 - chip // 2)


def ring_chip(place, chips):
    return jnp.where(place < chips // 2, 2 * place, 2 * (chips - 1 - place) + 1)


def send_slots(chips):
    return min(chips, 8)


def whole_blocks(rows, n_dp):
    unit = 16 * n_dp
    return -(-rows // unit) * unit


class Here:
    def __init__(self, chips):
        dp, mp = lax.axis_index("dp"), lax.axis_index("mp")
        self.chips = chips
        self.core, chip = dp % 2, dp // 2
        self.place = ring_place(chip, chips)
        self.following = {"dp": ring_chip((self.place + 1) % chips, chips) * 2 + self.core}
        self.previous = {"dp": ring_chip((self.place + chips - 1) % chips, chips) * 2 + self.core}
        self.sibling = {"dp": chip * 2 + 1 - self.core}
        self.partner = {"mp": 1 - mp}
        self.side = chip % 2
        self.beside = {"dp": (chip + 1 - 2 * self.side) * 2 + self.core}


def remote(src, dst, send, recv, to):
    return pltpu.make_async_remote_copy(
        src_ref=src, dst_ref=dst, send_sem=send, recv_sem=recv, device_id=to, device_id_type=MESH
    )


class Segment:
    def __init__(self, here, base, rows, grads, from_core, landed, result, sems, own_sems=None):
        self.here, self.base, self.chips = here, base, here.chips
        self.block = rows // (2 * here.chips)
        self.slots = send_slots(here.chips)
        self.own_sems = own_sems
        self.grads, self.from_core, self.landed, self.result = grads, from_core, landed, result
        (
            self.core_send,
            self.core_recv,
            self.rs_send,
            self.rs_recv,
            self.ag_send,
            self.ag_recv,
            self.pair_send,
            self.pair_recv,
        ) = sems

    def rows_of(self, core, blk):
        start = self.base + (core * self.chips + blk) * self.block
        return pl.ds(pl.multiple_of(start, 16), self.block)

    def near_rows(self, blk):
        start = self.base // 2 + blk * self.block
        return pl.ds(pl.multiple_of(start, 16), self.block)

    def columns(self, ring):
        return pl.ds(ring * LANES, LANES)

    def rs_block(self, ring, step):
        if ring < GROUPS:
            return (self.here.place + 2 * self.chips - 1 - step) % self.chips
        return (self.here.place + 1 + step) % self.chips

    def ag_block(self, ring, step):
        if ring < GROUPS:
            return (self.here.place + self.chips - step) % self.chips
        return (self.here.place + step) % self.chips

    def toward(self, ring):
        return self.here.following if ring < GROUPS else self.here.previous

    def core_copy(self, half, step):
        blk = self.rs_block(half * GROUPS, step)
        cols = pl.ds(half * GROUPS * LANES, GROUPS * LANES)
        return remote(
            self.grads.at[self.rows_of(1 - self.here.core, blk), cols],
            self.from_core.at[self.near_rows(blk), cols],
            self.core_send.at[half, step],
            self.core_recv.at[half, step],
            self.here.sibling,
        )

    def rs_copy(self, ring, step):
        cols = self.columns(ring)
        return remote(
            self.grads.at[self.rows_of(self.here.core, self.rs_block(ring, step)), cols],
            self.landed.at[step, :, cols],
            self.rs_send.at[ring, step % self.slots],
            self.rs_recv.at[ring, step],
            self.toward(ring),
        )

    def result_copy(self, ring, step, send, recv, to, wide=1):
        rows = self.rows_of(self.here.core, self.ag_block(ring, step))
        cols = pl.ds(ring * LANES, wide * LANES)
        spot = self.result.at[rows, cols]
        own = self.own_sems is not None and isinstance(step, int) and step == 0
        held = self.grads.at[rows, cols] if own else spot
        lane = ring // wide
        return remote(held, spot, send.at[lane, step % self.slots], recv.at[lane, step], to)

    def own_copy(self, ring):
        spot = (self.rows_of(self.here.core, self.here.place), self.columns(ring))
        return pltpu.make_async_copy(
            self.grads.at[spot], self.result.at[spot], self.own_sems.at[ring]
        )

    def ag_copy(self, ring, step):
        return self.result_copy(ring, step, self.ag_send, self.ag_recv, self.toward(ring))

    def pair_copy(self, way, step):
        to = self.here.sibling
        return self.result_copy(way * GROUPS, step, self.pair_send, self.pair_recv, to, GROUPS)

    def pass_on(self, group, step):
        if group == GROUPS - 1:
            self.send(self.pair_copy, 0, step)
            self.send(self.pair_copy, 1, step)

    def summed(self, ring, step, first):
        blk = self.rs_block(ring, step)
        rows, cols = self.rows_of(self.here.core, blk), self.columns(ring)
        value = self.grads[rows, cols].astype(jnp.float32)
        value = value + self.from_core[self.near_rows(blk), cols].astype(jnp.float32)
        if not first:
            value = value + self.landed[step - 1, :, cols].astype(jnp.float32)
        return rows, cols, value.astype(jnp.bfloat16)

    def send(self, copy, ring, step):
        if self.slots < self.chips:

            @pl.when(step >= self.slots)
            def _():
                copy(ring, step - self.slots).wait_send()

        copy(ring, step).start()

    def swap_cores(self):
        def start(step, carry):
            self.core_copy(0, step).start()
            self.core_copy(1, step).start()
            return carry

        lax.fori_loop(0, self.chips, start, 0)

    def wait_core(self, step):
        self.core_copy(0, step).wait_recv()
        self.core_copy(1, step).wait_recv()

    def begin(self):
        self.wait_core(0)
        for group in range(GROUPS):
            for ring in (group, group + GROUPS):
                rows, cols, value = self.summed(ring, 0, True)
                self.grads[rows, cols] = value
                self.send(self.rs_copy, ring, 0)

    def stage(self, group, step):
        n = self.chips
        rings = (group, group + GROUPS)

        @pl.when(step <= n - 2)
        def _():
            if group == 0:
                self.wait_core(step)
            for ring in rings:
                self.rs_copy(ring, step - 1).wait_recv()
                rows, cols, value = self.summed(ring, step, False)
                self.grads[rows, cols] = value
                self.send(self.rs_copy, ring, step)

        @pl.when(step == n - 1)
        def _():
            if group == 0:
                self.wait_core(n - 1)
            for ring in rings:
                self.rs_copy(ring, n - 2).wait_recv()
                rows, cols, value = self.summed(ring, n - 1, False)
                if self.own_sems is None:
                    self.result[rows, cols] = value
                else:
                    self.grads[rows, cols] = value
                    self.own_copy(ring).start()
                self.send(self.ag_copy, ring, 0)
            self.pass_on(group, 0)

        @pl.when((step >= n) & (step <= 2 * n - 3))
        def _():
            for ring in rings:
                self.ag_copy(ring, step - n).wait_recv()
                self.send(self.ag_copy, ring, step - n + 1)
            self.pass_on(group, step - n + 1)

        @pl.when(step == 2 * n - 2)
        def _():
            for ring in rings:
                self.ag_copy(ring, n - 2).wait_recv()
            self.pass_on(group, n - 1)

    def stages(self, first, last):
        def run(step, carry):
            for group in range(GROUPS):
                self.stage(group, step)
            return carry

        lax.fori_loop(first, last, run, 0)

    def arrive(self):
        def run(step, carry):
            for way in range(2):
                self.pair_copy(way, step).wait_recv()
            return carry

        lax.fori_loop(0, self.chips, run, 0)
        if self.own_sems is not None:
            for ring in range(2 * GROUPS):
                self.own_copy(ring).wait()

    def drain(self):
        def cores(step, carry):
            self.core_copy(0, step).wait_send()
            self.core_copy(1, step).wait_send()
            return carry

        def pairs(step, carry):
            for way in range(2):
                self.pair_copy(way, step).wait_send()
            return carry

        def ring_steps(step, carry):
            for ring in range(2 * GROUPS):
                self.rs_copy(ring, step).wait_send()
                self.ag_copy(ring, step).wait_send()
            return carry

        n, slots = self.chips, self.slots
        lax.fori_loop(0, n, cores, 0)
        lax.fori_loop(n - slots, n, pairs, 0)
        lax.fori_loop(max(n - 1 - slots, 0), n - 1, ring_steps, 0)


def segment_sems(chips):
    dma = pltpu.SemaphoreType.DMA
    rings = 2 * GROUPS
    slots = send_slots(chips)
    both = [dma((rings, slots)), dma((rings, chips))]
    return [dma((2, chips))] * 2 + both * 2 + [dma((2, slots)), dma((2, chips))]


class Small:
    def __init__(self, here, from_core, from_mp, every, pair_sems, ring_sems):
        self.here, self.from_core, self.from_mp, self.every = here, from_core, from_mp, every
        self.pair_sems, self.ring_sems = pair_sems, ring_sems
        self.forward = here.chips // 2
        self.backward = here.chips - 1 - self.forward

    def pair(self, which, src, dst, to):
        return remote(src, dst, self.pair_sems.at[0, which], self.pair_sems.at[1, which], to)

    def start(self, src):
        self.src = src
        self.to_core = self.pair(0, src, self.from_core, self.here.sibling)
        self.to_core.start()

    def core_done(self):
        self.to_core.wait()
        place = self.here.place
        self.every[place] = self.src[...] + self.from_core[...]
        spot = self.every.at[place, pl.ds(8, 8)]
        self.to_mp = self.pair(1, spot, self.from_mp, self.here.partner)
        self.to_mp.start()

    def mp_done(self):
        self.to_mp.wait()
        place = self.here.place
        self.every[place, pl.ds(8, 8)] = self.every[place, pl.ds(8, 8)] + self.from_mp[...]
        self.step(0, 0).start()
        if self.backward:
            self.step(1, 0).start()

    def step(self, way, step):
        n = self.here.chips
        at = (self.here.place + n - step) % n if way == 0 else (self.here.place + step) % n
        spot = self.every.at[at]
        to = self.here.following if way == 0 else self.here.previous
        sems = self.ring_sems
        return remote(spot, spot, sems.at[0, way, step], sems.at[1, way, step], to)

    def hop(self, step):
        for way, count in ((0, self.forward), (1, self.backward)):

            @pl.when(step < count)
            def _():
                self.step(way, step - 1).wait_recv()
                self.step(way, step).start()

    def finish(self, out, hops):
        def run(step, carry):
            self.hop(step)
            return carry

        if hops < self.forward:
            lax.fori_loop(hops, self.forward, run, 0)
        self.step(0, self.forward - 1).wait_recv()
        if self.backward:
            self.step(1, self.backward - 1).wait_recv()
        out[...] = self.every[0]

        def add(chip, carry):
            out[...] += self.every[chip]
            return carry

        lax.fori_loop(1, self.here.chips, add, 0)

        def sent(way, count):
            def run(step, carry):
                self.step(way, step).wait_send()
                return carry

            lax.fori_loop(0, count, run, 0)

        sent(0, self.forward)
        sent(1, self.backward)


def small_scratch(chips):
    dma = pltpu.SemaphoreType.DMA
    return [
        pltpu.VMEM((16, WIDE), jnp.float32),
        pltpu.VMEM((8, WIDE), jnp.float32),
        pltpu.VMEM((chips, 16, WIDE), jnp.float32),
        dma((2, 2)),
        dma((2, 2, chips)),
    ]


LOW = jnp.bfloat16
F32 = jnp.float32
HALF = 512
TILE = 256
SPAN = 128
STRIP = 32
HIDDEN = 256
EPS = 1e-06
FAR = -1e30
SCALE = HEAD_DIM**-0.5
NT = (((1,), (1,)), ((), ()))
TN = (((0,), (0,)), ((), ()))


def nt_dot(a, b):
    return lax.dot_general(a, b, NT, preferred_element_type=F32)


def tn_dot(a, b):
    return lax.dot_general(a, b, TN, preferred_element_type=F32)


def dot(a, b):
    return jnp.dot(a, b, preferred_element_type=F32)


def normal_parts(values):
    centred = values - jnp.mean(values, axis=-1, keepdims=True)
    spread = jnp.mean(centred * centred, axis=-1, keepdims=True)
    return centred, lax.rsqrt(spread + EPS)


def norm_back(d_out, unit, inverse, gain):
    e = d_out * gain
    share = e - jnp.mean(e, -1, keepdims=True)
    return inverse * (share - unit * jnp.mean(e * unit, -1, keepdims=True))


def column_sum(values):
    return jnp.sum(values, axis=0, keepdims=True)


def split_heads(pair):
    low_lanes = lax.broadcasted_iota(jnp.int32, pair.shape, 1) < HEAD_DIM
    zero = jnp.zeros_like(pair)
    return jnp.concatenate([jnp.where(low_lanes, pair, zero), jnp.where(low_lanes, zero, pair)])


def own_blocks(both):
    return jnp.concatenate([both[:HEAD_DIM, :SPAN], both[HEAD_DIM:, SPAN:]], axis=0)


def twice(values):
    return jnp.concatenate([values, values], axis=1)


SCRATCH = (
    "x_own", "h1", "cot", "h2", "wq", "w_mine", "w_got", "q", "k", "v", "att32", "att_send",
    "att_got", "lse", "key_code", "query_seg", "bias", "middle", "out_sum", "out_send", "out_got",
    "dh_own", "dh2_send", "dh2_got", "d_branch", "d_att", "go_send", "go_core", "go_got",
    "small_ref", "grads", "from_core", "result", "landed_m", "landed_q", "local_sems", "swap_sems",
    "pass_sems", "own_sems",
)


def twice_rows(values):
    return jnp.concatenate([values[0:1], values[1:2]], axis=1)


def fold(values, op, rows=8):
    while values.shape[0] > rows:
        half = values.shape[0] // 2
        values = op(values[:half], values[half:])
    return values


def strips(rows):
    return [slice(at, at + STRIP) for at in range(0, rows, STRIP)]


def result_in_hbm(chips):
    return chips > 8


class Names:
    pass


def block_kernel(chips, sizes, *refs):
    (
        x_hbm,
        cot_hbm,
        wq_hbm,
        w_out_hbm,
        up_hbm,
        down_hbm,
        lengths,
        mask_ref,
        gain1,
        bias1,
        b_qv,
        b_out,
        gain2,
        bias2,
        b_up,
        b_down,
        summed_ref,
        out_ref,
        dx_ref,
        small_out,
    ) = refs[:20]
    m = Names()
    for name, ref in zip(SCRATCH, refs[20:]):
        setattr(m, name, ref)
    more = refs[20 + len(SCRATCH) :]
    sems_m, sems_q, small_refs = more[:8], more[8:16], more[16:]
    rows_m, rows_q = sizes
    here = Here(chips)
    direct = result_in_hbm(chips)
    result = summed_ref if direct else m.result
    ring_m = Segment(
        here, 0, rows_m, m.grads, m.from_core, m.landed_m, result, sems_m,
        m.own_sems.at[0] if direct else None,
    )
    ring_q = Segment(
        here, rows_m, rows_q, m.grads, m.from_core, m.landed_q, result, sems_q,
        m.own_sems.at[1] if direct else None,
    )
    small = Small(here, *small_refs)
    width = m.k.shape[1]
    pairs = width // 128
    row_len = 2 * HALF
    hidden = up_hbm.shape[1]
    blocks = row_len // SPAN

    def local(which, src, dst):
        return pltpu.make_async_copy(src, dst, m.local_sems.at[which])

    def swapped(which, src, dst):
        return remote(src, dst, m.swap_sems.at[0, which], m.swap_sems.at[1, which], here.partner)

    def part(chunk):
        return pl.ds(pl.multiple_of(chunk * TILE, TILE), TILE)

    def other(chunk):
        return pl.ds(pl.multiple_of(HALF + chunk * TILE, TILE), TILE)

    def x_swap(chunk):
        return swapped(chunk, x_hbm.at[part(chunk)], m.h1.at[other(chunk)])

    def cot_swap(chunk):
        return swapped(2 + chunk, cot_hbm.at[part(chunk)], m.cot.at[other(chunk)])

    def h2_swap(chunk):
        return swapped(4 + chunk, m.h2.at[part(chunk)], m.h2.at[other(chunk)])

    def dh2_swap(chunk):
        return swapped(6 + chunk, m.dh2_send.at[part(chunk)], m.dh2_got.at[part(chunk)])

    def out_swap(chunk):
        return swapped(8 + chunk, m.out_send.at[part(chunk)], m.out_got.at[part(chunk)])

    def dh1_swap(chunk):
        return swapped(10 + chunk, m.dh2_send.at[part(chunk)], m.dh2_got.at[part(chunk)])

    quarter = width // 2
    w_rows = pl.ds(pl.multiple_of(here.core * quarter, 16), quarter)
    piece = pl.ds(pl.multiple_of((here.core * 2 + here.side) * (quarter // 2), 16), quarter // 2)
    w_swap = swapped(12, w_out_hbm.at[piece], m.w_got.at[piece])
    w_share = remote(
        m.w_got.at[piece], m.w_got.at[piece], m.pass_sems.at[4], m.pass_sems.at[5], here.beside
    )
    w_pass = remote(
        m.w_got.at[w_rows], m.w_got.at[w_rows], m.pass_sems.at[0], m.pass_sems.at[1], here.sibling
    )
    att_swap = swapped(13, m.att_send, m.att_got)
    da_swap = swapped(14, m.att_send, m.d_att.at[pl.ds(HALF, HALF)])
    other_rows = pl.ds(pl.multiple_of((1 - here.core) * quarter, 16), quarter)
    go_pass = remote(
        m.go_send.at[other_rows], m.go_core, m.pass_sems.at[2], m.pass_sems.at[3], here.sibling
    )
    go_swap = swapped(15, m.go_core, m.go_got)

    def as_row(ref):
        return ref[...].reshape(1, ref.shape[0])

    load_x = local(0, x_hbm, m.x_own)
    load_wq = local(1, wq_hbm, m.wq)
    load_w = local(2, w_out_hbm, m.w_mine)
    load_cot = local(3, cot_hbm, m.cot.at[pl.ds(0, HALF)])
    for load in (load_x, load_wq, load_w, load_cot):
        load.start()
    barrier = pltpu.get_barrier_semaphore()
    near = (here.sibling, here.following, here.previous, here.partner, here.beside)
    for device in near:
        pl.semaphore_signal(barrier, inc=1, device_id=device, device_id_type=MESH)
    pl.semaphore_wait(barrier, len(near))
    x_swap(0).start()

    shift = lax.axis_index("mp") * HALF
    ends, total = [], lengths[0, 0]
    for slot in range(lengths.shape[1]):
        ends.append(total)
        if slot + 1 < lengths.shape[1]:
            total = total + lengths[0, slot + 1]

    def segment(shape, axis):
        at = (lax.broadcasted_iota(jnp.int32, shape, axis) + shift) % row_len
        found = jnp.zeros(shape, jnp.int32)
        for end in ends:
            found = found + (at >= end).astype(jnp.int32)
        return found

    seg_row = segment((1, row_len), 1)
    for block in range(blocks):
        m.query_seg[block] = seg_row[:, block * SPAN : (block + 1) * SPAN]
    mask = mask_ref[...]
    turned = jnp.concatenate([mask[:, HALF:], mask[:, :HALF]], axis=1)
    mask = jnp.where(shift == 0, mask, turned)
    code = jnp.where(mask == 1, seg_row, -1).astype(F32)
    m.key_code[...] = jnp.broadcast_to(code, (8, row_len)).T[:, :1].astype(jnp.int32)

    def project(values, rows):
        centred, inverse = normal_parts(values.astype(F32))
        h1 = (centred * inverse * as_row(gain1) + as_row(bias1)).astype(LOW)
        m.h1[rows] = h1
        m.q[rows] = ((dot(h1, m.wq[0]) + b_qv[0:1]) * SCALE).astype(LOW)
        m.k[rows] = dot(h1, m.wq[1]).astype(LOW)
        m.v[rows] = (dot(h1, m.wq[2]) + b_qv[1:2]).astype(LOW)

    load_x.wait()
    load_wq.wait()

    def project_own(chunk, carry):
        project(m.x_own[part(chunk)], part(chunk))
        return carry

    lax.fori_loop(0, HALF // TILE, project_own, 0)
    x_swap(1).start()

    def project_got(chunk, carry):
        x_swap(chunk).wait_recv()

        @pl.when(chunk == HALF // TILE - 1)
        def _():
            w_swap.start()
            cot_swap(0).start()

        project(m.h1[other(chunk)], other(chunk))
        return carry

    lax.fori_loop(0, HALF // TILE, project_got, 0)

    def set_bias(block):
        shape = (row_len, SPAN)
        key_at = lax.broadcasted_iota(jnp.int32, shape, 0)
        query_at = lax.broadcasted_iota(jnp.int32, shape, 1) + block * SPAN
        allowed = (m.key_code[...] == m.query_seg[block]) | (key_at == query_at)
        m.bias[...] = jnp.where(allowed, 0.0, FAR)

    def block_rows(block):
        return pl.ds(pl.multiple_of(block * SPAN, SPAN), SPAN)

    def attend_scope(vt, scores, raised):
        vt[...] = m.v[...].T

        def block_at(at):
            return (at + blocks // 2) % blocks

        def score(block, pair, slot):
            cols = slice(128 * pair, 128 * pair + 128)
            scores[slot] = nt_dot(m.k[:, cols], split_heads(m.q[block_rows(block), cols]))

        def weigh(slot):
            held, out = scores.at[slot], raised.at[slot]
            top = None
            for keys in strips(row_len):
                here = held[keys] + twice(m.bias[keys])
                top = here if top is None else jnp.maximum(top, here)
            top = jnp.max(fold(top, jnp.maximum), axis=0, keepdims=True)
            whole = None
            for keys in strips(row_len):
                here = jnp.exp(held[keys] + twice(m.bias[keys]) - top)
                out[keys] = here.astype(LOW)
                whole = here if whole is None else whole + here
            return top, jnp.sum(fold(whole, jnp.add), axis=0, keepdims=True)

        def gather(block, pair, slot, top, whole):
            cols = slice(128 * pair, 128 * pair + 128)
            outs = own_blocks(dot(vt[cols], raised[slot]) / whole)
            m.att32[block_rows(block), cols] = outs.T
            m.lse[block, pair : pair + 1] = top + jnp.log(whole)

        def attend(couple, carry):
            @pl.when(couple == blocks // 8)
            def _():
                w_swap.wait_recv()
                w_share.start()

            @pl.when(couple == blocks // 4)
            def _():
                m.att_send[...] = m.att32[pl.ds(HALF, HALF)].astype(LOW)
                att_swap.start()
                w_share.wait_recv()
                w_pass.start()

            held = None
            for at in range(2 * pairs):
                pair, slot = at % pairs, at % 2
                turn = couple * 2 + at // pairs
                block = block_at(turn)
                if pair == 0:
                    set_bias(block)
                if pair + 1 < pairs:
                    score(block, pair + 1, 1 - slot)
                else:
                    score(block_at(jnp.minimum(turn + 1, blocks - 1)), 0, 1 - slot)
                now = weigh(slot)
                if held is not None:
                    gather(*held)
                held = (block, pair, slot, *now)
            gather(*held)
            return carry

        score(block_at(0), 0, 0)
        lax.fori_loop(0, blocks // 2, attend, 0)

    pl.run_scoped(
        attend_scope,
        pltpu.VMEM((width, row_len), LOW),
        pltpu.VMEM((2, row_len, 2 * SPAN), F32),
        pltpu.VMEM((2, row_len, 2 * SPAN), LOW),
    )

    load_w.wait()
    w_pass.wait_recv()
    att_swap.wait_recv()
    cot_swap(1).start()

    def branch(chunk, carry):
        rows = part(chunk)
        got = dot(m.att32[rows].astype(LOW), m.w_mine[...]) + dot(m.att_got[rows], m.w_got[...])
        middle = m.x_own[rows].astype(F32) + got + as_row(b_out)
        m.middle[rows] = middle
        centred, inverse = normal_parts(middle)
        m.h2[rows] = (centred * inverse * as_row(gain2) + as_row(bias2)).astype(LOW)

        @pl.when(chunk == 0)
        def _():
            h2_swap(0).start()

        return carry

    lax.fori_loop(0, HALF // TILE, branch, 0)
    load_cot.wait()

    if rows_m > 2 * hidden:
        m.grads[pl.ds(2 * hidden, rows_m - 2 * hidden)] = jnp.zeros(
            (rows_m - 2 * hidden, WIDE), LOW
        )

    def mlp_scope(act_ref, pre_ref, up_sum):
        def chunks_scope(up, down, pre_buf, d_buf, up_row, ht):
            load_up, load_down = local(0, up_hbm, up), local(1, down_hbm, down)
            load_up.start()
            load_down.start()
            load_up.wait()
            load_down.wait()
            up_sum[...] = jnp.zeros_like(up_sum)
            up_row[...] = as_row(b_up)
            tiles = hidden // HIDDEN

            def through(begin, tokens):
                rows = pl.ds(begin, tokens)

                def enter(tile):
                    cols = slice(tile * HIDDEN, tile * HIDDEN + HIDDEN)
                    pre_buf[tile % 2, :tokens] = dot(m.h2[rows], up[:, cols])
                    d_buf[tile % 2, :tokens] = nt_dot(m.cot[rows], down[cols])

                def bend(tile):
                    cols = slice(tile * HIDDEN, tile * HIDDEN + HIDDEN)
                    shift_up = up_row[:, cols]
                    total = None
                    for at in range(0, tokens, STRIP):
                        pre = pre_buf[tile % 2, at : at + STRIP] + shift_up
                        cdf = 0.5 * (1.0 + lax.erf(pre * 0.7071067811865476))
                        slope = cdf + pre * (jnp.exp(-0.5 * pre * pre) * 0.3989422804014327)
                        d_pre = (d_buf[tile % 2, at : at + STRIP] * slope).astype(LOW)
                        spot = pl.ds(begin + at, STRIP)
                        act_ref[spot, cols] = (pre * cdf).astype(LOW)
                        pre_ref[spot, cols] = d_pre
                        d_pre = d_pre.astype(F32)
                        total = d_pre if total is None else total + d_pre
                    up_sum[:, cols] += column_sum(fold(total, jnp.add))

                enter(0)
                for tile in range(tiles):
                    if tile + 1 < tiles:
                        enter(tile + 1)
                    bend(tile)

            def grad_part(begin, count):
                span = WIDE // 2
                tokens = pl.ds(begin, count)
                ht[:, :count] = m.h2[tokens].T

                def put(rows, cols, value):
                    if begin:
                        value = value + m.grads[rows, cols].astype(F32)
                    m.grads[rows, cols] = value.astype(LOW)

                def grad_step(at, carry):
                    cols = pl.ds(pl.multiple_of(at * span, 128), span)
                    up_rows = pl.ds(pl.multiple_of(at // 2 * WIDE, WIDE), WIDE)
                    up_cols = pl.ds(pl.multiple_of(at % 2 * span, 128), span)
                    put(up_rows, up_cols, dot(ht[:, :count], pre_ref[tokens, cols]))
                    down_rows = pl.ds(pl.multiple_of(hidden + at * span, 128), span)
                    put(down_rows, slice(None), tn_dot(act_ref[tokens, cols], m.cot[tokens]))
                    return carry

                lax.fori_loop(0, hidden // span, grad_step, 0)

            def products_out(begin, tokens):
                rows = pl.ds(begin, tokens)
                return dot(act_ref[rows], down[...]), nt_dot(pre_ref[rows], up[...])

            through(0, HALF)
            h2_swap(1).start()
            for chunk in range(2):
                rows = pl.ds(chunk * TILE, TILE)
                out, m.dh_own[rows] = products_out(chunk * TILE, TILE)
                m.out_sum[rows] = out + m.middle[rows] + as_row(b_down)
            for chunk in range(2):
                begin = HALF + chunk * TILE
                if chunk == 0:
                    grad_part(0, HALF)
                    h2_swap(0).wait_recv()
                    cot_swap(0).wait_recv()
                else:
                    grad_part(HALF, TILE)
                    h2_swap(1).wait_recv()
                    cot_swap(1).wait_recv()
                    dh2_swap(0).start()
                through(begin, TILE)
                if chunk == 1:
                    grad_part(begin, TILE)
                    ring_m.swap_cores()
                    ring_m.begin()
                out, d_h = products_out(begin, TILE)
                sent = pl.ds(chunk * TILE, TILE)
                m.dh2_send[sent] = d_h.astype(LOW)
                m.out_send[sent] = out.astype(LOW)
            dh2_swap(1).start()

        pl.run_scoped(
            chunks_scope,
            pltpu.VMEM((WIDE, hidden), LOW),
            pltpu.VMEM((hidden, WIDE), LOW),
            pltpu.VMEM((2, HALF, HIDDEN), F32),
            pltpu.VMEM((2, HALF, HIDDEN), F32),
            pltpu.VMEM((1, hidden), F32),
            pltpu.VMEM((WIDE, HALF), LOW),
        )
        m.small_ref[...] = jnp.zeros_like(m.small_ref)
        m.small_ref[0:1] = up_sum[:, :WIDE]
        m.small_ref[1:2] = up_sum[:, WIDE:]

    pl.run_scoped(
        mlp_scope,
        pltpu.VMEM((row_len, hidden), LOW),
        pltpu.VMEM((row_len, hidden), LOW),
        pltpu.VMEM((1, hidden), F32),
    )
    begun = 2
    done = begun + blocks + 2
    out_rows = width
    att_swap.wait_send()

    def back_scope(d_qkv, dk_acc, dv_acc, kt, ht, scores, d_probs, probs, d_scores):
        kt[...] = m.k[...].T
        dk_acc[...] = jnp.zeros_like(dk_acc)
        dv_acc[...] = jnp.zeros_like(dv_acc)
        heads_of = jnp.where(
            lax.broadcasted_iota(jnp.int32, (8, 128), 1) // HEAD_DIM
            == lax.broadcasted_iota(jnp.int32, (8, 128), 0),
            1.0,
            0.0,
        ).astype(LOW)

        ht[...] = m.h1[...].T
        probs[...] = jnp.zeros_like(probs)
        d_scores[...] = jnp.zeros_like(d_scores)

        def middle_back(chunk):
            dh2_swap(chunk).wait_recv()

            def some_rows(at, carry):
                rows = pl.ds(pl.multiple_of(chunk * TILE + at * SPAN, SPAN), SPAN)
                d_h2 = m.dh_own[rows] + m.dh2_got[rows].astype(F32)
                cot = m.cot[rows].astype(F32)
                centred, inverse = normal_parts(m.middle[rows])
                unit = centred * inverse
                d_middle = cot + norm_back(d_h2, unit, inverse, as_row(gain2))
                m.middle[rows] = d_middle
                d_branch = d_middle.astype(LOW)
                m.d_branch[rows] = d_branch
                m.att_send[rows] = nt_dot(d_branch, m.w_got[...]).astype(LOW)
                m.d_att[rows] = nt_dot(d_branch, m.w_mine[...]).astype(LOW)
                for at, term in enumerate((d_middle, d_h2 * unit, d_h2, cot)):
                    m.small_ref[10 + at : 11 + at] += column_sum(term)
                return carry

            lax.fori_loop(0, TILE // SPAN, some_rows, 0)

        def out_grads():
            def send_rows(pair, carry):
                cols = pl.ds(pl.multiple_of(pair * 128, 128), 128)
                m.go_send[cols] = tn_dot(m.att_got[:, cols], m.d_branch[...]).astype(LOW)
                return carry

            def own_rows(pair, carry):
                cols = pl.ds(pl.multiple_of(pair * 128, 128), 128)
                rows = pl.ds(pl.multiple_of(rows_m + pair * 128, 128), 128)
                held = m.att32[pl.ds(0, HALF), cols].astype(LOW)
                m.grads[rows] = tn_dot(held, m.d_branch[...]).astype(LOW)
                return carry

            lax.fori_loop(0, pairs, send_rows, 0)
            go_pass.start()
            lax.fori_loop(0, pairs, own_rows, 0)

        def out_grads_on():
            go_pass.wait()
            go = m.go_send[w_rows].astype(F32) + m.go_core[...].astype(F32)
            m.go_core[...] = go.astype(LOW)
            go_swap.start()
            out_swap(0).start()
            out_swap(1).start()

        def enter(block, pair, slot):
            rows, cols = block_rows(block), slice(128 * pair, 128 * pair + 128)
            scores[slot] = nt_dot(m.k[:, cols], split_heads(m.q[rows, cols]))
            d_probs[slot] = nt_dot(m.v[:, cols], split_heads(m.d_att[rows, cols]))

        def weigh(block, pair, slot):
            rows, cols = block_rows(block), slice(128 * pair, 128 * pair + 128)
            weighed = m.d_att[rows, cols].astype(F32) * m.att32[rows, cols]
            high = weighed.astype(LOW)
            rest = (weighed - high.astype(F32)).astype(LOW)
            inner = nt_dot(heads_of, high) + nt_dot(heads_of, rest)
            inner = twice_rows(inner)
            lse = m.lse[block, pair : pair + 1]
            for keys in strips(row_len):
                prob = jnp.exp(scores[slot, keys] + twice(m.bias[keys]) - lse)
                probs[slot, keys] = prob.astype(LOW)
                d_scores[slot, keys] = (prob * (d_probs[slot, keys] - inner)).astype(LOW)

        def leave(block, pair, slot):
            rows, cols = block_rows(block), slice(128 * pair, 128 * pair + 128)
            dk_acc[:, cols] += dot(d_scores[slot], split_heads(m.q[rows, cols]))
            dv_acc[:, cols] += dot(probs[slot], split_heads(m.d_att[rows, cols]))
            d_query = own_blocks(dot(kt[cols], d_scores[slot])).T.astype(LOW)
            d_qkv[0, rows, cols] = d_query * jnp.asarray(SCALE, LOW)

        def two_blocks(couple, carry):
            for at in range(2 * pairs):
                block, pair, slot = couple * 2 + at // pairs, at % pairs, at % 2
                before, after = (pair + pairs - 1) % pairs, (pair + 1) % pairs
                block_in = block if pair + 1 < pairs else jnp.minimum(block + 1, blocks - 1)
                block_out = block if pair > 0 else jnp.maximum(block - 1, 0)
                if pair == 0:
                    set_bias(block)
                if at == 2 * pairs - 1:

                    @pl.when(couple == blocks // 8 - 1)
                    def _():
                        middle_back(1)
                        da_swap.start()
                        out_grads()

                    @pl.when(couple == blocks // 4 - 1)
                    def _():
                        da_swap.wait_recv()
                        out_grads_on()

                enter(block_in, after, 1 - slot)
                leave(block_out, before, 1 - slot)
                weigh(block, pair, slot)
                ring_m.stage(pair, begun + block + 2 * jnp.minimum(couple, 1))
                if at == 2 * pairs - 1:

                    @pl.when(couple == 0)
                    def _():
                        ring_m.stages(begun + 2, begun + 4)

            return carry

        ring_m.stages(1, begun)
        middle_back(0)
        enter(0, 0, 0)
        lax.fori_loop(0, blocks // 2, two_blocks, 0)
        leave(blocks - 1, pairs - 1, (blocks * pairs - 1) % 2)
        d_qkv[1] = dk_acc[...].astype(LOW)
        d_qkv[2] = dv_acc[...].astype(LOW)

        for t in range(3):
            full = dot(ht[...], d_qkv[t]).astype(LOW)
            at = rows_m + out_rows + t * width
            m.grads[pl.ds(at, width), pl.ds(0, width)] = full[:width]
            m.grads[pl.ds(at, width), pl.ds(width, width)] = full[width:]
        go_swap.wait_recv()
        own_rows = pl.ds(pl.multiple_of(rows_m + here.core * quarter, 16), quarter)
        own = m.grads[own_rows].astype(F32)
        m.grads[own_rows] = (own + m.go_got[...].astype(F32)).astype(LOW)
        used = out_rows + 3 * width
        if rows_q > used:
            m.grads[pl.ds(rows_m + used, rows_q - used)] = jnp.zeros((rows_q - used, WIDE), LOW)
        ring_q.swap_cores()
        ring_m.stages(done, done + 1)
        ring_q.begin()

        def input_rows(rows):
            terms = [nt_dot(d_qkv[t, rows], m.wq[t]) for t in range(3)]
            return terms[0] + terms[1] + terms[2]

        dh2_swap(0).wait_send()
        dh2_swap(1).wait_send()

        def input_got(chunk, carry):
            m.dh2_send[part(chunk)] = input_rows(other(chunk)).astype(LOW)
            dh1_swap(chunk).start()
            return carry

        lax.fori_loop(0, HALF // TILE, input_got, 0)
        ring_q.stages(1, 2)
        m.small_ref[2:3, :width] = column_sum(d_qkv[0].astype(F32))
        m.small_ref[2:3, width:] = column_sum(d_qkv[2].astype(F32))

        def input_own(chunk, carry):
            m.dh_own[part(chunk)] = input_rows(part(chunk))
            return carry

        lax.fori_loop(0, HALF // TILE, input_own, 0)

    pl.run_scoped(
        back_scope,
        pltpu.VMEM((3, row_len, width), LOW),
        pltpu.VMEM((row_len, width), F32),
        pltpu.VMEM((row_len, width), F32),
        pltpu.VMEM((width, row_len), LOW),
        pltpu.VMEM((WIDE, row_len), LOW),
        pltpu.VMEM((2, row_len, 2 * SPAN), F32),
        pltpu.VMEM((2, row_len, 2 * SPAN), F32),
        pltpu.VMEM((2, row_len, 2 * SPAN), LOW),
        pltpu.VMEM((2, row_len, 2 * SPAN), LOW),
    )

    def both(step, carry):
        for group in range(GROUPS):
            ring_m.stage(group, done + step)
            ring_q.stage(group, step + 1)
        return carry

    left = max(2 * chips - 1 - (done + 1), 0)
    lax.fori_loop(1, left + 1, both, 0)
    out_swap(0).wait_recv()
    out_swap(1).wait_recv()
    out_ref[...] = (m.out_sum[...] + m.out_got[...].astype(F32)).astype(LOW)
    passed = max(chips + 1, left + 2)
    ring_q.stages(left + 2, passed)

    def first_back(chunk, carry):
        rows = part(chunk)
        dh1_swap(chunk).wait_recv()
        d_h1 = m.dh_own[rows] + m.dh2_got[rows].astype(F32)
        centred, inverse = normal_parts(m.x_own[rows].astype(F32))
        unit = centred * inverse
        dx_ref[rows] = (m.middle[rows] + norm_back(d_h1, unit, inverse, as_row(gain1))).astype(LOW)
        m.small_ref[8:9] += column_sum(d_h1 * unit)
        m.small_ref[9:10] += column_sum(d_h1)
        return carry

    lax.fori_loop(0, HALF // TILE, first_back, 0)
    ring_m.arrive()
    writes = []

    def write_out(which, start, rows):
        if not direct:
            spot = pl.ds(start, rows)
            writes.append(local(which, m.result.at[spot], summed_ref.at[spot]))
            writes[-1].start()

    write_out(0, 0, rows_m)
    small.start(m.small_ref)
    at = passed
    for then in (small.core_done, small.mp_done):
        ring_q.stages(at, at + 1)
        then()
        at += 1
    for hop in range(1, 4):
        ring_q.stages(at, at + 1)
        small.hop(hop)
        at += 1
    ring_q.stages(at, 2 * chips - 1)
    small.finish(small_out, 4)
    ring_q.arrive()
    write_out(1, rows_m, rows_q)
    ring_m.drain()
    ring_q.drain()
    for chunk in range(2):
        for copy in (x_swap, cot_swap, h2_swap, out_swap, dh1_swap):
            copy(chunk).wait_send()
    for copy in (w_swap, w_share, w_pass, da_swap, go_swap):
        copy.wait_send()
    for write in writes:
        write.wait()


def whole_block(x, cot, wq, w_out, w_up, w_down, lengths, mask, gain1, bias1, b_qv, b_out, gain2, bias2, b_up, b_down):
    n_dp = lax.axis_size("dp")
    chips = n_dp // 2
    width = w_out.shape[0]
    hidden = w_up.shape[1]
    row_len = 2 * HALF
    rows_m = whole_blocks(2 * hidden, n_dp)
    rows_q = whole_blocks(4 * width, n_dp)
    rows = rows_m + rows_q
    any_spec = pl.BlockSpec(memory_space=pl.ANY)
    vmem = pl.BlockSpec(memory_space=pltpu.VMEM)
    dma = pltpu.SemaphoreType.DMA
    blocks, pairs = row_len // SPAN, width // 128

    def low(*shape):
        return pltpu.VMEM(shape, LOW)

    def full(*shape):
        return pltpu.VMEM(shape, F32)

    scratch = dict(
        x_own=low(HALF, WIDE),
        h1=low(row_len, WIDE),
        cot=low(row_len, WIDE),
        h2=low(row_len, WIDE),
        wq=low(3, WIDE, width),
        w_mine=low(width, WIDE),
        w_got=low(width, WIDE),
        q=low(row_len, width),
        k=low(row_len, width),
        v=low(row_len, width),
        att32=full(row_len, width),
        att_send=low(HALF, width),
        att_got=low(HALF, width),
        lse=full(blocks, pairs, 2 * SPAN),
        key_code=pltpu.VMEM((row_len, 1), jnp.int32),
        query_seg=pltpu.VMEM((blocks, 1, SPAN), jnp.int32),
        bias=full(row_len, SPAN),
        middle=full(HALF, WIDE),
        out_sum=full(HALF, WIDE),
        out_send=low(HALF, WIDE),
        out_got=low(HALF, WIDE),
        dh_own=full(HALF, WIDE),
        dh2_send=low(HALF, WIDE),
        dh2_got=low(HALF, WIDE),
        d_branch=low(HALF, WIDE),
        d_att=low(row_len, width),
        go_send=low(width, WIDE),
        go_core=low(width // 2, WIDE),
        go_got=low(width // 2, WIDE),
        small_ref=full(16, WIDE),
        grads=low(rows, WIDE),
        from_core=low(rows // 2, WIDE),
        result=low(16 if result_in_hbm(chips) else rows, WIDE),
        landed_m=low(chips - 1, rows_m // n_dp, WIDE),
        landed_q=low(chips - 1, rows_q // n_dp, WIDE),
        local_sems=dma((4,)),
        swap_sems=dma((2, 16)),
        pass_sems=dma((6,)),
        own_sems=dma((2, 2 * GROUPS)),
    )
    return pl.pallas_call(
        functools.partial(block_kernel, chips, (rows_m, rows_q)),
        out_shape=(
            jax.ShapeDtypeStruct((rows, WIDE), LOW),
            jax.ShapeDtypeStruct((HALF, WIDE), LOW),
            jax.ShapeDtypeStruct((HALF, WIDE), LOW),
            jax.ShapeDtypeStruct((16, WIDE), F32),
        ),
        in_specs=[any_spec] * 6 + [pl.BlockSpec(memory_space=pltpu.SMEM)] + [vmem] * 9,
        out_specs=(any_spec, vmem, vmem, vmem),
        scratch_shapes=[scratch[name] for name in SCRATCH]
        + segment_sems(chips) * 2
        + small_scratch(chips),
        compiler_params=pltpu.CompilerParams(
            collective_id=0, has_side_effects=True, vmem_limit_bytes=63 * 2**20
        ),
        cost_estimate=pl.CostEstimate(
            flops=int(40e9), bytes_accessed=int(40e6), transcendentals=0
        ),
        name="whole_block",
    )(x, cot, wq, w_out, w_up, w_down, lengths, mask, gain1, bias1, b_qv, b_out, gain2, bias2, b_up, b_down)


def unpack_kernel(base, pieces, sum_ref, small_ref, a_ref, b_ref, *refs):
    low_buf, full_buf, tokens, in_sems, out_sems, copy_sems = refs[-6:]
    up_ref, down_ref, out_ref, qkv_ref, a_out, b_out, up_sum, qv_ref = refs[:8]
    vectors = refs[8:-6]
    span = low_buf.shape[1]
    half = WIDE // 2
    firm = 2 * (WIDE * 2) // span
    starts = [at * span if at < firm else base + (at - firm) * span for at in range(pieces)]
    fetches = [
        pltpu.make_async_copy(sum_ref.at[pl.ds(start, span)], low_buf.at[at], in_sems.at[at])
        for at, start in enumerate(starts)
    ]
    for fetch in fetches:
        fetch.start()
    ins = [
        pltpu.make_async_copy(ref, tokens.at[at], copy_sems.at[0, at])
        for at, ref in enumerate((a_ref, b_ref))
    ]
    outs = [
        pltpu.make_async_copy(tokens.at[at], ref, copy_sems.at[1, at])
        for at, ref in enumerate((a_out, b_out))
    ]
    for copy in ins:
        copy.start()
    writes = []

    def write(at, lane, src, dst):
        writes.append(pltpu.make_async_copy(src, dst, out_sems.at[at, lane]))
        writes[-1].start()

    for at, fetch in enumerate(fetches):
        fetch.wait()
        held = full_buf.at[at]
        held[...] = low_buf[at].astype(F32)
        row = at * span
        if row < 2 * WIDE:
            rows, cols = pl.ds(row % WIDE, span), pl.ds(row // WIDE * WIDE, WIDE)
            write(at, 0, held, up_ref.at[rows, cols])
        elif row < 4 * WIDE:
            write(at, 0, held, down_ref.at[pl.ds(row - 2 * WIDE, span)])
        elif row < 4 * WIDE + half:
            write(at, 0, held, out_ref.at[pl.ds(row - 4 * WIDE, span)])
        else:
            row = row - 4 * WIDE - half
            for side in range(2):
                rows = pl.ds(side * half + row % half, span)
                write(at, side, held.at[:, pl.ds(side * half, half)], qkv_ref.at[row // half, rows])
    for come, go in zip(ins, outs):
        come.wait()
        go.start()
    up_sum[...] = jnp.concatenate([small_ref[0:1], small_ref[1:2]], axis=1).reshape(2 * WIDE)
    qv_ref[0:1] = small_ref[2:3, :half]
    qv_ref[1:2] = small_ref[2:3, half:]
    for at, vector in enumerate(vectors):
        vector[...] = small_ref[8 + at : 9 + at].reshape(WIDE)
    for copy in outs + writes:
        copy.wait()


def unpack(summed, small, block_out, d_block_in, base, hidden, width):
    pieces = 12
    span = WIDE // 2
    any_spec = pl.BlockSpec(memory_space=pl.ANY)
    vmem = pl.BlockSpec(memory_space=pltpu.VMEM)
    shapes = [(WIDE, hidden), (hidden, WIDE), (width, WIDE), (3, WIDE, width)]
    dma = pltpu.SemaphoreType.DMA
    return pl.pallas_call(
        functools.partial(unpack_kernel, base, pieces),
        out_shape=[jax.ShapeDtypeStruct(s, F32) for s in shapes]
        + [jax.ShapeDtypeStruct((HALF, WIDE), LOW)] * 2
        + [jax.ShapeDtypeStruct((hidden,), F32), jax.ShapeDtypeStruct((2, width), F32)]
        + [jax.ShapeDtypeStruct((WIDE,), F32)] * 6,
        in_specs=[any_spec, vmem, any_spec, any_spec],
        out_specs=[any_spec] * 6 + [vmem] * 8,
        scratch_shapes=[
            pltpu.VMEM((pieces, span, WIDE), LOW),
            pltpu.VMEM((pieces, span, WIDE), F32),
            pltpu.VMEM((2, HALF, WIDE), LOW),
            dma((pieces,)),
            dma((pieces, 2)),
            dma((2, 2)),
        ],
        compiler_params=pltpu.CompilerParams(vmem_limit_bytes=62 * 2**20),
        cost_estimate=pl.CostEstimate(flops=int(1e6), bytes_accessed=int(24e6), transcendentals=0),
        name="unpack",
    )(summed, small, block_out, d_block_in)


def local(
    block_in,
    cotangent,
    lengths,
    token_mask,
    ln1_gain,
    ln1_bias,
    w_qkv,
    b_qv,
    w_out,
    b_out,
    ln2_gain,
    ln2_bias,
    w_up,
    b_up,
    w_down,
    b_down,
):
    summed, block_out, d_block_in, small = whole_block(
        block_in,
        cotangent,
        w_qkv.transpose(1, 0, 2),
        w_out,
        w_up,
        w_down,
        lengths,
        token_mask,
        ln1_gain,
        ln1_bias,
        b_qv,
        b_out,
        ln2_gain,
        ln2_bias,
        b_up,
        b_down,
    )
    base = whole_blocks(2 * w_up.shape[1], lax.axis_size("dp"))
    (
        d_w_up,
        d_w_down,
        d_w_out,
        d_w_qkv,
        block_out,
        d_block_in,
        d_b_up,
        d_b_qv,
        d_ln1_gain,
        d_ln1_bias,
        d_b_out,
        d_ln2_gain,
        d_ln2_bias,
        d_b_down,
    ) = unpack(summed, small, block_out, d_block_in, base, w_up.shape[1], w_out.shape[0])
    return (
        block_out,
        d_block_in,
        d_ln1_gain,
        d_ln1_bias,
        d_w_qkv.transpose(1, 0, 2),
        d_b_qv,
        d_w_out,
        d_b_out,
        d_ln2_gain,
        d_ln2_bias,
        d_w_up,
        d_b_up,
        d_w_down,
        d_b_down,
    )


def solution(mesh):
    in_specs = (
        P(("dp", "mp"), None),
        P(("dp", "mp"), None),
        P("dp", None),
        P("dp", None),
        P(),
        P(),
        P(None, None, "mp"),
        P(None, "mp"),
        P("mp", None),
        P(),
        P(),
        P(),
        P(None, "mp"),
        P("mp"),
        P("mp", None),
        P(),
    )
    out_specs = (
        P(("dp", "mp"), None),
        P(("dp", "mp"), None),
        P(),
        P(),
        P(None, None, "mp"),
        P(None, "mp"),
        P("mp", None),
        P(),
        P(),
        P(),
        P(None, "mp"),
        P("mp"),
        P("mp", None),
        P(),
    )
    return jax.shard_map(local, mesh=mesh, in_specs=in_specs, out_specs=out_specs, check_vma=False)
```
